256 devices in a mesh: dp: 8 (over x, y_hi), tm: 32 (over z, y_lo, core).
Axes of the slice: x: 4, y: 4 (y_hi: 2, y_lo: 2; y = y_hi * 2 + y_lo), z: 8, core: 2. Of those that a mesh axis runs over, the one named last changes fastest.
Arguments:
- frames: bfloat16 [8, 8192, 1536], P('dp', 'tm'), may hold values from -6 to 6
- live_mask: int32 [8, 8192], P('dp', 'tm'), may hold values from 0 to 1, as said below
- stretch_target: int32 [8, 256], P('dp', 'tm'), may hold values from -1 to 47, as said below
- pw_weight: bfloat16 [1536, 3072], P(('dp', 'tm')), may hold values from -0.15625 to 0.15625
- kernel: float32 [31, 1536], replicated, may hold values from -1 to 1
- out_grad: bfloat16 [8, 6144, 1536], P('dp', 'tm'), may hold values from -6 to 6
Outputs:
- mixed: bfloat16 [8, 6144, 1536], P('dp', 'tm')
- frame_grad: bfloat16 [8, 8192, 1536], P('dp', 'tm')
- weight_grad: float32 [1536, 3072], P(('dp', 'tm'))
- kernel_grad: float32 [31, 1536], replicated
The draws below stay inside these ranges and needn't reach their ends.
Inputs may be any that keep to these rules, and one draw needn't show every extreme that they name: `stretch_target`: at each tm position, every compute slot h * 6 + c of every group h is named by exactly one time slot. A device names 2 to 8 slots, and its own group at most 6 times; it names any other group at most 2 times, and some devices reach that. Named slots stand first among a device's slots at even tm positions and last at odd ones. `live_mask`: frames of unnamed time slots are 0. In a run of consecutive named slots all frames are 1 except a tail of the run's last stretch.
All inputs are finite; a program needn't handle non-finite values.
Results may differ from the reference program's by a relative error of at most 0.033.
Values may be sent and summed in bfloat16 or wider, within the bound.
No kernel may reach another device: no remote copies, remote signals or barrier semaphores. Data moves between devices by JAX's collectives and lax.ppermute only.
A program may use at most 128 MiB of HBM per device.

```python
import jax
import jax.numpy as jnp
from jax import lax

D = 1536
KERNEL = 31
STRETCH = 32
TCH = 8
CAP = 6
N_DP = 8
N_TM = 32


def layout_plan(key):
    role_key = jax.random.fold_in(key, 11)
    slot_key = jax.random.fold_in(key, 12)
    length_key = jax.random.fold_in(key, 13)
    order_key = jax.random.fold_in(key, 14)
    moved = TCH // 4
    role_scores = jax.random.randint(role_key, (N_TM, N_DP), 0, 1 << 20) * N_DP + jnp.arange(N_DP, dtype=jnp.int32)
    arrangement = jnp.argsort(role_scores, axis=-1, stable=True).astype(jnp.int32)
    standing = jnp.argsort(arrangement, axis=-1, stable=True).astype(jnp.int32)
    role = standing % 4
    small_group = jnp.take_along_axis(arrangement, standing // 4 * 4 + 3, axis=-1)
    slot_scores = jax.random.randint(slot_key, (N_TM, N_DP, CAP), 0, 1 << 20) * CAP + jnp.arange(CAP, dtype=jnp.int32)
    slot_order = jnp.argsort(slot_scores, axis=-1, stable=True).astype(jnp.int32)
    entry_ids = jnp.arange(TCH, dtype=jnp.int32)[None, None, :]
    role_col = role[:, :, None]
    own_count = jnp.where(role_col < 3, CAP, moved)
    group_here = jnp.broadcast_to(jnp.arange(N_DP, dtype=jnp.int32)[None, :, None], (N_TM, N_DP, TCH))
    stay = entry_ids < own_count
    leave = (entry_ids >= CAP) & (role_col < 2)
    dest = jnp.where(stay, group_here, jnp.where(leave, small_group[:, :, None], -1))
    index_in = jnp.where(stay, entry_ids, jnp.where(leave, moved + role_col * moved + entry_ids - CAP, 0))
    named_entry = dest >= 0
    flat_order = slot_order.reshape(N_TM, N_DP * CAP)
    lookup = (jnp.maximum(dest, 0) * CAP + index_in).reshape(N_TM, N_DP * TCH)
    chosen = jnp.take_along_axis(flat_order, lookup, axis=1).reshape(N_TM, N_DP, TCH)
    entries = jnp.where(named_entry, jnp.maximum(dest, 0) * CAP + chosen, -1)
    entries = entries.transpose(1, 0, 2)
    shuffle = jax.random.randint(order_key, (N_DP, N_TM, TCH), 0, 1 << 20) * TCH + jnp.arange(TCH, dtype=jnp.int32)
    keyed = (entries < 0).astype(jnp.int32) * (1 << 24) + shuffle
    ordering = jnp.argsort(keyed, axis=-1, stable=True)
    placed = jnp.take_along_axis(entries, ordering, axis=-1)
    odd_place = (jnp.arange(N_TM) % 2 == 1)[None, :, None]
    placed = jnp.where(odd_place, placed[:, :, ::-1], placed)
    target = placed.reshape(N_DP, N_TM * TCH).astype(jnp.int32)
    named = target >= 0
    following = jnp.concatenate([named[:, 1:], jnp.zeros((N_DP, 1), bool)], axis=1)
    ending = named & jnp.logical_not(following)
    counts = jax.random.randint(length_key, (N_DP, N_TM * TCH), 1, STRETCH + 1)
    counts = jnp.where(ending, counts, STRETCH) * named.astype(jnp.int32)
    frame_ids = jnp.arange(STRETCH, dtype=jnp.int32)
    live = (frame_ids[None, None, :] < counts[:, :, None]).astype(jnp.int32)
    return (target, live.reshape(N_DP, N_TM * TCH * STRETCH))


def draw_stretch_target(key, part):
    plan_target, plan_live = layout_plan(key)
    return plan_target


def draw_live_mask(key, part):
    plan_target, plan_live = layout_plan(key)
    return plan_live


def steps_of(own_key, shape, cuts, low, top_value):
    level, own = 1.0, jax.random.fold_in(own_key, 6)
    for dim, blocks in cuts:
        steps = jnp.exp(jax.random.uniform(jax.random.fold_in(own, dim), (blocks,), jnp.float32, low / len(cuts), top_value / len(cuts)))
        level = level * jnp.repeat(steps, shape[dim] // blocks).reshape([-1 if axis == dim else 1 for axis in range(len(shape))])
    return level


def centred(key, shape, deviation, reach, cuts=(), kind=jnp.bfloat16):
    gain = steps_of(key, shape, cuts, -0.22, 0.18) if cuts else 1.0
    values = jax.random.normal(key, shape, jnp.float32) * deviation * gain
    return jnp.minimum(jnp.maximum(values, -reach), reach).astype(kind)


def setup_inputs(seed: int = 0) -> dict:
    arg_keys = jax.random.split(jax.random.key(seed), 7)
    frames = centred(arg_keys[0], (N_DP, N_TM * TCH * STRETCH, D), 1.0, 6.0, ((0, 8), (1, 32)))
    live_mask = draw_live_mask(jax.random.fold_in(arg_keys[6], 71), 0)
    stretch_target = draw_stretch_target(jax.random.fold_in(arg_keys[6], 71), 0)
    pw_weight = centred(arg_keys[3], (D, 2 * D), D ** -0.5, 0.15625, ((0, 256),))
    kernel = centred(arg_keys[4], (KERNEL, D), KERNEL ** -0.5, 1.0, (), jnp.float32)
    out_grad = centred(arg_keys[5], (N_DP, N_TM * CAP * STRETCH, D), 1.0, 6.0, ((0, 8), (1, 32)))
    return {"frames": frames, "live_mask": live_mask, "stretch_target": stretch_target, "pw_weight": pw_weight, "kernel": kernel, "out_grad": out_grad}


EPSILON = 1e-05

def normalize(values):
    center = lax.optimization_barrier(jnp.mean(values, axis=-1, keepdims=True))
    shifted = values - center
    spread = lax.optimization_barrier(jnp.mean(shifted * shifted, axis=-1, keepdims=True))
    inverse_scale = lax.rsqrt(spread + EPSILON)
    return (shifted * inverse_scale, inverse_scale)

def depthwise(padded, kernel, length):
    running = jnp.zeros((length, padded.shape[1]), jnp.float32)
    for offset in range(kernel.shape[0]):
        running = running + kernel[offset] * padded[offset:offset + length].astype(jnp.float32)
    return running

def kernel_terms(grad_mixed, padded, length, taps):
    grad_float = grad_mixed.astype(jnp.float32)
    return jnp.stack([lax.optimization_barrier(jnp.sum(grad_float * padded[offset:offset + length].astype(jnp.float32), axis=0)) for offset in range(taps)])

def time_group(frames_group, unit_group, live_group, grad_group, kernel):
    length = frames_group.shape[0]
    half_span = (kernel.shape[0] - 1) // 2
    live_col = live_group.astype(jnp.float32)[:, None]
    unit_group = jnp.where(live_group[:, None] > 0, unit_group, jnp.zeros_like(unit_group))
    unit_padded = jnp.pad(unit_group, ((half_span, half_span), (0, 0)))
    mixed_time = live_col * depthwise(unit_padded, kernel, length)
    norm_time, norm_scale = normalize(mixed_time)
    sigma_time = jax.nn.sigmoid(norm_time)
    output_time = (frames_group.astype(jnp.float32) + norm_time * sigma_time).astype(jnp.bfloat16)
    grad_norm = grad_group.astype(jnp.float32) * sigma_time * (1.0 + norm_time * (1.0 - sigma_time))
    grad_mixed = live_col * norm_scale * (grad_norm - lax.optimization_barrier(jnp.mean(grad_norm, axis=-1, keepdims=True)) - norm_time * lax.optimization_barrier(jnp.mean(grad_norm * norm_time, axis=-1, keepdims=True)))
    grad_mixed = grad_mixed.astype(jnp.bfloat16)
    grad_padded = jnp.pad(grad_mixed, ((half_span, half_span), (0, 0)))
    grad_unit = (live_col * depthwise(grad_padded, kernel[::-1], length)).astype(jnp.bfloat16)
    return (output_time, grad_unit, kernel_terms(grad_mixed, unit_padded, length, kernel.shape[0]))

def reference(frames, live_mask, stretch_target, pw_weight, kernel, out_grad):
    model_width = frames.shape[2]
    loss_scale = (N_DP * N_TM * CAP * STRETCH) ** (-0.5)
    targets = stretch_target.reshape(N_DP, N_TM, TCH)
    slot_shape = targets.shape
    group_ids = jnp.broadcast_to(jnp.arange(N_DP, dtype=jnp.int32)[:, None, None], slot_shape)
    position_ids = jnp.broadcast_to(jnp.arange(N_TM, dtype=jnp.int32)[None, :, None], slot_shape)
    slot_ids = jnp.broadcast_to(jnp.arange(TCH, dtype=jnp.int32)[None, None, :], slot_shape)
    named = targets >= 0
    dest_group = jnp.where(named, targets // CAP, N_DP).astype(jnp.int32)
    dest_slot = jnp.where(named, targets % CAP, 0).astype(jnp.int32)
    empty_map = jnp.zeros((N_DP + 1, N_TM, CAP), jnp.int32)
    source_group = empty_map.at[dest_group, position_ids, dest_slot].set(group_ids)[:N_DP]
    source_slot = empty_map.at[dest_group, position_ids, dest_slot].set(slot_ids)[:N_DP]
    position_rows = jnp.broadcast_to(jnp.arange(N_TM, dtype=jnp.int32)[None, :, None], (N_DP, N_TM, CAP))

    def to_rows(values):
        pieces = values.reshape(N_DP, N_TM, TCH, STRETCH, model_width)
        return pieces[source_group, position_rows, source_slot].reshape(N_DP * N_TM, CAP * STRETCH, model_width)

    def to_time(values):
        pieces = values.reshape(N_DP, N_TM, CAP, STRETCH, model_width)
        empty_time = jnp.zeros((N_DP, N_TM, TCH, STRETCH, model_width), values.dtype)
        filled = empty_time.at[source_group, position_rows, source_slot].set(pieces)
        return filled.reshape(N_DP, N_TM * TCH * STRETCH, model_width)
    frame_rows = to_rows(frames)

    def forward_rows(block):
        normed, inverse_scale = normalize(block.astype(jnp.float32))
        projected = jnp.dot(normed.astype(jnp.bfloat16), pw_weight, preferred_element_type=jnp.float32)
        gate_value = jax.nn.sigmoid(projected[:, model_width:])
        return (projected[:, :model_width] * gate_value).astype(jnp.bfloat16)
    unit_rows = lax.map(forward_rows, frame_rows)
    unit_time = to_time(unit_rows)
    grad_time = to_time(out_grad)
    output_time, grad_unit_time, kernel_parts = lax.map(lambda items: time_group(items[0], items[1], items[2], items[3], kernel), (frames, unit_time, live_mask, grad_time))
    mixed = to_rows(output_time).reshape(N_DP, N_TM * CAP * STRETCH, model_width)
    grad_rows = to_rows(grad_unit_time)
    cotangent_rows = out_grad.reshape(N_DP * N_TM, CAP * STRETCH, model_width)

    def backward_rows(running, items):
        block, grad_block, cotangent_block = items
        normed, inverse_scale = normalize(block.astype(jnp.float32))
        normed_bf = normed.astype(jnp.bfloat16)
        projected = jnp.dot(normed_bf, pw_weight, preferred_element_type=jnp.float32)
        linear_half = projected[:, :model_width]
        gate_value = jax.nn.sigmoid(projected[:, model_width:])
        grad_float = grad_block.astype(jnp.float32)
        grad_pre = jnp.concatenate([grad_float * gate_value, grad_float * linear_half * gate_value * (1.0 - gate_value)], axis=1).astype(jnp.bfloat16)
        grad_normed = lax.dot_general(grad_pre, pw_weight, (((1,), (1,)), ((), ())), preferred_element_type=jnp.float32)
        branch = inverse_scale * (grad_normed - lax.optimization_barrier(jnp.mean(grad_normed, axis=-1, keepdims=True)) - normed * lax.optimization_barrier(jnp.mean(grad_normed * normed, axis=-1, keepdims=True)))
        step_grad = (cotangent_block.astype(jnp.float32) + branch).astype(jnp.bfloat16)
        term = lax.dot_general(normed_bf, grad_pre, (((0,), (0,)), ((), ())), preferred_element_type=jnp.float32)
        term = (loss_scale * term).astype(jnp.bfloat16)
        return (running + term.astype(jnp.float32), step_grad)
    weight_grad, step_rows = lax.scan(backward_rows, jnp.zeros((model_width, 2 * model_width), jnp.float32), (frame_rows, grad_rows, cotangent_rows))
    frame_grad = to_time(step_rows)
    kernel_grad = loss_scale * lax.optimization_barrier(jnp.sum(kernel_parts, axis=0))
    return (mixed, frame_grad, weight_grad, kernel_grad)
```

```python
import jax
import jax.numpy as jnp
from jax import lax
from jax.sharding import Mesh
from jax.sharding import PartitionSpec as P

EPSILON = 1e-05
X, YH, Z, YL, CORE = 4, 2, 8, 2, 2
Y = YH * YL
XA, YA, ZA, CA = "x", ("yh", "yl"), "z", "core"
DP = ("x", "yh")
TM = ("z", "yl", "core")
SHARE = 6


def shift(value, axis, count, by):
    return lax.ppermute(value, axis, [(i, (i + by) % count) for i in range(count)])


def gather(value, axis, count):
    return [value] + [shift(value, axis, count, k) for k in range(1, count)]


def scatter(chunks, axis, count):
    arrived = [chunks[0]] + [shift(chunks[k], axis, count, -k) for k in range(1, count)]
    total = arrived[0].astype(jnp.float32)
    for piece in arrived[1:]:
        total = total + piece.astype(jnp.float32)
    return total


def normalize(values):
    center = jnp.mean(values, axis=-1, keepdims=True)
    shifted = values - center
    spread = jnp.mean(shifted * shifted, axis=-1, keepdims=True)
    inverse_scale = lax.rsqrt(spread + EPSILON)
    return (shifted * inverse_scale, inverse_scale)


def depthwise(padded, kernel, length):
    running = jnp.zeros((length, padded.shape[1]), jnp.float32)
    for offset in range(kernel.shape[0]):
        running = running + kernel[offset] * padded[offset : offset + length].astype(jnp.float32)
    return running


def kernel_terms(grad_mixed, padded, length, taps):
    grad_float = grad_mixed.astype(jnp.float32)
    return jnp.stack(
        [
            jnp.sum(grad_float * padded[offset : offset + length].astype(jnp.float32), axis=0)
            for offset in range(taps)
        ]
    )


def rims(values, width):
    count = Z * YL * CORE
    head = values[:width]
    tail = values[values.shape[0] - width :]
    before = lax.ppermute(tail, TM, [(i, i + 1) for i in range(count - 1)])
    after = lax.ppermute(head, TM, [(i + 1, i) for i in range(count - 1)])
    return jnp.concatenate([before, values, after], axis=0)


def feature_order(first, second):
    row = jnp.arange(X * Y * Z * CORE * SHARE, dtype=jnp.int32)
    within = row % SHARE
    kz = row // SHARE % Z
    k_second = row // (SHARE * Z) % 4
    k_first = row // (SHARE * Z * 4) % 4
    kc = row // (SHARE * Z * 16)
    kx, ky = (k_first, k_second) if first == "x" else (k_second, k_first)
    xs = (lax.axis_index(XA) - kx) % X
    ys = (lax.axis_index(YA) - ky) % Y
    zs = (lax.axis_index(ZA) - kz) % Z
    cs = (lax.axis_index(CA) - kc) % CORE
    device = ((((xs * YH + ys // YL) * Z + zs) * YL) + ys % YL) * CORE + cs
    return device * SHARE + within


def gather_weight(shard):
    half = shard.shape[1] // 2
    column = jnp.concatenate(gather(shard, ZA, Z), axis=0)
    lin, gate = column[:, :half], column[:, half:]
    lin = jnp.concatenate(gather(lin, YA, Y), axis=0)
    gate = jnp.concatenate(gather(gate, XA, X), axis=0)
    lin = gather(lin, XA, X)
    gate = gather(gate, YA, Y)
    lin = lin + [shift(piece, CA, CORE, 1) for piece in lin]
    gate = gate + [shift(piece, CA, CORE, 1) for piece in gate]
    return jnp.concatenate(lin, axis=0), jnp.concatenate(gate, axis=0)


def split(value, count):
    rows = value.shape[0] // count
    return [value[k * rows : (k + 1) * rows] for k in range(count)]


def scatter_weight(lin, gate):
    bf = jnp.bfloat16
    lin = scatter(split(lin, CORE), CA, CORE).astype(bf)
    gate = scatter(split(gate, CORE), CA, CORE).astype(bf)
    lin = scatter(split(lin, X), XA, X).astype(bf)
    gate = scatter(split(gate, Y), YA, Y).astype(bf)
    lin = scatter(split(lin, Y), YA, Y).astype(bf)
    gate = scatter(split(gate, X), XA, X).astype(bf)
    return scatter(split(jnp.concatenate([lin, gate], axis=1), Z), ZA, Z)


def in_turn(pieces, at):
    count = len(pieces)
    ring = jnp.stack([pieces[(-j) % count] for j in range(2 * count - 1)])
    return lax.dynamic_slice_in_dim(ring, (-at) % count, count, axis=0)


def sum_taps(terms):
    taps, width = terms.shape
    rows = 32
    terms = jnp.pad(terms, ((0, rows - taps), (0, 0)))
    core, at = lax.axis_index(CA), lax.axis_index(XA)
    halves = terms.reshape(CORE, rows // CORE, width)
    pieces = [
        lax.dynamic_index_in_dim(halves, (core - k) % CORE, 0, keepdims=False) for k in range(CORE)
    ]
    part = scatter(pieces, CA, CORE)
    quarters = part.reshape(X, rows // CORE // X, width)
    pieces = [lax.dynamic_index_in_dim(quarters, (at - k) % X, 0, keepdims=False) for k in range(X)]
    part = scatter(pieces, XA, X)
    part = scatter([part] * Y, YA, Y)
    part = scatter([part] * Z, ZA, Z)
    part = in_turn(gather(part, XA, X), at).reshape(rows // CORE, width)
    part = in_turn(gather(part, CA, CORE), core).reshape(rows, width)
    return part[:taps]


def shards(frames, live_mask, stretch_target, pw_weight, kernel, out_grad):
    bf = jnp.bfloat16
    groups = X * YH
    own_group = lax.axis_index(DP)
    slot_count = stretch_target.shape[1]
    width = frames.shape[2]
    stretch_len = frames.shape[1] // slot_count
    capacity = out_grad.shape[1] // stretch_len
    per_peer = slot_count // 4
    entries = groups * per_peer
    taps = kernel.shape[0]
    half_span = (taps - 1) // 2
    length = slot_count * stretch_len
    rows_here = capacity * stretch_len
    loss_scale = float(groups * Z * YL * CORE * rows_here) ** (-0.5)

    target = stretch_target[0]
    named_slot = target >= 0
    dest_group = jnp.where(named_slot, target // capacity, -1)
    remote = named_slot & (dest_group != own_group)
    local = named_slot & (dest_group == own_group)
    slot_index = jnp.arange(slot_count, dtype=jnp.int32)
    entry_ids = jnp.arange(entries, dtype=jnp.int32)
    earlier = slot_index[:, None] > slot_index[None, :]
    alike = (dest_group[:, None] == dest_group[None, :]) & remote[None, :] & earlier
    rank_within = jnp.sum(alike.astype(jnp.int32), axis=1)
    entry_index = jnp.where(remote, dest_group * per_peer + rank_within, -1)
    selection = entry_index[None, :] == entry_ids[:, None]
    selector = selection.astype(bf)
    slot_codes = jnp.sum(jnp.where(selection, (target % capacity + 1)[None, :], 0), axis=1) - 1
    capacity_index = jnp.arange(capacity, dtype=jnp.int32)
    local_pick = ((target % capacity)[None, :] == capacity_index[:, None]) & local[None, :]
    local_pick = local_pick.astype(bf)

    def exchange(values):
        return lax.all_to_all(values, DP, split_axis=0, concat_axis=0, tiled=True)

    codes_home = exchange(slot_codes)

    def send_home(values):
        pieces = values.reshape(slot_count, stretch_len, width)
        outgoing = jnp.einsum(
            "es,sfw->efw", selector, pieces, preferred_element_type=jnp.float32
        ).astype(bf)
        arrived = exchange(outgoing)
        placing = (codes_home[None, :] == capacity_index[:, None]).astype(bf)
        placed = jnp.einsum("ce,efw->cfw", placing, arrived, preferred_element_type=jnp.float32)
        placed = placed + jnp.einsum(
            "cs,sfw->cfw", local_pick, pieces, preferred_element_type=jnp.float32
        )
        return placed.astype(bf).reshape(rows_here, width)

    def send_back(values):
        pieces = values.reshape(capacity, stretch_len, width)
        picking = (codes_home[:, None] == capacity_index[None, :]).astype(bf)
        outgoing = jnp.einsum(
            "ec,cfw->efw", picking, pieces, preferred_element_type=jnp.float32
        ).astype(bf)
        arrived = exchange(outgoing)
        placed = jnp.einsum("es,efw->sfw", selector, arrived, preferred_element_type=jnp.float32)
        placed = placed + jnp.einsum(
            "cs,cfw->sfw", local_pick, pieces, preferred_element_type=jnp.float32
        )
        return placed.astype(bf).reshape(length, width)

    weight_lin, weight_gate = gather_weight(pw_weight)

    own = slice(2 * half_span, 2 * half_span + length)
    frames_ext = rims(frames[0], 2 * half_span)
    live_ext = rims(live_mask[0][:, None], 2 * half_span)
    grad_ext = rims(send_back(out_grad[0]), half_span)

    feature = jnp.arange(width, dtype=jnp.int32)
    to_lin = (feature[:, None] == feature_order("x", "y")[None, :]).astype(bf)
    to_gate = (feature[:, None] == feature_order("y", "x")[None, :]).astype(bf)
    normed, inverse_scale = normalize(frames_ext.astype(jnp.float32))
    normed_bf = normed.astype(bf)
    normed_lin = jnp.dot(normed_bf, to_lin, preferred_element_type=jnp.float32).astype(bf)
    normed_gate = jnp.dot(normed_bf, to_gate, preferred_element_type=jnp.float32).astype(bf)

    linear = jnp.dot(normed_lin, weight_lin, preferred_element_type=jnp.float32)
    gate = jax.nn.sigmoid(jnp.dot(normed_gate, weight_gate, preferred_element_type=jnp.float32))
    unit_ext = jnp.where(live_ext > 0, linear * gate, 0.0).astype(bf)

    inner = length + 2 * half_span
    live_inner = live_ext[half_span : half_span + inner].astype(jnp.float32)
    live_own = live_ext[own].astype(jnp.float32)
    mixed_time = live_inner * depthwise(unit_ext, kernel, inner)
    norm_time, norm_scale = normalize(mixed_time)
    sigma = jax.nn.sigmoid(norm_time)
    core_rows = slice(half_span, half_span + length)
    output_time = (
        frames[0].astype(jnp.float32) + norm_time[core_rows] * sigma[core_rows]
    ).astype(bf)
    mixed_rows = send_home(output_time)
    grad_norm = grad_ext.astype(jnp.float32) * sigma * (1.0 + norm_time * (1.0 - sigma))
    grad_mixed = (
        live_inner
        * norm_scale
        * (
            grad_norm
            - jnp.mean(grad_norm, axis=-1, keepdims=True)
            - norm_time * jnp.mean(grad_norm * norm_time, axis=-1, keepdims=True)
        )
    ).astype(bf)
    grad_unit = (live_own * depthwise(grad_mixed, kernel[::-1], length)).astype(bf)
    terms = kernel_terms(
        grad_mixed[core_rows], unit_ext[half_span : half_span + inner], length, taps
    )
    kernel_grad = sum_taps(terms) * loss_scale

    grad_float = grad_unit.astype(jnp.float32)
    gate_own = gate[own]
    pre_lin = (grad_float * gate_own).astype(bf)
    pre_gate = (grad_float * linear[own] * gate_own * (1.0 - gate_own)).astype(bf)

    def term(left, right):
        value = lax.dot_general(
            left[own], right, (((0,), (0,)), ((), ())), preferred_element_type=jnp.float32
        )
        return (loss_scale * value).astype(bf)

    weight_grad = scatter_weight(term(normed_lin, pre_lin), term(normed_gate, pre_gate))

    def back(pre, weight, order):
        value = lax.dot_general(
            pre, weight, (((1,), (1,)), ((), ())), preferred_element_type=jnp.float32
        )
        high = value.astype(bf)
        low = (value - high.astype(jnp.float32)).astype(bf)
        turn = (((1,), (1,)), ((), ()))
        return lax.dot_general(
            high, order, turn, preferred_element_type=jnp.float32
        ) + lax.dot_general(low, order, turn, preferred_element_type=jnp.float32)

    grad_normed = back(pre_lin, weight_lin, to_lin) + back(pre_gate, weight_gate, to_gate)
    normed_own = normed[own]
    branch = inverse_scale[own] * (
        grad_normed
        - jnp.mean(grad_normed, axis=-1, keepdims=True)
        - normed_own * jnp.mean(grad_normed * normed_own, axis=-1, keepdims=True)
    )
    named_rows = jnp.repeat(named_slot, stretch_len)[:, None]
    step_grad = grad_ext[core_rows].astype(jnp.float32) + branch
    frame_grad = jnp.where(named_rows, step_grad, 0.0).astype(bf)
    return (mixed_rows[None], frame_grad[None], weight_grad, kernel_grad)


def solution(mesh):
    fine = Mesh(mesh.devices.reshape(X, YH, Z, YL, CORE), ("x", "yh", "z", "yl", "core"))
    every = DP + TM
    placed = (
        P(DP, TM, None),
        P(DP, TM),
        P(DP, TM),
        P(every, None),
        P(),
        P(DP, TM, None),
    )
    return jax.shard_map(
        shards,
        mesh=fine,
        in_specs=placed,
        out_specs=(P(DP, TM, None), P(DP, TM, None), P(every, None), P()),
        check_vma=False,
    )
```

```python
import jax
import jax.numpy as jnp
from jax import lax
from jax.sharding import Mesh
from jax.sharding import PartitionSpec as P

EPSILON = 1e-05
X, YH, Z, YL, CORE = 4, 2, 8, 2, 2
Y = YH * YL
XA, YA, ZA, CA = "x", ("yh", "yl"), "z", "core"
DP = ("x", "yh")
TM = ("z", "yl", "core")
SHARE = 6


def swap(value):
    return lax.ppermute(value, CA, [(0, 1), (1, 0)])


def exchange(value, axis):
    return lax.all_to_all(value, axis, split_axis=0, concat_axis=0, tiled=True)


def gather(value, axis, count):
    rows, width = value.shape
    copies = jnp.broadcast_to(value[None], (count, rows, width))
    return exchange(copies, axis).reshape(count * rows, width)


def scatter(value, axis, count):
    rows, width = value.shape
    arrived = exchange(value.reshape(count, rows // count, width), axis)
    return jnp.sum(arrived.astype(jnp.float32), axis=0)


def shift(value, axis, count, by):
    return lax.ppermute(value, axis, [(i, (i + by) % count) for i in range(count)])


def gather_ring(value, axis, count):
    return jnp.concatenate([value] + [shift(value, axis, count, k) for k in range(1, count)], axis=0)


def scatter_ring(value, axis, count):
    rows = value.shape[0] // count
    total = value[:rows].astype(jnp.float32)
    for k in range(1, count):
        chunk = shift(value[k * rows : (k + 1) * rows], axis, count, -k)
        total = total + chunk.astype(jnp.float32)
    return total


def butterfly(value, axis, count):
    step = 1
    while step < count:
        value = value + lax.ppermute(value, axis, [(i, i ^ step) for i in range(count)])
        step *= 2
    return value


def after(value, earlier):
    return lax.optimization_barrier((value, earlier))[0]


def normalize(values):
    center = jnp.mean(values, axis=-1, keepdims=True)
    shifted = values - center
    spread = jnp.mean(shifted * shifted, axis=-1, keepdims=True)
    inverse_scale = lax.rsqrt(spread + EPSILON)
    return (shifted * inverse_scale, inverse_scale)


def depthwise(padded, kernel, length):
    running = jnp.zeros((length, padded.shape[1]), jnp.float32)
    for offset in range(kernel.shape[0]):
        running = running + kernel[offset] * padded[offset : offset + length].astype(jnp.float32)
    return running


def kernel_terms(grad_mixed, padded, length, taps):
    grad_float = grad_mixed.astype(jnp.float32)
    return jnp.stack(
        [
            jnp.sum(grad_float * padded[offset : offset + length].astype(jnp.float32), axis=0)
            for offset in range(taps)
        ]
    )


def rims(values, width, marks=None):
    count = Z * YL * CORE
    head = values[:width]
    tail = values[values.shape[0] - width :]
    if marks is not None:
        wide = (0, values.shape[1] - width)
        row = jnp.pad(marks.astype(values.dtype)[:width], wide)[None]
        head = jnp.concatenate([head, row], axis=0)
        row = jnp.pad(marks.astype(values.dtype)[marks.shape[0] - width :], wide)[None]
        tail = jnp.concatenate([tail, row], axis=0)
    before = lax.ppermute(tail, TM, [(i, i + 1) for i in range(count - 1)])
    after = lax.ppermute(head, TM, [(i + 1, i) for i in range(count - 1)])
    full = jnp.concatenate([before[:width], values, after[:width]], axis=0)
    if marks is None:
        return full
    sides = [side[width, :width].astype(marks.dtype) for side in (before, after)]
    return full, jnp.concatenate([sides[0], marks, sides[1]])


def feature_order(x_first):
    row = jnp.arange(X * Y * Z * CORE * SHARE, dtype=jnp.int32)
    within = row % SHARE
    zs = row // SHARE % Z
    second = row // (SHARE * Z) % 4
    first = row // (SHARE * Z * 4) % 4
    cs = (lax.axis_index(CA) + row // (SHARE * Z * 16)) % CORE
    xs, ky = (first, second) if x_first else (second, first)
    ys = (lax.axis_index(YA) - ky) % Y
    device = ((((xs * YH + ys // YL) * Z + zs) * YL) + ys % YL) * CORE + cs
    return device * SHARE + within


def gather_weight(shard):
    half = shard.shape[1] // 2
    column = gather(shard, ZA, Z)
    lin = gather_ring(column[:, :half], YA, Y)
    gate = gather(column[:, half:], XA, X)
    gate = gather_ring(gate, YA, Y)
    return gather(lin, XA, X), gate


def scatter_weight(lin, gate):
    bf = jnp.bfloat16
    gate = scatter_ring(gate, YA, Y).astype(bf)
    lin = scatter(lin, XA, X).astype(bf)
    lin = scatter_ring(lin, YA, Y).astype(bf)
    gate = scatter(gate, XA, X).astype(bf)
    return scatter(jnp.concatenate([lin, gate], axis=1), ZA, Z)


def sum_taps(terms, earlier):
    taps, width = terms.shape
    rows = 16
    core = lax.axis_index(CA)
    halves = jnp.pad(terms, ((0, CORE * rows - taps), (0, 0))).reshape(CORE, rows, width)
    part = lax.dynamic_index_in_dim(halves, core, 0, keepdims=False) + swap(
        lax.dynamic_index_in_dim(halves, 1 - core, 0, keepdims=False)
    )
    part = after(part, earlier)
    part = butterfly(butterfly(butterfly(part, ZA, Z), YA, Y), XA, X)
    other = swap(part)
    first, second = jnp.where(core == 0, part, other), jnp.where(core == 0, other, part)
    return jnp.concatenate([first, second], axis=0)[:taps]


def shards(frames, live_mask, stretch_target, pw_weight, kernel, out_grad):
    bf = jnp.bfloat16
    groups = X * YH
    own_group = lax.axis_index(DP)
    slot_count = stretch_target.shape[1]
    width = frames.shape[2]
    stretch_len = frames.shape[1] // slot_count
    capacity = out_grad.shape[1] // stretch_len
    per_peer = slot_count // 4
    entries = groups * per_peer
    taps = kernel.shape[0]
    half_span = (taps - 1) // 2
    length = slot_count * stretch_len
    rows_here = capacity * stretch_len
    loss_scale = float(groups * Z * YL * CORE * rows_here) ** (-0.5)

    target = stretch_target[0]
    named_slot = target >= 0
    dest_group = jnp.where(named_slot, target // capacity, -1)
    remote = named_slot & (dest_group != own_group)
    local = named_slot & (dest_group == own_group)
    slot_index = jnp.arange(slot_count, dtype=jnp.int32)
    entry_ids = jnp.arange(entries, dtype=jnp.int32)
    earlier = slot_index[:, None] > slot_index[None, :]
    alike = (dest_group[:, None] == dest_group[None, :]) & remote[None, :] & earlier
    rank_within = jnp.sum(alike.astype(jnp.int32), axis=1)
    entry_index = jnp.where(remote, dest_group * per_peer + rank_within, -1)
    selection = entry_index[None, :] == entry_ids[:, None]
    selector = selection.astype(bf)
    slot_codes = jnp.sum(jnp.where(selection, (target % capacity + 1)[None, :], 0), axis=1) - 1
    capacity_index = jnp.arange(capacity, dtype=jnp.int32)
    local_pick = ((target % capacity)[None, :] == capacity_index[:, None]) & local[None, :]
    local_pick = local_pick.astype(bf)

    codes_home = exchange(slot_codes, DP)

    def send_home(values):
        pieces = values.reshape(slot_count, stretch_len, width)
        outgoing = jnp.einsum(
            "es,sfw->efw", selector, pieces, preferred_element_type=jnp.float32
        ).astype(bf)
        arrived = exchange(outgoing, DP)
        placing = (codes_home[None, :] == capacity_index[:, None]).astype(bf)
        placed = jnp.einsum("ce,efw->cfw", placing, arrived, preferred_element_type=jnp.float32)
        placed = placed + jnp.einsum(
            "cs,sfw->cfw", local_pick, pieces, preferred_element_type=jnp.float32
        )
        return placed.astype(bf).reshape(rows_here, width)

    def send_back(values):
        pieces = values.reshape(capacity, stretch_len, width)
        picking = (codes_home[:, None] == capacity_index[None, :]).astype(bf)
        outgoing = jnp.einsum(
            "ec,cfw->efw", picking, pieces, preferred_element_type=jnp.float32
        ).astype(bf)
        arrived = exchange(outgoing, DP)
        placed = jnp.einsum("es,efw->sfw", selector, arrived, preferred_element_type=jnp.float32)
        placed = placed + jnp.einsum(
            "cs,cfw->sfw", local_pick, pieces, preferred_element_type=jnp.float32
        )
        return placed.astype(bf).reshape(length, width)

    weight_lin, weight_gate = gather_weight(pw_weight)
    cotangent = after(out_grad[0], (weight_lin, weight_gate))

    own = slice(2 * half_span, 2 * half_span + length)
    frames_ext, live_ext = rims(frames[0], 2 * half_span, live_mask[0])
    live_ext = live_ext[:, None]
    grad_ext = rims(send_back(cotangent), half_span)

    feature = jnp.arange(width, dtype=jnp.int32)
    to_lin = (feature[:, None] == feature_order(True)[None, :]).astype(bf)
    to_gate = (feature[:, None] == feature_order(False)[None, :]).astype(bf)
    normed, inverse_scale = normalize(frames_ext.astype(jnp.float32))
    normed_bf = normed.astype(bf)
    normed_lin = jnp.dot(normed_bf, to_lin, preferred_element_type=jnp.float32).astype(bf)
    normed_gate = jnp.dot(normed_bf, to_gate, preferred_element_type=jnp.float32).astype(bf)

    half = width // CORE
    lin_other, gate_other = swap(weight_lin), swap(weight_gate)

    def project(rows, here, there):
        return jnp.dot(rows[:, :half], here, preferred_element_type=jnp.float32) + jnp.dot(
            rows[:, half:], there, preferred_element_type=jnp.float32
        )

    linear = project(normed_lin, weight_lin, lin_other)
    gate = jax.nn.sigmoid(project(normed_gate, weight_gate, gate_other))
    unit_ext = jnp.where(live_ext > 0, linear * gate, 0.0).astype(bf)

    inner = length + 2 * half_span
    live_inner = live_ext[half_span : half_span + inner].astype(jnp.float32)
    live_own = live_ext[own].astype(jnp.float32)
    mixed_time = live_inner * depthwise(unit_ext, kernel, inner)
    norm_time, norm_scale = normalize(mixed_time)
    sigma = jax.nn.sigmoid(norm_time)
    core_rows = slice(half_span, half_span + length)
    output_time = (
        frames[0].astype(jnp.float32) + norm_time[core_rows] * sigma[core_rows]
    ).astype(bf)
    mixed_rows = send_home(output_time)
    grad_norm = grad_ext.astype(jnp.float32) * sigma * (1.0 + norm_time * (1.0 - sigma))
    grad_mixed = (
        live_inner
        * norm_scale
        * (
            grad_norm
            - jnp.mean(grad_norm, axis=-1, keepdims=True)
            - norm_time * jnp.mean(grad_norm * norm_time, axis=-1, keepdims=True)
        )
    ).astype(bf)
    grad_unit = (live_own * depthwise(grad_mixed, kernel[::-1], length)).astype(bf)
    terms = kernel_terms(
        grad_mixed[core_rows], unit_ext[half_span : half_span + inner], length, taps
    )
    grad_float = grad_unit.astype(jnp.float32)
    gate_own = gate[own]
    pre_lin = (grad_float * gate_own).astype(bf)
    pre_gate = (grad_float * linear[own] * gate_own * (1.0 - gate_own)).astype(bf)

    def term(left, right):
        value = lax.dot_general(
            left[own], right, (((0,), (0,)), ((), ())), preferred_element_type=jnp.float32
        )
        return (loss_scale * value).astype(bf)

    def half_grad(left, right):
        away = swap(term(left[:, half:], right))
        here = term(left[:, :half], right)
        return (here.astype(jnp.float32) + away.astype(jnp.float32)).astype(bf)

    grad_lin = half_grad(normed_lin, pre_lin)
    grad_gate = half_grad(normed_gate, pre_gate)
    kernel_grad = sum_taps(terms, (grad_lin, grad_gate)) * loss_scale
    pre_lin, pre_gate = after((pre_lin, pre_gate), (grad_lin, grad_gate))
    weight_grad = scatter_weight(after(grad_lin, mixed_rows), grad_gate)

    turn = (((1,), (1,)), ((), ()))

    def back(pre, here, there, order):
        value = jnp.concatenate(
            [
                lax.dot_general(pre, part, turn, preferred_element_type=jnp.float32)
                for part in (here, there)
            ],
            axis=1,
        )
        high = value.astype(bf)
        low = (value - high.astype(jnp.float32)).astype(bf)
        return lax.dot_general(
            high, order, turn, preferred_element_type=jnp.float32
        ) + lax.dot_general(low, order, turn, preferred_element_type=jnp.float32)

    grad_normed = back(pre_lin, weight_lin, lin_other, to_lin) + back(
        pre_gate, weight_gate, gate_other, to_gate
    )
    normed_own = normed[own]
    branch = inverse_scale[own] * (
        grad_normed
        - jnp.mean(grad_normed, axis=-1, keepdims=True)
        - normed_own * jnp.mean(grad_normed * normed_own, axis=-1, keepdims=True)
    )
    named_rows = jnp.repeat(named_slot, stretch_len)[:, None]
    step_grad = grad_ext[core_rows].astype(jnp.float32) + branch
    frame_grad = jnp.where(named_rows, step_grad, 0.0).astype(bf)
    return (mixed_rows[None], frame_grad[None], weight_grad, kernel_grad)


def solution(mesh):
    fine = Mesh(mesh.devices.reshape(X, YH, Z, YL, CORE), ("x", "yh", "z", "yl", "core"))
    every = DP + TM
    placed = (
        P(DP, TM, None),
        P(DP, TM),
        P(DP, TM),
        P(every, None),
        P(),
        P(DP, TM, None),
    )
    return jax.shard_map(
        shards,
        mesh=fine,
        in_specs=placed,
        out_specs=(P(DP, TM, None), P(DP, TM, None), P(every, None), P()),
        check_vma=False,
    )
```

```python
import jax
import jax.numpy as jnp
from jax import lax
from jax.sharding import Mesh
from jax.sharding import PartitionSpec as P

EPSILON = 1e-05
X, YH, Z, YL, CORE = 4, 2, 8, 2, 2
Y = YH * YL
XA, YA, ZA, CA = "x", ("yh", "yl"), "z", "core"
DP = ("x", "yh")
TM = ("z", "yl", "core")
CHIPS = ("z", "yl")
SHARE = 6
SPAN = 16
F32, BF16 = jnp.float32, jnp.bfloat16


def swap(value):
    return lax.ppermute(value, CA, [(0, 1), (1, 0)])


def pick(low, high):
    return jnp.where(lax.axis_index(CA) == 0, low, high)


def exchange(value, axis):
    return lax.all_to_all(value, axis, split_axis=0, concat_axis=0, tiled=True)


def gather(value, axis, count):
    rows, width = value.shape
    copies = jnp.broadcast_to(value[None], (count, rows, width))
    return exchange(copies, axis).reshape(count * rows, width)


def scatter(value, axis, count):
    rows, width = value.shape
    arrived = exchange(value.reshape(count, rows // count, width), axis)
    return jnp.sum(arrived.astype(F32), axis=0)


def shift(value, axis, count, by):
    return lax.ppermute(value, axis, [(i, (i + by) % count) for i in range(count)])


def gather_ring(value, axis, count):
    return jnp.concatenate([value] + [shift(value, axis, count, k) for k in range(1, count)], axis=0)


def ring_chunks(value, axis, count):
    rows = value.shape[0] // count
    return [value[:rows]] + [
        shift(value[k * rows : (k + 1) * rows], axis, count, -k) for k in range(1, count)
    ]


def add_up(chunks):
    total = chunks[0].astype(F32)
    for chunk in chunks[1:]:
        total = total + chunk.astype(F32)
    return total.astype(BF16)


def tie(*values):
    return lax.optimization_barrier(values)


def normalize(values):
    center = jnp.mean(values, axis=-1, keepdims=True)
    shifted = values - center
    spread = jnp.mean(shifted * shifted, axis=-1, keepdims=True)
    inverse_scale = lax.rsqrt(spread + EPSILON)
    return (shifted * inverse_scale, inverse_scale)


def depthwise(padded, kernel, length):
    running = jnp.zeros((length, padded.shape[1]), F32)
    for offset in range(kernel.shape[0]):
        running = running + kernel[offset] * padded[offset : offset + length].astype(F32)
    return running


def kernel_terms(grad_mixed, padded, length, taps):
    grad_float = grad_mixed.astype(F32)
    return jnp.stack(
        [
            jnp.sum(grad_float * padded[offset : offset + length].astype(F32), axis=0)
            for offset in range(taps)
        ]
    )


def marked(values, marks):
    row = jnp.pad(marks.astype(values.dtype), (0, values.shape[1] - marks.shape[0]))[None]
    return jnp.concatenate([values, row], axis=0)


def both_cores(own, other):
    return pick(jnp.concatenate([own, other], axis=0), jnp.concatenate([other, own], axis=0))


def from_neighbours(head, tail):
    count = Z * YL
    before = lax.ppermute(tail, CHIPS, [(i, i + 1) for i in range(count - 1)])
    after_ = lax.ppermute(head, CHIPS, [(i + 1, i) for i in range(count - 1)])
    return before, after_


def feature_order(x_first):
    row = jnp.arange(X * Y * Z * CORE * SHARE, dtype=jnp.int32)
    within = row % (CORE * SHARE)
    zs = row // (CORE * SHARE) % Z
    second = row // (CORE * SHARE * Z) % 4
    first = row // (CORE * SHARE * Z * 4) % 4
    xs, ky = (first, second) if x_first else (second, first)
    ys = (lax.axis_index(YA) - ky) % Y
    device = (((xs * YH + ys // YL) * Z + zs) * YL + ys % YL) * CORE
    return device * SHARE + within


def own_columns(value):
    rows, width = value.shape
    parts = value.reshape(rows, 2, CORE, width // 4)
    low = parts[:, :, 0].reshape(rows, width // 2)
    high = parts[:, :, 1].reshape(rows, width // 2)
    return pick(low, high), pick(high, low)


def gather_weight(pair):
    half = pair.shape[1] // 2
    column = gather(pair, ZA, Z)
    lin = gather_ring(column[:, :half], YA, Y)
    gate = gather(column[:, half:], XA, X)
    gate = gather_ring(gate, YA, Y)
    return gather(lin, XA, X), gate


def scatter_rest(lin, gate, part):
    rows, width = lin.shape[0] // Y, lin.shape[1]
    taps = part.shape[0]
    stacked = jnp.concatenate(
        [piece for k in range(Y) for piece in (lin[k * rows : (k + 1) * rows], part)], axis=0
    )
    lin = add_up(ring_chunks(stacked, YA, Y))
    part = lin[rows:].reshape(taps // 2, 2 * width)
    gate = scatter(gate, XA, X).astype(BF16)
    pair = jnp.concatenate([lin[:rows], gate], axis=1).reshape(Z, rows // Z, 2 * width)
    full = jnp.concatenate([pair, jnp.broadcast_to(part[None], (Z,) + part.shape)], axis=1)
    total = jnp.sum(exchange(full, ZA).astype(F32), axis=0)
    low, high, part = total[:SHARE], total[SHARE : 2 * SHARE], total[2 * SHARE :]
    mine = pick(low, high)
    there = swap(jnp.concatenate([pick(high, low), part], axis=0))
    other = there[:SHARE]
    first, second = pick(mine, other), pick(other, mine)
    weight_grad = jnp.concatenate(
        [first[:, :width], second[:, :width], first[:, width:], second[:, width:]], axis=1
    )
    part, other = part.reshape(taps, width), there[SHARE:].reshape(taps, width)
    part = jnp.concatenate([pick(part, other), pick(other, part)], axis=1)
    return weight_grad, gather(part, XA, X)


def shards(frames, live_mask, stretch_target, pw_weight, kernel, out_grad):
    groups = X * YH
    own_group = lax.axis_index(DP)
    slot_count = stretch_target.shape[1]
    width = frames.shape[2]
    stretch_len = frames.shape[1] // slot_count
    capacity = out_grad.shape[1] // stretch_len
    per_peer = slot_count // 4
    entries = groups * per_peer
    taps = kernel.shape[0]
    length = slot_count * stretch_len
    rows_here = capacity * stretch_len
    half = width // CORE
    loss_scale = float(groups * Z * YL * CORE * rows_here) ** (-0.5)
    capacity_index = jnp.arange(capacity, dtype=jnp.int32)
    entry_ids = jnp.arange(entries, dtype=jnp.int32)
    slot_index = jnp.arange(slot_count, dtype=jnp.int32)
    earlier = slot_index[:, None] > slot_index[None, :]

    columns, others = own_columns(pw_weight)
    pair = both_cores(columns, swap(others))
    pair, frames, stretch_target = tie(pair, frames, stretch_target)
    weight_lin, weight_gate = gather_weight(pair)

    def entries_of(target, group):
        dest = jnp.where(target >= 0, target // capacity, -1)
        away = (target >= 0) & (dest != group)
        alike = (dest[:, None] == dest[None, :]) & away[None, :] & earlier
        rank = jnp.sum(alike.astype(jnp.int32), axis=1)
        return jnp.where(away, dest * per_peer + rank, -1)

    target = stretch_target[0]
    named_slot = target >= 0
    local = named_slot & (target // capacity == own_group)
    selector = (entries_of(target, own_group)[None, :] == entry_ids[:, None]).astype(BF16)
    local_pick = ((target % capacity)[None, :] == capacity_index[:, None]) & local[None, :]
    local_pick = local_pick.astype(BF16)

    all_targets = lax.all_gather(stretch_target, DP, axis=0, tiled=True)
    group_ids = jnp.arange(groups, dtype=jnp.int32)
    arriving = jax.vmap(entries_of)(all_targets, group_ids)
    wanted = own_group * per_peer + jnp.arange(per_peer, dtype=jnp.int32)
    carried = arriving[:, None, :] == wanted[None, :, None]
    codes_home = (
        jnp.sum(jnp.where(carried, (all_targets % capacity + 1)[:, None, :], 0), axis=2) - 1
    ).reshape(entries)

    def send_home(values):
        pieces = values.reshape(slot_count, stretch_len, width)
        outgoing = jnp.einsum(
            "es,sfw->efw", selector, pieces, preferred_element_type=F32
        ).astype(BF16)
        arrived = exchange(outgoing, DP)
        placing = (codes_home[None, :] == capacity_index[:, None]).astype(BF16)
        placed = jnp.einsum("ce,efw->cfw", placing, arrived, preferred_element_type=F32)
        placed = placed + jnp.einsum("cs,sfw->cfw", local_pick, pieces, preferred_element_type=F32)
        return placed.astype(BF16).reshape(rows_here, width)

    def send_back(values, unit):
        pieces = values.reshape(capacity, stretch_len, width)
        picking = (codes_home[:, None] == capacity_index[None, :]).astype(BF16)
        outgoing = jnp.einsum("ec,cfw->efw", picking, pieces, preferred_element_type=F32).astype(BF16)
        arrived, unit = tie(exchange(outgoing, DP), unit)
        placed = jnp.einsum("es,efw->sfw", selector, arrived, preferred_element_type=F32)
        placed = placed + jnp.einsum("cs,cfw->sfw", local_pick, pieces, preferred_element_type=F32)
        return placed.astype(BF16).reshape(length, width), unit

    window = CORE * length
    outer = 2 * SPAN
    normed, inverse_scale = normalize(frames[0].astype(F32))
    packet = marked(normed.astype(BF16), live_mask[0])
    packet_other = swap(packet)
    rows_win = both_cores(packet[:length], packet_other[:length])
    live_win = both_cores(packet[length, :length], packet_other[length, :length])
    before, behind = from_neighbours(
        marked(rows_win[:outer], live_win[:outer]),
        marked(rows_win[window - outer :], live_win[window - outer :]),
    )
    rows_ext = jnp.concatenate([before[:outer], rows_win, behind[:outer]], axis=0)
    live_ext = jnp.concatenate([before[outer, :outer], live_win, behind[outer, :outer]]).astype(F32)
    live_ext = live_ext[:, None]

    feature = jnp.arange(width, dtype=jnp.int32)
    to_lin = (feature[:, None] == feature_order(True)[None, :]).astype(BF16)
    to_gate = (feature[:, None] == feature_order(False)[None, :]).astype(BF16)
    normed_lin = jnp.dot(rows_ext, to_lin, preferred_element_type=F32).astype(BF16)
    normed_gate = jnp.dot(rows_ext, to_gate, preferred_element_type=F32).astype(BF16)

    cotangent, weight_lin, weight_gate, normed_lin, normed_gate = tie(
        out_grad[0], weight_lin, weight_gate, normed_lin, normed_gate
    )
    linear = jnp.dot(normed_lin, weight_lin, preferred_element_type=F32)
    gate = jax.nn.sigmoid(jnp.dot(normed_gate, weight_gate, preferred_element_type=F32))
    unit_ext = jnp.where(live_ext > 0, linear * gate, 0.0).astype(BF16)

    grad_time, unit_ext = send_back(cotangent, unit_ext)
    mine = pick(grad_time[:, :half], grad_time[:, half:])
    grad_win = both_cores(mine, swap(pick(grad_time[:, half:], grad_time[:, :half])))
    before, behind = from_neighbours(grad_win[:SPAN], grad_win[window - SPAN :])
    grad_ext = jnp.concatenate([before, grad_win, behind], axis=0).astype(F32)

    core = lax.axis_index(CA)
    taps_own = lax.dynamic_slice_in_dim(kernel, core * half, half, axis=1)
    inner = window + 2 * SPAN
    live_inner = live_ext[SPAN : SPAN + inner]
    live_own = live_ext[outer : outer + window]
    mixed_time = live_inner * depthwise(unit_ext[1:], taps_own, inner)
    mean_own = jnp.mean(mixed_time, axis=-1)
    rest_own = mixed_time - mean_own[:, None]
    square_own = jnp.sum(rest_own * rest_own, axis=-1)
    mean_there, square_there = swap(jnp.stack([mean_own, square_own]))
    apart = 0.5 * (mean_there - mean_own)
    spread = (square_own + square_there) / width + apart * apart
    norm_scale = lax.rsqrt(spread + EPSILON)[:, None]
    norm_time = (rest_own - apart[:, None]) * norm_scale
    sigma = jax.nn.sigmoid(norm_time)
    inner_rows = slice(SPAN, SPAN + window)
    silu = (norm_time * sigma)[inner_rows].astype(BF16)
    silu_low, silu_high = silu[:length], silu[length:]
    silu_there = swap(pick(silu_high, silu_low))
    silu_here = pick(silu_low, silu_high)
    silu_own = jnp.concatenate([pick(silu_here, silu_there), pick(silu_there, silu_here)], axis=1)
    output_time = (frames[0].astype(F32) + silu_own.astype(F32)).astype(BF16)

    grad_norm = grad_ext * sigma * (1.0 + norm_time * (1.0 - sigma))
    sums = jnp.stack([jnp.sum(grad_norm, axis=-1), jnp.sum(grad_norm * norm_time, axis=-1)])
    means = (sums + swap(sums)) / width
    grad_mixed = (
        live_inner * norm_scale * (grad_norm - means[0][:, None] - norm_time * means[1][:, None])
    ).astype(BF16)
    grad_mixed, output_time = tie(grad_mixed, output_time)
    mixed_rows = send_home(output_time)
    grad_unit = (live_own * depthwise(grad_mixed[1:], taps_own[::-1], window)).astype(BF16)
    terms = kernel_terms(grad_mixed[inner_rows], unit_ext[SPAN + 1 :], window, taps)

    outer_rows = slice(outer, outer + window)
    grad_float = grad_unit.astype(F32)
    gate_own = gate[outer_rows]
    pre_lin = (grad_float * gate_own).astype(BF16)
    pre_gate = (grad_float * linear[outer_rows] * gate_own * (1.0 - gate_own)).astype(BF16)

    def term(left, right):
        value = lax.dot_general(
            left[outer_rows], right, (((0,), (0,)), ((), ())), preferred_element_type=F32
        )
        return (loss_scale * value).astype(BF16)

    term_lin, term_gate = term(normed_lin, pre_lin), term(normed_gate, pre_gate)
    terms = (loss_scale * jnp.pad(terms, ((0, 1), (0, 0)))).astype(BF16)
    term_lin, term_gate, mixed_rows = tie(term_lin, term_gate, mixed_rows)
    chunks = ring_chunks(term_gate, YA, Y)
    chunks[1], pre_lin, pre_gate = tie(chunks[1], pre_lin, pre_gate)
    rows, part_rows = width // X, terms.shape[0] // X
    stacked = jnp.concatenate(
        [
            piece
            for k in range(X)
            for piece in (
                term_lin[k * rows : (k + 1) * rows],
                terms[k * part_rows : (k + 1) * part_rows],
            )
        ],
        axis=0,
    )
    lin, gate_sum = tie(scatter(stacked, XA, X).astype(BF16), add_up(chunks))
    weight_grad, kernel_grad = scatter_rest(lin[:rows], gate_sum, lin[rows:])
    kernel_grad = kernel_grad[:taps]

    turn = (((1,), (1,)), ((), ()))

    def back(pre, weight, order):
        value = lax.dot_general(pre, weight, turn, preferred_element_type=F32).astype(BF16)
        return lax.dot_general(value, order, turn, preferred_element_type=F32)

    partial_grad = back(pre_lin, weight_lin, to_lin) + back(pre_gate, weight_gate, to_gate)
    low, high = partial_grad[:length], partial_grad[length:]
    grad_normed = pick(low, high) + swap(pick(high, low).astype(BF16)).astype(F32)
    branch = inverse_scale * (
        grad_normed
        - jnp.mean(grad_normed, axis=-1, keepdims=True)
        - normed * jnp.mean(grad_normed * normed, axis=-1, keepdims=True)
    )
    named_rows = jnp.repeat(named_slot, stretch_len)[:, None]
    frame_grad = jnp.where(named_rows, grad_time.astype(F32) + branch, 0.0).astype(BF16)
    return (mixed_rows[None], frame_grad[None], weight_grad, kernel_grad)


def solution(mesh):
    fine = Mesh(mesh.devices.reshape(X, YH, Z, YL, CORE), ("x", "yh", "z", "yl", "core"))
    every = DP + TM
    placed = (
        P(DP, TM, None),
        P(DP, TM),
        P(DP, TM),
        P(every, None),
        P(),
        P(DP, TM, None),
    )
    return jax.shard_map(
        shards,
        mesh=fine,
        in_specs=placed,
        out_specs=(P(DP, TM, None), P(DP, TM, None), P(every, None), P()),
        check_vma=False,
    )
```

```python
import jax
import jax.numpy as jnp
from jax import lax
from jax.sharding import Mesh
from jax.sharding import PartitionSpec as P

EPSILON = 1e-05
X, YH, Z, YL, CORE = 4, 2, 8, 2, 2
Y = YH * YL
XA, YA, ZA, CA = "x", ("yh", "yl"), "z", "core"
DP = ("x", "yh")
TM = ("z", "yl", "core")
CHIPS = ("z", "yl")
SHARE = 6
SPAN = 16
F32, BF16 = jnp.float32, jnp.bfloat16


def swap(value):
    return lax.ppermute(value, CA, [(0, 1), (1, 0)])


def pick(low, high):
    return jnp.where(lax.axis_index(CA) == 0, low, high)


def exchange(value, axis):
    return lax.all_to_all(value, axis, split_axis=0, concat_axis=0, tiled=True)


def gather(value, axis, count):
    rows, width = value.shape
    copies = jnp.broadcast_to(value[None], (count, rows, width))
    return exchange(copies, axis).reshape(count * rows, width)


def scatter(value, axis, count):
    rows, width = value.shape
    arrived = exchange(value.reshape(count, rows // count, width), axis)
    return jnp.sum(arrived.astype(F32), axis=0)


def shift(value, axis, count, by):
    return lax.ppermute(value, axis, [(i, (i + by) % count) for i in range(count)])


def gather_ring(value, axis, count):
    return jnp.concatenate([value] + [shift(value, axis, count, k) for k in range(1, count)], axis=0)


def ring_chunks(value, axis, count):
    rows = value.shape[0] // count
    return [value[:rows]] + [
        shift(value[k * rows : (k + 1) * rows], axis, count, -k) for k in range(1, count)
    ]


def add_up(chunks):
    total = chunks[0].astype(F32)
    for chunk in chunks[1:]:
        total = total + chunk.astype(F32)
    return total.astype(BF16)


def tie(*values):
    return lax.optimization_barrier(values)


def normalize(values):
    center = jnp.mean(values, axis=-1, keepdims=True)
    shifted = values - center
    spread = jnp.mean(shifted * shifted, axis=-1, keepdims=True)
    inverse_scale = lax.rsqrt(spread + EPSILON)
    return (shifted * inverse_scale, inverse_scale)


def depthwise(padded, kernel, length):
    running = jnp.zeros((length, padded.shape[1]), F32)
    for offset in range(kernel.shape[0]):
        running = running + kernel[offset] * padded[offset : offset + length].astype(F32)
    return running


def kernel_terms(grad_mixed, padded, length, taps):
    grad_float = grad_mixed.astype(F32)
    return jnp.stack(
        [
            jnp.sum(grad_float * padded[offset : offset + length].astype(F32), axis=0)
            for offset in range(taps)
        ]
    )


def marked(values, marks):
    row = jnp.pad(marks.astype(values.dtype), (0, values.shape[1] - marks.shape[0]))[None]
    return jnp.concatenate([values, row], axis=0)


def both_cores(own, other):
    return pick(jnp.concatenate([own, other], axis=0), jnp.concatenate([other, own], axis=0))


def from_neighbours(head, tail):
    count = Z * YL
    before = lax.ppermute(tail, CHIPS, [(i, i + 1) for i in range(count - 1)])
    after_ = lax.ppermute(head, CHIPS, [(i + 1, i) for i in range(count - 1)])
    return before, after_


def from_edges(near, far):
    ends = range(Z * YL - 1)
    ahead = [(2 * i + 1, 2 * i + 2) for i in ends] + [(2 * i + 2, 2 * i + 1) for i in ends]
    along = [(2 * i + 1, 2 * i + 3) for i in ends] + [(2 * i + 2, 2 * i) for i in ends]
    return lax.ppermute(near, TM, ahead), lax.ppermute(far, TM, along)


def feature_order(x_first):
    row = jnp.arange(X * Y * Z * CORE * SHARE, dtype=jnp.int32)
    within = row % (CORE * SHARE)
    zs = row // (CORE * SHARE) % Z
    second = row // (CORE * SHARE * Z) % 4
    first = row // (CORE * SHARE * Z * 4) % 4
    xs, ky = (first, second) if x_first else (second, first)
    ys = (lax.axis_index(YA) - ky) % Y
    device = (((xs * YH + ys // YL) * Z + zs) * YL + ys % YL) * CORE
    return device * SHARE + within


def own_columns(value):
    rows, width = value.shape
    parts = value.reshape(rows, 2, CORE, width // 4)
    low = parts[:, :, 0].reshape(rows, width // 2)
    high = parts[:, :, 1].reshape(rows, width // 2)
    return pick(low, high), pick(high, low)


def gather_weight(pair, target):
    rows, width = pair.shape[0] * Z, pair.shape[1] // 2
    slots = target.shape[1]

    def numbers(values):
        return jnp.pad(values.astype(BF16), ((0, 7), (0, width - values.shape[1])))

    column = gather(pair, ZA, Z)
    lin = gather_ring(column[:, :width], YA, Y)
    gate = jnp.concatenate([column[:, width:], numbers(target)], axis=0)
    gate = gather(gate, XA, X).reshape(X, rows + 8, width)
    here = gate[:, rows, :slots]
    gate = gate[:, :rows].reshape(X * rows, width)
    gate = jnp.concatenate([gate, numbers(here.reshape(1, X * slots))], axis=0)
    chunks = [gate] + [shift(gate, YA, Y, k) for k in range(1, Y)]
    there = chunks[Y // YH][X * rows, : X * slots].reshape(X, slots)
    first = lax.axis_index("yh") == 0
    targets = jnp.stack([jnp.where(first, here, there), jnp.where(first, there, here)], axis=1)
    gate = jnp.concatenate([chunk[: X * rows] for chunk in chunks], axis=0)
    return gather(lin, XA, X), gate, targets.reshape(X * YH, slots).astype(jnp.int32)


def in_turn(pieces, at):
    count = len(pieces)
    ring = jnp.stack([pieces[(-j) % count] for j in range(2 * count - 1)])
    turned = lax.dynamic_slice_in_dim(ring, (-at) % count, count, axis=0)
    return turned.reshape(count * pieces[0].shape[0], pieces[0].shape[1])


def scatter_rest(lin, gate, part):
    rows, width = lin.shape[0] // Y, lin.shape[1]
    taps = part.shape[0]
    stacked = jnp.concatenate(
        [piece for k in range(Y) for piece in (lin[k * rows : (k + 1) * rows], part)], axis=0
    )
    lin = add_up(ring_chunks(stacked, YA, Y))
    part = lin[rows:].reshape(taps // 2, 2 * width)
    gate = scatter(gate, XA, X).astype(BF16)
    pair = jnp.concatenate([lin[:rows], gate], axis=1).reshape(Z, rows // Z, 2 * width)
    full = jnp.concatenate([pair, jnp.broadcast_to(part[None], (Z,) + part.shape)], axis=1)
    total = jnp.sum(exchange(full, ZA).astype(F32), axis=0)
    low, high, part = total[:SHARE], total[SHARE : 2 * SHARE], total[2 * SHARE :]
    mine = pick(low, high)
    there = swap(jnp.concatenate([pick(high, low), part], axis=0))
    other = there[:SHARE]
    first, second = pick(mine, other), pick(other, mine)
    weight_grad = jnp.concatenate(
        [first[:, :width], second[:, :width], first[:, width:], second[:, width:]], axis=1
    )
    part, other = part.reshape(taps, width), there[SHARE:].reshape(taps, width)
    part = jnp.concatenate([pick(part, other), pick(other, part)], axis=1)
    parts = [part] + [shift(part, XA, X, k) for k in range(1, X)]
    return weight_grad, in_turn(parts, lax.axis_index(XA))


def shards(frames, live_mask, stretch_target, pw_weight, kernel, out_grad):
    groups = X * YH
    own_group = lax.axis_index(DP)
    slot_count = stretch_target.shape[1]
    width = frames.shape[2]
    stretch_len = frames.shape[1] // slot_count
    capacity = out_grad.shape[1] // stretch_len
    per_peer = slot_count // 4
    entries = groups * per_peer
    taps = kernel.shape[0]
    length = slot_count * stretch_len
    rows_here = capacity * stretch_len
    half = width // CORE
    loss_scale = float(groups * Z * YL * CORE * rows_here) ** (-0.5)
    capacity_index = jnp.arange(capacity, dtype=jnp.int32)
    entry_ids = jnp.arange(entries, dtype=jnp.int32)
    slot_index = jnp.arange(slot_count, dtype=jnp.int32)
    earlier = slot_index[:, None] > slot_index[None, :]

    columns, others = own_columns(pw_weight)
    pair = both_cores(columns, swap(others))
    pair, frames, stretch_target = tie(pair, frames, stretch_target)
    weight_lin, weight_gate, all_targets = gather_weight(pair, stretch_target)

    def entries_of(target, group):
        dest = jnp.where(target >= 0, target // capacity, -1)
        away = (target >= 0) & (dest != group)
        alike = (dest[:, None] == dest[None, :]) & away[None, :] & earlier
        rank = jnp.sum(alike.astype(jnp.int32), axis=1)
        return jnp.where(away, dest * per_peer + rank, -1)

    target = stretch_target[0]
    named_slot = target >= 0
    local = named_slot & (target // capacity == own_group)
    selector = (entries_of(target, own_group)[None, :] == entry_ids[:, None]).astype(BF16)
    local_pick = ((target % capacity)[None, :] == capacity_index[:, None]) & local[None, :]
    local_pick = local_pick.astype(BF16)

    group_ids = jnp.arange(groups, dtype=jnp.int32)
    arriving = jax.vmap(entries_of)(all_targets, group_ids)
    wanted = own_group * per_peer + jnp.arange(per_peer, dtype=jnp.int32)
    carried = arriving[:, None, :] == wanted[None, :, None]
    codes_home = (
        jnp.sum(jnp.where(carried, (all_targets % capacity + 1)[:, None, :], 0), axis=2) - 1
    ).reshape(entries)

    def send_home(values):
        pieces = values.reshape(slot_count, stretch_len, width)
        outgoing = jnp.einsum(
            "es,sfw->efw", selector, pieces, preferred_element_type=F32
        ).astype(BF16)
        arrived = exchange(outgoing, DP)
        placing = (codes_home[None, :] == capacity_index[:, None]).astype(BF16)
        placed = jnp.einsum("ce,efw->cfw", placing, arrived, preferred_element_type=F32)
        placed = placed + jnp.einsum("cs,sfw->cfw", local_pick, pieces, preferred_element_type=F32)
        return placed.astype(BF16).reshape(rows_here, width)

    def send_back(values, mark):
        pieces = values.reshape(capacity, stretch_len, width)
        picking = (codes_home[:, None] == capacity_index[None, :]).astype(BF16)
        outgoing = jnp.einsum("ec,cfw->efw", picking, pieces, preferred_element_type=F32).astype(BF16)
        arrived, mark = tie(exchange(outgoing, DP), mark)
        placed = jnp.einsum("es,efw->sfw", selector, arrived, preferred_element_type=F32)
        placed = placed + jnp.einsum("cs,cfw->sfw", local_pick, pieces, preferred_element_type=F32)
        return placed.astype(BF16).reshape(length, width), mark

    window = CORE * length
    outer = 2 * SPAN
    normed, inverse_scale = normalize(frames[0].astype(F32))
    packet = marked(normed.astype(BF16), live_mask[0])
    packet_other = swap(packet)
    rows_win = both_cores(packet[:length], packet_other[:length])
    live_win = both_cores(packet[length, :length], packet_other[length, :length])
    before, behind = from_neighbours(
        marked(rows_win[:outer], live_win[:outer]),
        marked(rows_win[window - outer :], live_win[window - outer :]),
    )
    rows_ext = jnp.concatenate([before[:outer], rows_win, behind[:outer]], axis=0)
    live_ext = jnp.concatenate([before[outer, :outer], live_win, behind[outer, :outer]]).astype(F32)
    live_ext = live_ext[:, None]

    feature = jnp.arange(width, dtype=jnp.int32)
    to_lin = (feature[:, None] == feature_order(True)[None, :]).astype(BF16)
    to_gate = (feature[:, None] == feature_order(False)[None, :]).astype(BF16)
    normed_lin = jnp.dot(rows_ext, to_lin, preferred_element_type=F32).astype(BF16)
    normed_gate = jnp.dot(rows_ext, to_gate, preferred_element_type=F32).astype(BF16)

    cotangent, weight_lin, weight_gate, normed_lin, normed_gate = tie(
        out_grad[0], weight_lin, weight_gate, normed_lin, normed_gate
    )
    linear = jnp.dot(normed_lin, weight_lin, preferred_element_type=F32)
    gate = jax.nn.sigmoid(jnp.dot(normed_gate, weight_gate, preferred_element_type=F32))
    unit_ext = jnp.where(live_ext > 0, linear * gate, 0.0).astype(BF16)

    core = lax.axis_index(CA)
    taps_own = lax.dynamic_slice_in_dim(kernel, core * half, half, axis=1)
    inner = window + 2 * SPAN
    live_inner = live_ext[SPAN : SPAN + inner]
    live_own = live_ext[outer : outer + window]
    mixed_time = live_inner * depthwise(unit_ext[1:], taps_own, inner)
    grad_time, mixed_time = send_back(cotangent, mixed_time)
    mine = pick(grad_time[:, :half], grad_time[:, half:])
    others = pick(grad_time[:, half:], grad_time[:, :half])
    grad_win = both_cores(mine, swap(others))
    near, far = from_edges(
        pick(others[:SPAN], others[length - SPAN :]), pick(mine[:SPAN], mine[length - SPAN :])
    )
    grad_ext = jnp.concatenate([pick(near, far), grad_win, pick(far, near)], axis=0).astype(F32)

    mean_own = jnp.mean(mixed_time, axis=-1)
    rest_own = mixed_time - mean_own[:, None]
    square_own = jnp.sum(rest_own * rest_own, axis=-1)
    mean_there, square_there = swap(jnp.stack([mean_own, square_own]))
    apart = 0.5 * (mean_there - mean_own)
    spread = (square_own + square_there) / width + apart * apart
    norm_scale = lax.rsqrt(spread + EPSILON)[:, None]
    norm_time = (rest_own - apart[:, None]) * norm_scale
    sigma = jax.nn.sigmoid(norm_time)
    inner_rows = slice(SPAN, SPAN + window)
    silu = (norm_time * sigma)[inner_rows].astype(BF16)
    silu_low, silu_high = silu[:length], silu[length:]
    silu_there = swap(pick(silu_high, silu_low))
    silu_here = pick(silu_low, silu_high)
    silu_own = jnp.concatenate([pick(silu_here, silu_there), pick(silu_there, silu_here)], axis=1)
    output_time = (frames[0].astype(F32) + silu_own.astype(F32)).astype(BF16)

    grad_norm = grad_ext * sigma * (1.0 + norm_time * (1.0 - sigma))
    sums = jnp.stack([jnp.sum(grad_norm, axis=-1), jnp.sum(grad_norm * norm_time, axis=-1)])
    means = (sums + swap(sums)) / width
    grad_mixed = (
        live_inner * norm_scale * (grad_norm - means[0][:, None] - norm_time * means[1][:, None])
    ).astype(BF16)
    grad_mixed, output_time = tie(grad_mixed, output_time)
    mixed_rows = send_home(output_time)
    grad_unit = (live_own * depthwise(grad_mixed[1:], taps_own[::-1], window)).astype(BF16)
    terms = kernel_terms(grad_mixed[inner_rows], unit_ext[SPAN + 1 :], window, taps)

    outer_rows = slice(outer, outer + window)
    grad_float = grad_unit.astype(F32)
    gate_own = gate[outer_rows]
    pre_lin = (grad_float * gate_own).astype(BF16)
    pre_gate = (grad_float * linear[outer_rows] * gate_own * (1.0 - gate_own)).astype(BF16)

    def term(left, right):
        value = lax.dot_general(
            left[outer_rows], right, (((0,), (0,)), ((), ())), preferred_element_type=F32
        )
        return (loss_scale * value).astype(BF16)

    term_lin, term_gate = term(normed_lin, pre_lin), term(normed_gate, pre_gate)
    terms = (loss_scale * jnp.pad(terms, ((0, 1), (0, 0)))).astype(BF16)
    term_lin, term_gate, mixed_rows = tie(term_lin, term_gate, mixed_rows)
    chunks = ring_chunks(term_gate, YA, Y)
    chunks[1], pre_lin = tie(chunks[1], pre_lin)
    rows, part_rows = width // X, terms.shape[0] // X
    stacked = jnp.concatenate(
        [
            piece
            for k in range(X)
            for piece in (
                term_lin[k * rows : (k + 1) * rows],
                terms[k * part_rows : (k + 1) * part_rows],
            )
        ],
        axis=0,
    )
    lin, gate_sum, pre_gate = tie(
        scatter(stacked, XA, X).astype(BF16), add_up(chunks), pre_gate
    )
    weight_grad, kernel_grad = scatter_rest(lin[:rows], gate_sum, lin[rows:])
    kernel_grad = kernel_grad[:taps]

    turn = (((1,), (1,)), ((), ()))

    def back(pre, weight, order):
        value = lax.dot_general(pre, weight, turn, preferred_element_type=F32).astype(BF16)
        return lax.dot_general(value, order, turn, preferred_element_type=F32)

    partial_grad = back(pre_lin, weight_lin, to_lin) + back(pre_gate, weight_gate, to_gate)
    low, high = partial_grad[:length], partial_grad[length:]
    grad_normed = pick(low, high) + swap(pick(high, low).astype(BF16)).astype(F32)
    branch = inverse_scale * (
        grad_normed
        - jnp.mean(grad_normed, axis=-1, keepdims=True)
        - normed * jnp.mean(grad_normed * normed, axis=-1, keepdims=True)
    )
    named_rows = jnp.repeat(named_slot, stretch_len)[:, None]
    frame_grad = jnp.where(named_rows, grad_time.astype(F32) + branch, 0.0).astype(BF16)
    return (mixed_rows[None], frame_grad[None], weight_grad, kernel_grad)


def solution(mesh):
    fine = Mesh(mesh.devices.reshape(X, YH, Z, YL, CORE), ("x", "yh", "z", "yl", "core"))
    every = DP + TM
    placed = (
        P(DP, TM, None),
        P(DP, TM),
        P(DP, TM),
        P(every, None),
        P(),
        P(DP, TM, None),
    )
    return jax.shard_map(
        shards,
        mesh=fine,
        in_specs=placed,
        out_specs=(P(DP, TM, None), P(DP, TM, None), P(every, None), P()),
        check_vma=False,
    )
```

```python
import jax
import jax.numpy as jnp
from jax import lax
from jax.experimental import pallas as pl
from jax.experimental.pallas import tpu as pltpu
from jax.sharding import Mesh
from jax.sharding import PartitionSpec as P

EPSILON = 1e-05
X, YH, Z, YL, CORE = 4, 2, 8, 2, 2
Y = YH * YL
XA, YA, ZA, CA = "x", ("yh", "yl"), "z", "core"
DP = ("x", "yh")
TM = ("z", "yl", "core")
CHIPS = ("z", "yl")
SHARE = 6
SPAN = 16
F32, BF16 = jnp.float32, jnp.bfloat16


def swap(value):
    return lax.ppermute(value, CA, [(0, 1), (1, 0)])


def pick(low, high):
    return jnp.where(lax.axis_index(CA) == 0, low, high)


def exchange(value, axis):
    return lax.all_to_all(value, axis, split_axis=0, concat_axis=0, tiled=True)


def gather(value, axis, count):
    rows, width = value.shape
    copies = jnp.broadcast_to(value[None], (count, rows, width))
    return exchange(copies, axis).reshape(count * rows, width)


def scatter(value, axis, count):
    rows, width = value.shape
    arrived = exchange(value.reshape(count, rows // count, width), axis)
    return jnp.sum(arrived.astype(F32), axis=0)


def shift(value, axis, count, by):
    return lax.ppermute(value, axis, [(i, (i + by) % count) for i in range(count)])


def gather_ring(value, axis, count):
    return jnp.concatenate([value] + [shift(value, axis, count, k) for k in range(1, count)], axis=0)


def ring_chunks(value, axis, count):
    rows = value.shape[0] // count
    return [value[:rows]] + [
        shift(value[k * rows : (k + 1) * rows], axis, count, -k) for k in range(1, count)
    ]


def gather_four(value, axis):
    cut = value.shape[0] // 16 * 8
    back, ahead = shift(value, axis, 4, 1), shift(value, axis, 4, -1)
    far = [shift(back[:cut], axis, 4, 1), shift(ahead[cut:], axis, 4, -1)]
    return [value, back, jnp.concatenate(far, axis=0), ahead]


def scatter_four(own, back, far, ahead, axis):
    cut = own.shape[0] // 16 * 8
    first = shift(jnp.concatenate([far[:cut], back[cut:]], axis=0), axis, 4, -1)
    second = shift(jnp.concatenate([ahead[:cut], far[cut:]], axis=0), axis, 4, 1)
    first_more = shift(add_up([back[:cut], first[:cut]]), axis, 4, -1)
    second_more = shift(add_up([ahead[cut:], second[cut:]]), axis, 4, 1)
    upper = add_up([own[:cut], second[:cut], first_more])
    lower = add_up([own[cut:], first[cut:], second_more])
    return jnp.concatenate([upper, lower], axis=0)


def add_up(chunks):
    total = chunks[0].astype(F32)
    for chunk in chunks[1:]:
        total = total + chunk.astype(F32)
    return total.astype(BF16)


def tie(*values):
    return lax.optimization_barrier(values)


def normalize(values):
    center = jnp.mean(values, axis=-1, keepdims=True)
    shifted = values - center
    spread = jnp.mean(shifted * shifted, axis=-1, keepdims=True)
    inverse_scale = lax.rsqrt(spread + EPSILON)
    return (shifted * inverse_scale, inverse_scale)


def depthwise(padded, kernel, length):
    running = jnp.zeros((length, padded.shape[1]), F32)
    for offset in range(kernel.shape[0]):
        running = running + kernel[offset] * padded[offset : offset + length].astype(F32)
    return running


def kernel_terms(grad_mixed, padded, length, taps):
    grad_float = grad_mixed.astype(F32)
    return jnp.stack(
        [
            jnp.sum(grad_float * padded[offset : offset + length].astype(F32), axis=0)
            for offset in range(taps)
        ]
    )


def marked(values, marks):
    row = jnp.pad(marks.astype(values.dtype), (0, values.shape[1] - marks.shape[0]))[None]
    return jnp.concatenate([values, row], axis=0)


def both_cores(own, other):
    return pick(jnp.concatenate([own, other], axis=0), jnp.concatenate([other, own], axis=0))


def from_neighbours(head, tail):
    count = Z * YL
    before = lax.ppermute(tail, CHIPS, [(i, i + 1) for i in range(count - 1)])
    after_ = lax.ppermute(head, CHIPS, [(i + 1, i) for i in range(count - 1)])
    return before, after_


def from_edges(near, far):
    ends = range(Z * YL - 1)
    ahead = [(2 * i + 1, 2 * i + 2) for i in ends] + [(2 * i + 2, 2 * i + 1) for i in ends]
    along = [(2 * i + 1, 2 * i + 3) for i in ends] + [(2 * i + 2, 2 * i) for i in ends]
    return lax.ppermute(near, TM, ahead), lax.ppermute(far, TM, along)


def feature_order(x_first):
    row = jnp.arange(X * Y * Z * CORE * SHARE, dtype=jnp.int32)
    within = row % (CORE * SHARE)
    zs = row // (CORE * SHARE) % Z
    second = row // (CORE * SHARE * Z) % 4
    first = row // (CORE * SHARE * Z * 4) % 4
    xs, ky = ((lax.axis_index(XA) - first) % X, second) if x_first else (second, first)
    ys = (lax.axis_index(YA) - ky) % Y
    device = (((xs * YH + ys // YL) * Z + zs) * YL + ys % YL) * CORE
    return device * SHARE + within


def own_columns(value):
    rows, width = value.shape
    parts = value.reshape(rows, 2, CORE, width // 4)
    low = parts[:, :, 0].reshape(rows, width // 2)
    high = parts[:, :, 1].reshape(rows, width // 2)
    return pick(low, high), pick(high, low)


def gather_weight(column, target, beside):
    rows, width = column.shape[0], column.shape[1] // 2
    slots = target.shape[1]

    def numbers(values):
        return jnp.pad(values.astype(BF16), ((0, 7), (0, width - values.shape[1])))

    lin = gather_ring(column[:, :width], YA, Y)
    gate = jnp.concatenate([column[:, width:], numbers(target)], axis=0)
    gate = gather(gate, XA, X).reshape(X, rows + 8, width)
    gate, beside = tie(gate, beside)
    here = gate[:, rows, :slots]
    gate = gate[:, :rows].reshape(X * rows, width)
    gate = jnp.concatenate([gate, numbers(here.reshape(1, X * slots))], axis=0)
    chunks = gather_four(gate, YA)
    there = chunks[Y // YH][X * rows, : X * slots].reshape(X, slots)
    first = lax.axis_index("yh") == 0
    targets = jnp.stack([jnp.where(first, here, there), jnp.where(first, there, here)], axis=1)
    gate = jnp.concatenate([chunk[: X * rows] for chunk in chunks], axis=0)
    lin = jnp.concatenate(gather_four(lin, XA), axis=0)
    return lin, gate, targets.reshape(X * YH, slots).astype(jnp.int32), beside


def in_turn(pieces, at):
    count = len(pieces)
    ring = jnp.stack([pieces[(-j) % count] for j in range(2 * count - 1)])
    turned = lax.dynamic_slice_in_dim(ring, (-at) % count, count, axis=0)
    return turned.reshape(count * pieces[0].shape[0], pieces[0].shape[1])


def scatter_rest(lin, gate, part, beside):
    rows, width = lin.shape[0] // Y, lin.shape[1]
    taps = part.shape[0]
    stacked = jnp.concatenate(
        [piece for k in range(Y) for piece in (lin[k * rows : (k + 1) * rows], part)], axis=0
    )
    lin = add_up(ring_chunks(stacked, YA, Y))
    part = lin[rows:].reshape(taps // 2, 2 * width)
    gate = scatter(gate, XA, X).astype(BF16)
    pair = jnp.concatenate([lin[:rows], gate], axis=1).reshape(Z, rows // Z, 2 * width)
    full = jnp.concatenate([pair, jnp.broadcast_to(part[None], (Z,) + part.shape)], axis=1)
    arrived, beside = tie(exchange(full, ZA), beside)
    total = jnp.sum(arrived.astype(F32), axis=0)
    low, high, part = total[:SHARE], total[SHARE : 2 * SHARE], total[2 * SHARE :]
    mine = pick(low, high)
    there = swap(jnp.concatenate([pick(high, low), part], axis=0))
    other = there[:SHARE]
    first, second = pick(mine, other), pick(other, mine)
    weight_grad = jnp.concatenate(
        [first[:, :width], second[:, :width], first[:, width:], second[:, width:]], axis=1
    )
    part, other = part.reshape(taps, width), there[SHARE:].reshape(taps, width)
    part = jnp.concatenate([pick(part, other), pick(other, part)], axis=1)
    parts = [part] + [shift(part, XA, X, k) for k in range(1, X)]
    return weight_grad, in_turn(parts, lax.axis_index(XA)), beside


def back_kernel(pre_lin, pre_gate, lin, gate, order_lin, order_gate, out):
    @pl.when(pl.program_id(0) == 0)
    def _():
        out[...] = jnp.zeros_like(out)

    across = (((1,), (1,)), ((), ()))
    total = out[...]
    for pre, weight, order in ((pre_lin, lin, order_lin), (pre_gate, gate, order_gate)):
        value = lax.dot_general(pre[...], weight[...], across, preferred_element_type=F32)
        feature = lax.broadcasted_iota(jnp.int32, (order.shape[0], out.shape[1]), 1)
        place = jnp.where(feature == order[...], 1.0, 0.0).astype(BF16)
        total = total + jnp.dot(value.astype(BF16), place, preferred_element_type=F32)
    out[...] = total


def back_product(pre_lin, pre_gate, lin, gate, order_lin, order_gate):
    rows, half = pre_lin.shape
    width, block = lin.shape[0], 384
    whole = pl.BlockSpec((rows, half), lambda i: (0, 0))
    part = pl.BlockSpec((block, half), lambda i: (i, 0))
    order = pl.BlockSpec((block, 1), lambda i: (i, 0))
    return pl.pallas_call(
        back_kernel,
        grid=(width // block,),
        in_specs=[whole, whole, part, part, order, order],
        out_specs=pl.BlockSpec((rows, width), lambda i: (0, 0)),
        out_shape=jax.ShapeDtypeStruct((rows, width), F32),
        compiler_params=pltpu.CompilerParams(vmem_limit_bytes=32 * 1024 * 1024),
        cost_estimate=pl.CostEstimate(
            flops=4 * rows * width * (half + width), bytes_accessed=8 * rows * width, transcendentals=0
        ),
        name="back_product",
    )(pre_lin, pre_gate, lin, gate, order_lin[:, None], order_gate[:, None])


def shards(frames, live_mask, stretch_target, pw_weight, kernel, out_grad):
    groups = X * YH
    own_group = lax.axis_index(DP)
    slot_count = stretch_target.shape[1]
    width = frames.shape[2]
    stretch_len = frames.shape[1] // slot_count
    capacity = out_grad.shape[1] // stretch_len
    per_peer = slot_count // 4
    entries = groups * per_peer
    taps = kernel.shape[0]
    length = slot_count * stretch_len
    rows_here = capacity * stretch_len
    half = width // CORE
    loss_scale = float(groups * Z * YL * CORE * rows_here) ** (-0.5)
    capacity_index = jnp.arange(capacity, dtype=jnp.int32)
    entry_ids = jnp.arange(entries, dtype=jnp.int32)
    slot_index = jnp.arange(slot_count, dtype=jnp.int32)
    earlier = slot_index[:, None] > slot_index[None, :]

    columns, others = own_columns(pw_weight)
    pair = both_cores(columns, swap(others))
    column = gather(pair, ZA, Z)

    window = CORE * length
    outer = 2 * SPAN
    normed, inverse_scale = normalize(frames[0].astype(F32))
    packet = marked(normed.astype(BF16), live_mask[0])
    packet_other = swap(packet)
    rows_win = both_cores(packet[:length], packet_other[:length])
    live_win = both_cores(packet[length, :length], packet_other[length, :length])
    before, behind = from_neighbours(
        marked(rows_win[:outer], live_win[:outer]),
        marked(rows_win[window - outer :], live_win[window - outer :]),
    )
    rows_ext = jnp.concatenate([before[:outer], rows_win, behind[:outer]], axis=0)
    live_ext = jnp.concatenate([before[outer, :outer], live_win, behind[outer, :outer]]).astype(F32)
    live_ext = live_ext[:, None]

    column, rows_ext = tie(column, rows_ext)
    weight_lin, weight_gate, all_targets, rows_ext = gather_weight(column, stretch_target, rows_ext)

    feature = jnp.arange(width, dtype=jnp.int32)
    order_lin, order_gate = feature_order(True), feature_order(False)
    to_lin = (feature[:, None] == order_lin[None, :]).astype(BF16)
    to_gate = (feature[:, None] == order_gate[None, :]).astype(BF16)
    normed_lin = jnp.dot(rows_ext, to_lin, preferred_element_type=F32).astype(BF16)
    normed_gate = jnp.dot(rows_ext, to_gate, preferred_element_type=F32).astype(BF16)


    def entries_of(target, group):
        dest = jnp.where(target >= 0, target // capacity, -1)
        away = (target >= 0) & (dest != group)
        alike = (dest[:, None] == dest[None, :]) & away[None, :] & earlier
        rank = jnp.sum(alike.astype(jnp.int32), axis=1)
        return jnp.where(away, dest * per_peer + rank, -1)

    target = stretch_target[0]
    named_slot = target >= 0
    local = named_slot & (target // capacity == own_group)
    selector = (entries_of(target, own_group)[None, :] == entry_ids[:, None]).astype(BF16)
    local_pick = ((target % capacity)[None, :] == capacity_index[:, None]) & local[None, :]
    local_pick = local_pick.astype(BF16)

    group_ids = jnp.arange(groups, dtype=jnp.int32)
    arriving = jax.vmap(entries_of)(all_targets, group_ids)
    wanted = own_group * per_peer + jnp.arange(per_peer, dtype=jnp.int32)
    carried = arriving[:, None, :] == wanted[None, :, None]
    codes_home = (
        jnp.sum(jnp.where(carried, (all_targets % capacity + 1)[:, None, :], 0), axis=2) - 1
    ).reshape(entries)

    def send_home(values):
        pieces = values.reshape(slot_count, stretch_len, width)
        outgoing = jnp.einsum(
            "es,sfw->efw", selector, pieces, preferred_element_type=F32
        ).astype(BF16)
        arrived = exchange(outgoing, DP)
        placing = (codes_home[None, :] == capacity_index[:, None]).astype(BF16)
        placed = jnp.einsum("ce,efw->cfw", placing, arrived, preferred_element_type=F32)
        placed = placed + jnp.einsum("cs,sfw->cfw", local_pick, pieces, preferred_element_type=F32)
        return placed.astype(BF16).reshape(rows_here, width)

    def send_back(values, mark):
        pieces = values.reshape(capacity, stretch_len, width)
        picking = (codes_home[:, None] == capacity_index[None, :]).astype(BF16)
        outgoing = jnp.einsum("ec,cfw->efw", picking, pieces, preferred_element_type=F32).astype(BF16)
        arrived, mark = tie(exchange(outgoing, DP), mark)
        placed = jnp.einsum("es,efw->sfw", selector, arrived, preferred_element_type=F32)
        placed = placed + jnp.einsum("cs,cfw->sfw", local_pick, pieces, preferred_element_type=F32)
        return placed.astype(BF16).reshape(length, width), mark

    cotangent, weight_lin, weight_gate, normed_lin, normed_gate = tie(
        out_grad[0], weight_lin, weight_gate, normed_lin, normed_gate
    )
    linear = jnp.dot(normed_lin, weight_lin, preferred_element_type=F32)
    gate = jax.nn.sigmoid(jnp.dot(normed_gate, weight_gate, preferred_element_type=F32))
    unit_ext = jnp.where(live_ext > 0, linear * gate, 0.0).astype(BF16)

    core = lax.axis_index(CA)
    taps_own = lax.dynamic_slice_in_dim(kernel, core * half, half, axis=1)
    inner = window + 2 * SPAN
    live_inner = live_ext[SPAN : SPAN + inner]
    live_own = live_ext[outer : outer + window]
    mixed_time = live_inner * depthwise(unit_ext[1:], taps_own, inner)
    grad_time, mixed_time = send_back(cotangent, mixed_time)
    mine = pick(grad_time[:, :half], grad_time[:, half:])
    others = pick(grad_time[:, half:], grad_time[:, :half])
    grad_win = both_cores(mine, swap(others))
    near, far = from_edges(
        pick(others[:SPAN], others[length - SPAN :]), pick(mine[:SPAN], mine[length - SPAN :])
    )
    grad_ext = jnp.concatenate([pick(near, far), grad_win, pick(far, near)], axis=0).astype(F32)

    mean_own = jnp.mean(mixed_time, axis=-1)
    rest_own = mixed_time - mean_own[:, None]
    square_own = jnp.sum(rest_own * rest_own, axis=-1)
    mean_there, square_there = swap(jnp.stack([mean_own, square_own]))
    apart = 0.5 * (mean_there - mean_own)
    spread = (square_own + square_there) / width + apart * apart
    norm_scale = lax.rsqrt(spread + EPSILON)[:, None]
    norm_time = (rest_own - apart[:, None]) * norm_scale
    sigma = jax.nn.sigmoid(norm_time)
    inner_rows = slice(SPAN, SPAN + window)
    silu = (norm_time * sigma)[inner_rows].astype(BF16)
    silu_low, silu_high = silu[:length], silu[length:]
    silu_there = swap(pick(silu_high, silu_low))
    silu_here = pick(silu_low, silu_high)
    silu_own = jnp.concatenate([pick(silu_here, silu_there), pick(silu_there, silu_here)], axis=1)
    output_time = (frames[0].astype(F32) + silu_own.astype(F32)).astype(BF16)

    grad_norm = grad_ext * sigma * (1.0 + norm_time * (1.0 - sigma))
    sums = jnp.stack([jnp.sum(grad_norm, axis=-1), jnp.sum(grad_norm * norm_time, axis=-1)])
    means = (sums + swap(sums)) / width
    grad_mixed = (
        live_inner * norm_scale * (grad_norm - means[0][:, None] - norm_time * means[1][:, None])
    ).astype(BF16)
    grad_mixed, output_time = tie(grad_mixed, output_time)
    mixed_rows = send_home(output_time)
    grad_unit = (live_own * depthwise(grad_mixed[1:], taps_own[::-1], window)).astype(BF16)
    terms = kernel_terms(grad_mixed[inner_rows], unit_ext[SPAN + 1 :], window, taps)

    outer_rows = slice(outer, outer + window)
    grad_float = grad_unit.astype(F32)
    gate_own = gate[outer_rows]
    pre_lin = (grad_float * gate_own).astype(BF16)
    pre_gate = (grad_float * linear[outer_rows] * gate_own * (1.0 - gate_own)).astype(BF16)

    def term(left, right):
        value = lax.dot_general(
            left[outer_rows], right, (((0,), (0,)), ((), ())), preferred_element_type=F32
        )
        return (loss_scale * value).astype(BF16)

    term_lin, term_gate = term(normed_lin, pre_lin), term(normed_gate, pre_gate)
    terms = (loss_scale * jnp.pad(terms, ((0, 1), (0, 0)))).astype(BF16)
    term_lin, term_gate, mixed_rows = tie(term_lin, term_gate, mixed_rows)
    term_lin, term_gate, pre_lin, pre_gate = tie(term_lin, term_gate, pre_lin, pre_gate)
    rows, quarters = width // X, terms.reshape(X, terms.shape[0] // X, half)
    at = lax.axis_index(XA)

    def with_taps(k):
        part = lax.dynamic_index_in_dim(quarters, (at - k) % X, 0, keepdims=False)
        return jnp.concatenate([term_lin[k * rows : (k + 1) * rows], part], axis=0)

    gate_sum = scatter_four(*[term_gate[k * rows : (k + 1) * rows] for k in range(Y)], YA)
    lin = scatter_four(*[with_taps(k) for k in range(X)], XA)
    partial_grad = back_product(pre_lin, pre_gate, weight_lin, weight_gate, order_lin, order_gate)
    lin, gate_sum, partial_grad = tie(lin, gate_sum, partial_grad)
    low, high = partial_grad[:length], partial_grad[length:]
    grad_normed = pick(low, high) + swap(pick(high, low).astype(BF16)).astype(F32)
    branch = inverse_scale * (
        grad_normed
        - jnp.mean(grad_normed, axis=-1, keepdims=True)
        - normed * jnp.mean(grad_normed * normed, axis=-1, keepdims=True)
    )
    named_rows = jnp.repeat(named_slot, stretch_len)[:, None]
    frame_grad = jnp.where(named_rows, grad_time.astype(F32) + branch, 0.0).astype(BF16)
    weight_grad, kernel_grad, frame_grad = scatter_rest(lin[:rows], gate_sum, lin[rows:], frame_grad)
    kernel_grad = kernel_grad[:taps]
    return (mixed_rows[None], frame_grad[None], weight_grad, kernel_grad)


def solution(mesh):
    fine = Mesh(mesh.devices.reshape(X, YH, Z, YL, CORE), ("x", "yh", "z", "yl", "core"))
    every = DP + TM
    placed = (
        P(DP, TM, None),
        P(DP, TM),
        P(DP, TM),
        P(every, None),
        P(),
        P(DP, TM, None),
    )
    return jax.shard_map(
        shards,
        mesh=fine,
        in_specs=placed,
        out_specs=(P(DP, TM, None), P(DP, TM, None), P(every, None), P()),
        check_vma=False,
    )
```

```python
import jax
import jax.numpy as jnp
from jax import lax
from jax.experimental import pallas as pl
from jax.experimental.pallas import tpu as pltpu
from jax.sharding import Mesh
from jax.sharding import PartitionSpec as P

EPSILON = 1e-05
X, YH, Z, YL, CORE = 4, 2, 8, 2, 2
Y = YH * YL
XA, YA, ZA, CA = "x", ("yh", "yl"), "z", "core"
DP = ("x", "yh")
TM = ("z", "yl", "core")
CHIPS = ("z", "yl")
SHARE = 6
SPAN = 16
F32, BF16 = jnp.float32, jnp.bfloat16


def swap(value):
    return lax.ppermute(value, CA, [(0, 1), (1, 0)])


def pick(low, high):
    return jnp.where(lax.axis_index(CA) == 0, low, high)


def exchange(value, axis):
    return lax.all_to_all(value, axis, split_axis=0, concat_axis=0, tiled=True)


def gather(value, axis, count):
    rows, width = value.shape
    copies = jnp.broadcast_to(value[None], (count, rows, width))
    return exchange(copies, axis).reshape(count * rows, width)


def scatter(value, axis, count):
    rows, width = value.shape
    arrived = exchange(value.reshape(count, rows // count, width), axis)
    return jnp.sum(arrived.astype(F32), axis=0)


def shift(value, axis, count, by):
    return lax.ppermute(value, axis, [(i, (i + by) % count) for i in range(count)])


def gather_ring(value, axis, count):
    return jnp.concatenate([value] + [shift(value, axis, count, k) for k in range(1, count)], axis=0)


def ring_chunks(value, axis, count):
    rows = value.shape[0] // count
    return [value[:rows]] + [
        shift(value[k * rows : (k + 1) * rows], axis, count, -k) for k in range(1, count)
    ]


def gather_four(value, axis, beside=None):
    cut = value.shape[0] // 16 * 8
    back, ahead = shift(value, axis, 4, 1), shift(value, axis, 4, -1)
    if beside is not None:
        back, ahead, beside = tie(back, ahead, beside)
    far = [shift(back[:cut], axis, 4, 1), shift(ahead[cut:], axis, 4, -1)]
    return jnp.concatenate([value, back] + far + [ahead], axis=0), beside


def messages(chunks):
    _, back, far, ahead = chunks
    cut = far.shape[0] // 16 * 8
    return (
        jnp.concatenate([far[:cut], back[cut:]], axis=0),
        jnp.concatenate([ahead[:cut], far[cut:]], axis=0),
    )


def scatter_four(chunks, down, up, axis):
    own, back, _, ahead = chunks
    cut = own.shape[0] // 16 * 8
    first, second = shift(down, axis, 4, -1), shift(up, axis, 4, 1)
    first_more = shift(add_up([back[:cut], first[:cut]]), axis, 4, -1)
    second_more = shift(add_up([ahead[cut:], second[cut:]]), axis, 4, 1)
    upper = add_up([own[:cut], second[:cut], first_more])
    lower = add_up([own[cut:], first[cut:], second_more])
    return jnp.concatenate([upper, lower], axis=0)


def add_up(chunks):
    total = chunks[0].astype(F32)
    for chunk in chunks[1:]:
        total = total + chunk.astype(F32)
    return total.astype(BF16)


def tie(*values):
    return lax.optimization_barrier(values)


def normalize(values):
    center = jnp.mean(values, axis=-1, keepdims=True)
    shifted = values - center
    spread = jnp.mean(shifted * shifted, axis=-1, keepdims=True)
    inverse_scale = lax.rsqrt(spread + EPSILON)
    return (shifted * inverse_scale, inverse_scale)


def depthwise(padded, kernel, length):
    running = jnp.zeros((length, padded.shape[1]), F32)
    for offset in range(kernel.shape[0]):
        running = running + kernel[offset] * padded[offset : offset + length].astype(F32)
    return running


def kernel_terms(grad_mixed, padded, length, taps):
    grad_float = grad_mixed.astype(F32)
    return jnp.stack(
        [
            jnp.sum(grad_float * padded[offset : offset + length].astype(F32), axis=0)
            for offset in range(taps)
        ]
    )


def marked(values, marks):
    row = jnp.pad(marks.astype(values.dtype), (0, values.shape[1] - marks.shape[0]))[None]
    return jnp.concatenate([values, row], axis=0)


def both_cores(own, other):
    return pick(jnp.concatenate([own, other], axis=0), jnp.concatenate([other, own], axis=0))


def from_neighbours(head, tail):
    count = Z * YL
    before = lax.ppermute(tail, CHIPS, [(i, i + 1) for i in range(count - 1)])
    after_ = lax.ppermute(head, CHIPS, [(i + 1, i) for i in range(count - 1)])
    return before, after_


def from_edges(near, far):
    ends = range(Z * YL - 1)
    ahead = [(2 * i + 1, 2 * i + 2) for i in ends] + [(2 * i + 2, 2 * i + 1) for i in ends]
    along = [(2 * i + 1, 2 * i + 3) for i in ends] + [(2 * i + 2, 2 * i) for i in ends]
    return lax.ppermute(near, TM, ahead), lax.ppermute(far, TM, along)


def feature_order(x_first):
    row = jnp.arange(X * Y * Z * CORE * SHARE, dtype=jnp.int32)
    within = row % (CORE * SHARE)
    zs = row // (CORE * SHARE) % Z
    second = row // (CORE * SHARE * Z) % 4
    first = row // (CORE * SHARE * Z * 4) % 4
    xs, ky = ((lax.axis_index(XA) - first) % X, second) if x_first else (second, first)
    ys = (lax.axis_index(YA) - ky) % Y
    device = (((xs * YH + ys // YL) * Z + zs) * YL + ys % YL) * CORE
    return device * SHARE + within


def own_columns(value):
    rows, width = value.shape
    parts = value.reshape(rows, 2, CORE, width // 4)
    low = parts[:, :, 0].reshape(rows, width // 2)
    high = parts[:, :, 1].reshape(rows, width // 2)
    return pick(low, high), pick(high, low)


def gather_weight(column, target, partner, beside):
    rows, width = column.shape[0], column.shape[1] // 2
    slots = target.shape[1]
    known = jnp.concatenate([target, partner], axis=1).astype(BF16)
    known = jnp.pad(known, ((0, 7), (0, width - 2 * slots)))
    lin = gather_ring(column[:, :width], YA, Y)
    gate = gather(jnp.concatenate([column[:, width:], known], axis=0), XA, X)
    gate, beside = tie(gate.reshape(X, rows + 8, width), beside)
    here, there = gate[:, rows, :slots], gate[:, rows, slots : 2 * slots]
    first = lax.axis_index("yh") == 0
    targets = jnp.stack([jnp.where(first, here, there), jnp.where(first, there, here)], axis=1)
    targets = targets.reshape(X * YH, slots).astype(jnp.int32)
    return lin, gate[:, :rows].reshape(X * rows, width), targets, beside


def in_turn(pieces, at):
    count = len(pieces)
    ring = jnp.stack([pieces[(-j) % count] for j in range(2 * count - 1)])
    turned = lax.dynamic_slice_in_dim(ring, (-at) % count, count, axis=0)
    return turned.reshape(count * pieces[0].shape[0], pieces[0].shape[1])


def scatter_rest(lin, gate, part, beside):
    rows, width = lin.shape[0] // Y, lin.shape[1]
    taps = part.shape[0]
    stacked = jnp.concatenate(
        [piece for k in range(Y) for piece in (lin[k * rows : (k + 1) * rows], part)], axis=0
    )
    lin = add_up(ring_chunks(stacked, YA, Y))
    part = lin[rows:].reshape(taps // 2, 2 * width)
    gate = scatter(gate, XA, X).astype(BF16)
    pair = jnp.concatenate([lin[:rows], gate], axis=1).reshape(Z, rows // Z, 2 * width)
    full = jnp.concatenate([pair, jnp.broadcast_to(part[None], (Z,) + part.shape)], axis=1)
    arrived, beside = tie(exchange(full, ZA), beside)
    total = jnp.sum(arrived.astype(F32), axis=0)
    low, high, part = total[:SHARE], total[SHARE : 2 * SHARE], total[2 * SHARE :]
    mine = pick(low, high)
    there = swap(jnp.concatenate([pick(high, low), part], axis=0))
    other = there[:SHARE]
    first, second = pick(mine, other), pick(other, mine)
    weight_grad = jnp.concatenate(
        [first[:, :width], second[:, :width], first[:, width:], second[:, width:]], axis=1
    )
    part, other = part.reshape(taps, width), there[SHARE:].reshape(taps, width)
    part = jnp.concatenate([pick(part, other), pick(other, part)], axis=1)
    parts = [part] + [shift(part, XA, X, k) for k in range(1, X)]
    return weight_grad, in_turn(parts, lax.axis_index(XA)), beside


def back_kernel(pre_lin, pre_gate, lin, gate, order_lin, order_gate, out):
    @pl.when(pl.program_id(0) == 0)
    def _():
        out[...] = jnp.zeros_like(out)

    across = (((1,), (1,)), ((), ()))
    total = out[...]
    for pre, weight, order in ((pre_lin, lin, order_lin), (pre_gate, gate, order_gate)):
        value = lax.dot_general(pre[...], weight[...], across, preferred_element_type=F32)
        feature = lax.broadcasted_iota(jnp.int32, (out.shape[1], order.shape[1]), 0)
        place = jnp.where(feature == order[...], 1.0, 0.0).astype(BF16)
        total = total + lax.dot_general(
            value.astype(BF16), place, across, preferred_element_type=F32
        )
    out[...] = total


def back_product(pre_lin, pre_gate, lin, gate, order_lin, order_gate):
    rows, half = pre_lin.shape
    width, block = lin.shape[0], 384
    whole = pl.BlockSpec((rows, half), lambda i: (0, 0))
    part = pl.BlockSpec((block, half), lambda i: (i, 0))
    order = pl.BlockSpec((1, block), lambda i: (0, i))
    return pl.pallas_call(
        back_kernel,
        grid=(width // block,),
        in_specs=[whole, whole, part, part, order, order],
        out_specs=pl.BlockSpec((rows, width), lambda i: (0, 0)),
        out_shape=jax.ShapeDtypeStruct((rows, width), F32),
        compiler_params=pltpu.CompilerParams(vmem_limit_bytes=32 * 1024 * 1024),
        cost_estimate=pl.CostEstimate(
            flops=4 * rows * width * (half + width), bytes_accessed=8 * rows * width, transcendentals=0
        ),
        name="back_product",
    )(pre_lin, pre_gate, lin, gate, order_lin[None], order_gate[None])


def shards(frames, live_mask, stretch_target, pw_weight, kernel, out_grad):
    groups = X * YH
    own_group = lax.axis_index(DP)
    slot_count = stretch_target.shape[1]
    width = frames.shape[2]
    stretch_len = frames.shape[1] // slot_count
    capacity = out_grad.shape[1] // stretch_len
    per_peer = slot_count // 4
    entries = groups * per_peer
    taps = kernel.shape[0]
    length = slot_count * stretch_len
    rows_here = capacity * stretch_len
    half = width // CORE
    loss_scale = float(groups * Z * YL * CORE * rows_here) ** (-0.5)
    capacity_index = jnp.arange(capacity, dtype=jnp.int32)
    entry_ids = jnp.arange(entries, dtype=jnp.int32)
    slot_index = jnp.arange(slot_count, dtype=jnp.int32)
    earlier = slot_index[:, None] > slot_index[None, :]

    columns, others = own_columns(pw_weight)
    pair = both_cores(columns, swap(others))
    partner = lax.ppermute(stretch_target, "yh", [(0, 1), (1, 0)])
    column = gather(pair, ZA, Z)

    window = CORE * length
    outer = 2 * SPAN
    normed, inverse_scale = normalize(frames[0].astype(F32))
    packet = marked(normed.astype(BF16), live_mask[0])
    packet_other = swap(packet)
    rows_win = both_cores(packet[:length], packet_other[:length])
    live_win = both_cores(packet[length, :length], packet_other[length, :length])
    before, behind = from_neighbours(
        marked(rows_win[:outer], live_win[:outer]),
        marked(rows_win[window - outer :], live_win[window - outer :]),
    )
    rows_ext = jnp.concatenate([before[:outer], rows_win, behind[:outer]], axis=0)
    live_ext = jnp.concatenate([before[outer, :outer], live_win, behind[outer, :outer]]).astype(F32)
    live_ext = live_ext[:, None]

    column, rows_ext, kernel, partner = tie(column, rows_ext, kernel, partner)
    lin, gate, all_targets, rows_ext = gather_weight(column, stretch_target, partner, rows_ext)

    feature = jnp.arange(width, dtype=jnp.int32)
    order_lin, order_gate = feature_order(True), feature_order(False)
    to_lin = (feature[:, None] == order_lin[None, :]).astype(BF16)
    to_gate = (feature[:, None] == order_gate[None, :]).astype(BF16)
    normed_lin = jnp.dot(rows_ext, to_lin, preferred_element_type=F32).astype(BF16)
    normed_gate = jnp.dot(rows_ext, to_gate, preferred_element_type=F32).astype(BF16)


    def entries_of(target, group):
        dest = jnp.where(target >= 0, target // capacity, -1)
        away = (target >= 0) & (dest != group)
        alike = (dest[:, None] == dest[None, :]) & away[None, :] & earlier
        rank = jnp.sum(alike.astype(jnp.int32), axis=1)
        return jnp.where(away, dest * per_peer + rank, -1)

    target = stretch_target[0]
    named_slot = target >= 0
    local = named_slot & (target // capacity == own_group)
    selector = (entries_of(target, own_group)[None, :] == entry_ids[:, None]).astype(BF16)
    local_pick = ((target % capacity)[None, :] == capacity_index[:, None]) & local[None, :]
    local_pick = local_pick.astype(BF16)

    group_ids = jnp.arange(groups, dtype=jnp.int32)
    arriving = jax.vmap(entries_of)(all_targets, group_ids)
    wanted = own_group * per_peer + jnp.arange(per_peer, dtype=jnp.int32)
    carried = arriving[:, None, :] == wanted[None, :, None]
    codes_home = (
        jnp.sum(jnp.where(carried, (all_targets % capacity + 1)[:, None, :], 0), axis=2) - 1
    ).reshape(entries)

    def leaving(values):
        pieces = values.reshape(slot_count, stretch_len, width)
        return jnp.einsum("es,sfw->efw", selector, pieces, preferred_element_type=F32).astype(BF16)

    def place_home(values, arrived):
        pieces = values.reshape(slot_count, stretch_len, width)
        placing = (codes_home[None, :] == capacity_index[:, None]).astype(BF16)
        placed = jnp.einsum("ce,efw->cfw", placing, arrived, preferred_element_type=F32)
        placed = placed + jnp.einsum("cs,sfw->cfw", local_pick, pieces, preferred_element_type=F32)
        return placed.astype(BF16).reshape(rows_here, width)

    def returning(values):
        pieces = values.reshape(capacity, stretch_len, width)
        picking = (codes_home[:, None] == capacity_index[None, :]).astype(BF16)
        return jnp.einsum("ec,cfw->efw", picking, pieces, preferred_element_type=F32).astype(BF16)

    def place_back(values, arrived):
        pieces = values.reshape(capacity, stretch_len, width)
        placed = jnp.einsum("es,efw->sfw", selector, arrived, preferred_element_type=F32)
        placed = placed + jnp.einsum("cs,cfw->sfw", local_pick, pieces, preferred_element_type=F32)
        return placed.astype(BF16).reshape(length, width)

    weight_lin, lin_mark = gather_four(lin, XA, returning(out_grad[0]))
    weight_gate, outgoing = gather_four(gate, YA, lin_mark)
    grad_arrived = exchange(outgoing, DP)

    linear = jnp.dot(normed_lin, weight_lin, preferred_element_type=F32)
    gate = jax.nn.sigmoid(jnp.dot(normed_gate, weight_gate, preferred_element_type=F32))
    unit_ext = jnp.where(live_ext > 0, linear * gate, 0.0).astype(BF16)

    core = lax.axis_index(CA)
    taps_own = lax.dynamic_slice_in_dim(kernel, core * half, half, axis=1)
    inner = window + 2 * SPAN
    live_inner = live_ext[SPAN : SPAN + inner]
    live_own = live_ext[outer : outer + window]
    mixed_time = live_inner * depthwise(unit_ext[1:], taps_own, inner)
    grad_arrived, mixed_time = tie(grad_arrived, mixed_time)
    grad_time = place_back(out_grad[0], grad_arrived)
    mine = pick(grad_time[:, :half], grad_time[:, half:])
    others = pick(grad_time[:, half:], grad_time[:, :half])
    grad_win = both_cores(mine, swap(others))
    near, far = from_edges(
        pick(others[:SPAN], others[length - SPAN :]), pick(mine[:SPAN], mine[length - SPAN :])
    )
    grad_ext = jnp.concatenate([pick(near, far), grad_win, pick(far, near)], axis=0).astype(F32)

    mean_own = jnp.mean(mixed_time, axis=-1)
    rest_own = mixed_time - mean_own[:, None]
    square_own = jnp.sum(rest_own * rest_own, axis=-1)
    mean_there, square_there = swap(jnp.stack([mean_own, square_own]))
    apart = 0.5 * (mean_there - mean_own)
    spread = (square_own + square_there) / width + apart * apart
    norm_scale = lax.rsqrt(spread + EPSILON)[:, None]
    norm_time = (rest_own - apart[:, None]) * norm_scale
    sigma = jax.nn.sigmoid(norm_time)
    inner_rows = slice(SPAN, SPAN + window)
    silu = (norm_time * sigma)[inner_rows].astype(BF16)
    silu_low, silu_high = silu[:length], silu[length:]
    silu_there = swap(pick(silu_high, silu_low))
    silu_here = pick(silu_low, silu_high)
    silu_own = jnp.concatenate([pick(silu_here, silu_there), pick(silu_there, silu_here)], axis=1)
    output_time = (frames[0].astype(F32) + silu_own.astype(F32)).astype(BF16)

    grad_norm = grad_ext * sigma * (1.0 + norm_time * (1.0 - sigma))
    sums = jnp.stack([jnp.sum(grad_norm, axis=-1), jnp.sum(grad_norm * norm_time, axis=-1)])
    means = (sums + swap(sums)) / width
    grad_mixed = (
        live_inner * norm_scale * (grad_norm - means[0][:, None] - norm_time * means[1][:, None])
    ).astype(BF16)
    grad_mixed, outgoing = tie(grad_mixed, leaving(output_time))
    mixed_arrived = exchange(outgoing, DP)
    grad_unit = (live_own * depthwise(grad_mixed[1:], taps_own[::-1], window)).astype(BF16)
    terms = kernel_terms(grad_mixed[inner_rows], unit_ext[SPAN + 1 :], window, taps)

    outer_rows = slice(outer, outer + window)
    grad_float = grad_unit.astype(F32)
    gate_own = gate[outer_rows]
    pre_lin = (grad_float * gate_own).astype(BF16)
    pre_gate = (grad_float * linear[outer_rows] * gate_own * (1.0 - gate_own)).astype(BF16)

    def term(left, right):
        value = lax.dot_general(
            left[outer_rows], right, (((0,), (0,)), ((), ())), preferred_element_type=F32
        )
        return (loss_scale * value).astype(BF16)

    term_lin, term_gate = term(normed_lin, pre_lin), term(normed_gate, pre_gate)
    terms = (loss_scale * jnp.pad(terms, ((0, 1), (0, 0)))).astype(BF16)
    term_lin, term_gate, mixed_arrived, pre_lin, pre_gate = tie(
        term_lin, term_gate, mixed_arrived, pre_lin, pre_gate
    )
    rows, quarters = width // X, terms.reshape(X, terms.shape[0] // X, half)
    at = lax.axis_index(XA)

    def with_taps(k):
        part = lax.dynamic_index_in_dim(quarters, (at - k) % X, 0, keepdims=False)
        return jnp.concatenate([term_lin[k * rows : (k + 1) * rows], part], axis=0)

    gate_chunks = [term_gate[k * rows : (k + 1) * rows] for k in range(Y)]
    lin_chunks = [with_taps(k) for k in range(X)]
    gate_down, gate_up, lin_down, lin_up, pre_lin, pre_gate = tie(
        *messages(gate_chunks), *messages(lin_chunks), pre_lin, pre_gate
    )
    gate_sum = scatter_four(gate_chunks, gate_down, gate_up, YA)
    lin = scatter_four(lin_chunks, lin_down, lin_up, XA)
    partial_grad = back_product(pre_lin, pre_gate, weight_lin, weight_gate, order_lin, order_gate)
    mixed_arrived, partial_grad = tie(mixed_arrived, partial_grad)
    mixed_rows = place_home(output_time, mixed_arrived)
    lin, gate_sum, partial_grad = tie(lin, gate_sum, partial_grad)
    low, high = partial_grad[:length], partial_grad[length:]
    grad_normed = pick(low, high) + swap(pick(high, low).astype(BF16)).astype(F32)
    branch = inverse_scale * (
        grad_normed
        - jnp.mean(grad_normed, axis=-1, keepdims=True)
        - normed * jnp.mean(grad_normed * normed, axis=-1, keepdims=True)
    )
    named_rows = jnp.repeat(named_slot, stretch_len)[:, None]
    frame_grad = jnp.where(named_rows, grad_time.astype(F32) + branch, 0.0).astype(BF16)
    weight_grad, kernel_grad, frame_grad = scatter_rest(lin[:rows], gate_sum, lin[rows:], frame_grad)
    kernel_grad = kernel_grad[:taps]
    return (mixed_rows[None], frame_grad[None], weight_grad, kernel_grad)


def solution(mesh):
    fine = Mesh(mesh.devices.reshape(X, YH, Z, YL, CORE), ("x", "yh", "z", "yl", "core"))
    every = DP + TM
    placed = (
        P(DP, TM, None),
        P(DP, TM),
        P(DP, TM),
        P(every, None),
        P(),
        P(DP, TM, None),
    )
    return jax.shard_map(
        shards,
        mesh=fine,
        in_specs=placed,
        out_specs=(P(DP, TM, None), P(DP, TM, None), P(every, None), P()),
        check_vma=False,
    )
```

```python
import jax
import jax.numpy as jnp
from jax import lax
from jax.experimental import pallas as pl
from jax.experimental.pallas import tpu as pltpu
from jax.sharding import Mesh
from jax.sharding import PartitionSpec as P

EPSILON = 1e-05
X, YH, Z, YL, CORE = 4, 2, 8, 2, 2
Y = YH * YL
XA, YA, ZA, CA = "x", ("yh", "yl"), "z", "core"
DP = ("x", "yh")
TM = ("z", "yl", "core")
CHIPS = ("z", "yl")
SHARE = 6
SPAN = 16
F32, BF16 = jnp.float32, jnp.bfloat16


def swap(value):
    return lax.ppermute(value, CA, [(0, 1), (1, 0)])


def pick(low, high):
    return jnp.where(lax.axis_index(CA) == 0, low, high)


def exchange(value, axis):
    return lax.all_to_all(value, axis, split_axis=0, concat_axis=0, tiled=True)


def gather(value, axis, count):
    rows, width = value.shape
    copies = jnp.broadcast_to(value[None], (count, rows, width))
    return exchange(copies, axis).reshape(count * rows, width)


def scatter(value, axis, count):
    rows, width = value.shape
    arrived = exchange(value.reshape(count, rows // count, width), axis)
    return jnp.sum(arrived.astype(F32), axis=0)


def shift(value, axis, count, by):
    return lax.ppermute(value, axis, [(i, (i + by) % count) for i in range(count)])


def gather_ring(value, axis, count):
    return jnp.concatenate([value] + [shift(value, axis, count, k) for k in range(1, count)], axis=0)


def ring_chunks(value, axis, count):
    rows = value.shape[0] // count
    return [value[:rows]] + [
        shift(value[k * rows : (k + 1) * rows], axis, count, -k) for k in range(1, count)
    ]


def gather_four(value, axis):
    cut = value.shape[0] // 16 * 8
    back, ahead = shift(value, axis, 4, 1), shift(value, axis, 4, -1)
    far = [shift(back[:cut], axis, 4, 1), shift(ahead[cut:], axis, 4, -1)]
    return jnp.concatenate([value, back] + far + [ahead], axis=0)


def messages(chunks):
    _, back, far, ahead = chunks
    cut = far.shape[0] // 16 * 8
    return (
        jnp.concatenate([far[:cut], back[cut:]], axis=0),
        jnp.concatenate([ahead[:cut], far[cut:]], axis=0),
    )


def scatter_four(chunks, down, up, axis):
    own, back, _, ahead = chunks
    cut = own.shape[0] // 16 * 8
    first, second = shift(down, axis, 4, -1), shift(up, axis, 4, 1)
    first_more = shift(add_up([back[:cut], first[:cut]]), axis, 4, -1)
    second_more = shift(add_up([ahead[cut:], second[cut:]]), axis, 4, 1)
    upper = add_up([own[:cut], second[:cut], first_more])
    lower = add_up([own[cut:], first[cut:], second_more])
    return jnp.concatenate([upper, lower], axis=0)


def add_up(chunks):
    total = chunks[0].astype(F32)
    for chunk in chunks[1:]:
        total = total + chunk.astype(F32)
    return total.astype(BF16)


def tie(*values):
    return lax.optimization_barrier(values)


def normalize(values):
    center = jnp.mean(values, axis=-1, keepdims=True)
    shifted = values - center
    spread = jnp.mean(shifted * shifted, axis=-1, keepdims=True)
    inverse_scale = lax.rsqrt(spread + EPSILON)
    return (shifted * inverse_scale, inverse_scale)


def depthwise(padded, kernel, length):
    running = jnp.zeros((length, padded.shape[1]), F32)
    for offset in range(kernel.shape[0]):
        running = running + kernel[offset] * padded[offset : offset + length].astype(F32)
    return running


def kernel_terms(grad_mixed, padded, length, taps):
    grad_float = grad_mixed.astype(F32)
    return jnp.stack(
        [
            jnp.sum(grad_float * padded[offset : offset + length].astype(F32), axis=0)
            for offset in range(taps)
        ]
    )


def marked(values, marks):
    row = jnp.pad(marks.astype(values.dtype), (0, values.shape[1] - marks.shape[0]))[None]
    return jnp.concatenate([values, row], axis=0)


def both_cores(own, other):
    return pick(jnp.concatenate([own, other], axis=0), jnp.concatenate([other, own], axis=0))


def from_neighbours(head, tail):
    count = Z * YL
    before = lax.ppermute(tail, CHIPS, [(i, i + 1) for i in range(count - 1)])
    after_ = lax.ppermute(head, CHIPS, [(i + 1, i) for i in range(count - 1)])
    return before, after_


def from_edges(near, far):
    ends = range(Z * YL - 1)
    ahead = [(2 * i + 1, 2 * i + 2) for i in ends] + [(2 * i + 2, 2 * i + 1) for i in ends]
    along = [(2 * i + 1, 2 * i + 3) for i in ends] + [(2 * i + 2, 2 * i) for i in ends]
    return lax.ppermute(near, TM, ahead), lax.ppermute(far, TM, along)


def feature_order(x_first):
    row = jnp.arange(X * Y * Z * CORE * SHARE, dtype=jnp.int32)
    within = row % (CORE * SHARE)
    zs = row // (CORE * SHARE) % Z
    second = row // (CORE * SHARE * Z) % 4
    first = row // (CORE * SHARE * Z * 4) % 4
    xs, ky = ((lax.axis_index(XA) - first) % X, second) if x_first else (second, first)
    ys = (lax.axis_index(YA) - ky) % Y
    device = (((xs * YH + ys // YL) * Z + zs) * YL + ys % YL) * CORE
    return device * SHARE + within


def own_columns(value):
    rows, width = value.shape
    parts = value.reshape(rows, 2, CORE, width // 4)
    low = parts[:, :, 0].reshape(rows, width // 2)
    high = parts[:, :, 1].reshape(rows, width // 2)
    return pick(low, high), pick(high, low)


def gather_weight(column, target, partner, beside):
    rows, width = column.shape[0], column.shape[1] // 2
    slots = target.shape[1]
    known = jnp.concatenate([target, partner], axis=1).astype(BF16)
    known = jnp.pad(known, ((0, 7), (0, width - 2 * slots)))
    lin = gather_ring(column[:, :width], YA, Y)
    gate = gather(jnp.concatenate([column[:, width:], known], axis=0), XA, X)
    gate, beside = tie(gate.reshape(X, rows + 8, width), beside)
    here, there = gate[:, rows, :slots], gate[:, rows, slots : 2 * slots]
    first = lax.axis_index("yh") == 0
    targets = jnp.stack([jnp.where(first, here, there), jnp.where(first, there, here)], axis=1)
    targets = targets.reshape(X * YH, slots).astype(jnp.int32)
    return lin, gate[:, :rows].reshape(X * rows, width), targets, beside


def in_turn(pieces, at):
    count = len(pieces)
    ring = jnp.stack([pieces[(-j) % count] for j in range(2 * count - 1)])
    turned = lax.dynamic_slice_in_dim(ring, (-at) % count, count, axis=0)
    return turned.reshape(count * pieces[0].shape[0], pieces[0].shape[1])


def scatter_middle(lin, gate, part, beside):
    rows, width = lin.shape[0] // Y, lin.shape[1]
    stacked = jnp.concatenate(
        [piece for k in range(Y) for piece in (lin[k * rows : (k + 1) * rows], part)], axis=0
    )
    lin = add_up(ring_chunks(stacked, YA, Y))
    part = lin[rows:].reshape(part.shape[0] // 2, 2 * width)
    gate = scatter(gate, XA, X).astype(BF16)
    pair = jnp.concatenate([lin[:rows], gate], axis=1).reshape(Z, rows // Z, 2 * width)
    full = jnp.concatenate([pair, jnp.broadcast_to(part[None], (Z,) + part.shape)], axis=1)
    return tie(full, beside)


def scatter_last(arrived, pair_rows):
    share, width = pair_rows // 2, arrived.shape[2] // 2
    taps = 2 * (arrived.shape[1] - pair_rows)
    total = jnp.sum(arrived.astype(F32), axis=0)
    low, high, part = total[:share], total[share:pair_rows], total[pair_rows:]
    mine = pick(low, high)
    there = swap(jnp.concatenate([pick(high, low), part], axis=0))
    other = there[:share]
    first, second = pick(mine, other), pick(other, mine)
    weight_grad = jnp.concatenate(
        [first[:, :width], second[:, :width], first[:, width:], second[:, width:]], axis=1
    )
    part, other = part.reshape(taps, width), there[share:].reshape(taps, width)
    part = jnp.concatenate([pick(part, other), pick(other, part)], axis=1)
    parts = [part] + [shift(part, XA, X, k) for k in range(1, X)]
    return weight_grad, in_turn(parts, lax.axis_index(XA))


def back_kernel(pre_lin, pre_gate, lin, gate, order_lin, order_gate, out):
    @pl.when(pl.program_id(0) == 0)
    def _():
        out[...] = jnp.zeros_like(out)

    across = (((1,), (1,)), ((), ()))
    total = out[...]
    for pre, weight, order in ((pre_lin, lin, order_lin), (pre_gate, gate, order_gate)):
        value = lax.dot_general(pre[...], weight[...], across, preferred_element_type=F32)
        feature = lax.broadcasted_iota(jnp.int32, (out.shape[1], order.shape[1]), 0)
        place = jnp.where(feature == order[...], 1.0, 0.0).astype(BF16)
        total = total + lax.dot_general(
            value.astype(BF16), place, across, preferred_element_type=F32
        )
    out[...] = total


def back_product(pre_lin, pre_gate, lin, gate, order_lin, order_gate):
    rows, half = pre_lin.shape
    width, block = lin.shape[0], 384
    whole = pl.BlockSpec((rows, half), lambda i: (0, 0))
    part = pl.BlockSpec((block, half), lambda i: (i, 0))
    order = pl.BlockSpec((1, block), lambda i: (0, i))
    return pl.pallas_call(
        back_kernel,
        grid=(width // block,),
        in_specs=[whole, whole, part, part, order, order],
        out_specs=pl.BlockSpec((rows, width), lambda i: (0, 0)),
        out_shape=jax.ShapeDtypeStruct((rows, width), F32),
        compiler_params=pltpu.CompilerParams(vmem_limit_bytes=32 * 1024 * 1024),
        cost_estimate=pl.CostEstimate(
            flops=4 * rows * width * (half + width), bytes_accessed=8 * rows * width, transcendentals=0
        ),
        name="back_product",
    )(pre_lin, pre_gate, lin, gate, order_lin[None], order_gate[None])


def shards(frames, live_mask, stretch_target, pw_weight, kernel, out_grad):
    groups = X * YH
    own_group = lax.axis_index(DP)
    slot_count = stretch_target.shape[1]
    width = frames.shape[2]
    stretch_len = frames.shape[1] // slot_count
    capacity = out_grad.shape[1] // stretch_len
    per_peer = slot_count // 4
    entries = groups * per_peer
    taps = kernel.shape[0]
    length = slot_count * stretch_len
    rows_here = capacity * stretch_len
    half = width // CORE
    loss_scale = float(groups * Z * YL * CORE * rows_here) ** (-0.5)
    capacity_index = jnp.arange(capacity, dtype=jnp.int32)
    entry_ids = jnp.arange(entries, dtype=jnp.int32)
    slot_index = jnp.arange(slot_count, dtype=jnp.int32)
    earlier = slot_index[:, None] > slot_index[None, :]

    columns, others = own_columns(pw_weight)
    pair = both_cores(columns, swap(others))
    pair, frames, stretch_target = tie(pair, frames, stretch_target)
    partner = lax.ppermute(stretch_target, "yh", [(0, 1), (1, 0)])
    column = gather(pair, ZA, Z)

    window = CORE * length
    outer = 2 * SPAN
    normed, inverse_scale = normalize(frames[0].astype(F32))
    packet = marked(normed.astype(BF16), live_mask[0])
    packet_other = swap(packet)
    rows_win = both_cores(packet[:length], packet_other[:length])
    live_win = both_cores(packet[length, :length], packet_other[length, :length])
    before, behind = from_neighbours(
        marked(rows_win[:outer], live_win[:outer]),
        marked(rows_win[window - outer :], live_win[window - outer :]),
    )
    rows_ext = jnp.concatenate([before[:outer], rows_win, behind[:outer]], axis=0)
    live_ext = jnp.concatenate([before[outer, :outer], live_win, behind[outer, :outer]]).astype(F32)
    live_ext = live_ext[:, None]

    column, rows_ext, kernel, partner = tie(column, rows_ext, kernel, partner)
    lin, gate, all_targets, rows_ext = gather_weight(column, stretch_target, partner, rows_ext)

    feature = jnp.arange(width, dtype=jnp.int32)
    order_lin, order_gate = feature_order(True), feature_order(False)
    to_lin = (feature[:, None] == order_lin[None, :]).astype(BF16)
    to_gate = (feature[:, None] == order_gate[None, :]).astype(BF16)
    normed_lin = jnp.dot(rows_ext, to_lin, preferred_element_type=F32).astype(BF16)
    normed_gate = jnp.dot(rows_ext, to_gate, preferred_element_type=F32).astype(BF16)


    def entries_of(target, group):
        dest = jnp.where(target >= 0, target // capacity, -1)
        away = (target >= 0) & (dest != group)
        alike = (dest[:, None] == dest[None, :]) & away[None, :] & earlier
        rank = jnp.sum(alike.astype(jnp.int32), axis=1)
        return jnp.where(away, dest * per_peer + rank, -1)

    target = stretch_target[0]
    named_slot = target >= 0
    local = named_slot & (target // capacity == own_group)
    selector = (entries_of(target, own_group)[None, :] == entry_ids[:, None]).astype(BF16)
    local_pick = ((target % capacity)[None, :] == capacity_index[:, None]) & local[None, :]
    local_pick = local_pick.astype(BF16)

    group_ids = jnp.arange(groups, dtype=jnp.int32)
    arriving = jax.vmap(entries_of)(all_targets, group_ids)
    wanted = own_group * per_peer + jnp.arange(per_peer, dtype=jnp.int32)
    carried = arriving[:, None, :] == wanted[None, :, None]
    codes_home = (
        jnp.sum(jnp.where(carried, (all_targets % capacity + 1)[:, None, :], 0), axis=2) - 1
    ).reshape(entries)

    def leaving(values):
        pieces = values.reshape(slot_count, stretch_len, width)
        return jnp.einsum("es,sfw->efw", selector, pieces, preferred_element_type=F32).astype(BF16)

    def place_home(values, arrived):
        pieces = values.reshape(slot_count, stretch_len, width)
        arrived = arrived.reshape((groups - 1) * per_peer, stretch_len, width)
        senders = (own_group - 1 - jnp.arange(groups - 1, dtype=jnp.int32)) % groups
        codes = codes_home.reshape(groups, per_peer)[senders].reshape(-1)
        placing = (codes[None, :] == capacity_index[:, None]).astype(BF16)
        placed = jnp.einsum("ce,efw->cfw", placing, arrived, preferred_element_type=F32)
        placed = placed + jnp.einsum("cs,sfw->cfw", local_pick, pieces, preferred_element_type=F32)
        return placed.astype(BF16).reshape(rows_here, width)

    def returning(values):
        pieces = values.reshape(capacity, stretch_len, width)
        picking = (codes_home[:, None] == capacity_index[None, :]).astype(BF16)
        return jnp.einsum("ec,cfw->efw", picking, pieces, preferred_element_type=F32).astype(BF16)

    def place_back(values, arrived):
        pieces = values.reshape(capacity, stretch_len, width)
        placed = jnp.einsum("es,efw->sfw", selector, arrived, preferred_element_type=F32)
        placed = placed + jnp.einsum("cs,cfw->sfw", local_pick, pieces, preferred_element_type=F32)
        return placed.astype(BF16).reshape(length, width)

    weight_lin, weight_gate = gather_four(lin, XA), gather_four(gate, YA)
    weight_lin, weight_gate, outgoing = tie(weight_lin, weight_gate, returning(out_grad[0]))
    grad_arrived = exchange(outgoing, DP)

    linear = jnp.dot(normed_lin, weight_lin, preferred_element_type=F32)
    gate = jax.nn.sigmoid(jnp.dot(normed_gate, weight_gate, preferred_element_type=F32))
    unit_ext = jnp.where(live_ext > 0, linear * gate, 0.0).astype(BF16)

    core = lax.axis_index(CA)
    taps_own = lax.dynamic_slice_in_dim(kernel, core * half, half, axis=1)
    inner = window + 2 * SPAN
    live_inner = live_ext[SPAN : SPAN + inner]
    live_own = live_ext[outer : outer + window]
    mixed_time = live_inner * depthwise(unit_ext[1:], taps_own, inner)
    grad_arrived, mixed_time = tie(grad_arrived, mixed_time)
    grad_time = place_back(out_grad[0], grad_arrived)
    mine = pick(grad_time[:, :half], grad_time[:, half:])
    others = pick(grad_time[:, half:], grad_time[:, :half])
    grad_win = both_cores(mine, swap(others))
    near, far = from_edges(
        pick(others[:SPAN], others[length - SPAN :]), pick(mine[:SPAN], mine[length - SPAN :])
    )
    grad_ext = jnp.concatenate([pick(near, far), grad_win, pick(far, near)], axis=0).astype(F32)

    mean_own = jnp.mean(mixed_time, axis=-1)
    rest_own = mixed_time - mean_own[:, None]
    square_own = jnp.sum(rest_own * rest_own, axis=-1)
    mean_there, square_there = swap(jnp.stack([mean_own, square_own]))
    apart = 0.5 * (mean_there - mean_own)
    spread = (square_own + square_there) / width + apart * apart
    norm_scale = lax.rsqrt(spread + EPSILON)[:, None]
    norm_time = (rest_own - apart[:, None]) * norm_scale
    sigma = jax.nn.sigmoid(norm_time)
    inner_rows = slice(SPAN, SPAN + window)
    silu = (norm_time * sigma)[inner_rows].astype(BF16)
    silu_low, silu_high = silu[:length], silu[length:]
    silu_there = swap(pick(silu_high, silu_low))
    silu_here = pick(silu_low, silu_high)
    silu_own = jnp.concatenate([pick(silu_here, silu_there), pick(silu_there, silu_here)], axis=1)
    output_time = (frames[0].astype(F32) + silu_own.astype(F32)).astype(BF16)

    grad_norm = grad_ext * sigma * (1.0 + norm_time * (1.0 - sigma))
    sums = jnp.stack([jnp.sum(grad_norm, axis=-1), jnp.sum(grad_norm * norm_time, axis=-1)])
    means = (sums + swap(sums)) / width
    grad_mixed = (
        live_inner * norm_scale * (grad_norm - means[0][:, None] - norm_time * means[1][:, None])
    ).astype(BF16)
    grad_unit = (live_own * depthwise(grad_mixed[1:], taps_own[::-1], window)).astype(BF16)
    terms = kernel_terms(grad_mixed[inner_rows], unit_ext[SPAN + 1 :], window, taps)

    outer_rows = slice(outer, outer + window)
    grad_float = grad_unit.astype(F32)
    gate_own = gate[outer_rows]
    pre_lin = (grad_float * gate_own).astype(BF16)
    pre_gate = (grad_float * linear[outer_rows] * gate_own * (1.0 - gate_own)).astype(BF16)

    def term(left, right):
        value = lax.dot_general(
            left[outer_rows], right, (((0,), (0,)), ((), ())), preferred_element_type=F32
        )
        return (loss_scale * value).astype(BF16)

    term_lin, term_gate = term(normed_lin, pre_lin), term(normed_gate, pre_gate)
    terms = (loss_scale * jnp.pad(terms, ((0, 1), (0, 0)))).astype(BF16)
    rows, quarters = width // X, terms.reshape(X, terms.shape[0] // X, half)
    at = lax.axis_index(XA)

    def with_taps(k):
        part = lax.dynamic_index_in_dim(quarters, (at - k) % X, 0, keepdims=False)
        return jnp.concatenate([term_lin[k * rows : (k + 1) * rows], part], axis=0)

    gate_chunks = [term_gate[k * rows : (k + 1) * rows] for k in range(Y)]
    lin_chunks = [with_taps(k) for k in range(X)]
    gate_down, gate_up, lin_down, lin_up, pre_lin, pre_gate = tie(
        *messages(gate_chunks), *messages(lin_chunks), pre_lin, pre_gate
    )
    gate_sum = scatter_four(gate_chunks, gate_down, gate_up, YA)
    lin = scatter_four(lin_chunks, lin_down, lin_up, XA)
    partial_grad = back_product(pre_lin, pre_gate, weight_lin, weight_gate, order_lin, order_gate)
    leaving_pairs = leaving(output_time).reshape(groups, per_peer * stretch_len, width)
    lin, gate_sum, partial_grad, leaving_pairs = tie(lin, gate_sum, partial_grad, leaving_pairs)
    full, partial_grad = scatter_middle(lin[:rows], gate_sum, lin[rows:], partial_grad)
    low, high = partial_grad[:length], partial_grad[length:]
    grad_there = swap(pick(high, low).astype(BF16))
    grad_there, leaving_pairs = tie(grad_there, leaving_pairs)
    grad_normed = pick(low, high) + grad_there.astype(F32)
    branch = inverse_scale * (
        grad_normed
        - jnp.mean(grad_normed, axis=-1, keepdims=True)
        - normed * jnp.mean(grad_normed * normed, axis=-1, keepdims=True)
    )
    named_rows = jnp.repeat(named_slot, stretch_len)[:, None]
    frame_grad = jnp.where(named_rows, grad_time.astype(F32) + branch, 0.0).astype(BF16)
    mixed_arrived = [
        shift(
            lax.dynamic_index_in_dim(leaving_pairs, (own_group + k) % groups, 0, keepdims=False),
            DP,
            groups,
            k,
        )
        for k in range(1, groups)
    ]
    arrived, frame_grad, *mixed_arrived = tie(exchange(full, ZA), frame_grad, *mixed_arrived)
    mixed_rows = place_home(output_time, jnp.concatenate(mixed_arrived, axis=0))
    weight_grad, kernel_grad = scatter_last(arrived, rows // Y // Z)
    kernel_grad = kernel_grad[:taps]
    return (mixed_rows[None], frame_grad[None], weight_grad, kernel_grad)


def solution(mesh):
    fine = Mesh(mesh.devices.reshape(X, YH, Z, YL, CORE), ("x", "yh", "z", "yl", "core"))
    every = DP + TM
    placed = (
        P(DP, TM, None),
        P(DP, TM),
        P(DP, TM),
        P(every, None),
        P(),
        P(DP, TM, None),
    )
    return jax.shard_map(
        shards,
        mesh=fine,
        in_specs=placed,
        out_specs=(P(DP, TM, None), P(DP, TM, None), P(every, None), P()),
        check_vma=False,
    )
```

```python
import jax
import jax.numpy as jnp
from jax import lax
from jax.experimental import pallas as pl
from jax.experimental.pallas import tpu as pltpu
from jax.sharding import Mesh
from jax.sharding import PartitionSpec as P

EPSILON = 1e-05
X, YH, Z, YL, CORE = 4, 2, 8, 2, 2
Y = YH * YL
XA, YA, ZA, CA = "x", ("yh", "yl"), "z", "core"
DP = ("x", "yh")
TM = ("z", "yl", "core")
CHIPS = ("z", "yl")
SHARE = 6
SPAN = 16
F32, BF16 = jnp.float32, jnp.bfloat16


def swap(value):
    return lax.ppermute(value, CA, [(0, 1), (1, 0)])


def pick(low, high):
    return jnp.where(lax.axis_index(CA) == 0, low, high)


def exchange(value, axis):
    return lax.all_to_all(value, axis, split_axis=0, concat_axis=0, tiled=True)


def gather(value, axis, count):
    rows, width = value.shape
    copies = jnp.broadcast_to(value[None], (count, rows, width))
    return exchange(copies, axis).reshape(count * rows, width)


def scatter(value, axis, count):
    rows, width = value.shape
    arrived = exchange(value.reshape(count, rows // count, width), axis)
    return jnp.sum(arrived.astype(F32), axis=0)


def shift(value, axis, count, by):
    return lax.ppermute(value, axis, [(i, (i + by) % count) for i in range(count)])


def gather_ring(value, axis, count):
    return jnp.concatenate([value] + [shift(value, axis, count, k) for k in range(1, count)], axis=0)


def ring_chunks(value, axis, count):
    rows = value.shape[0] // count
    return [value[:rows]] + [
        shift(value[k * rows : (k + 1) * rows], axis, count, -k) for k in range(1, count)
    ]


def gather_four(value, axis):
    cut = value.shape[0] // 16 * 8
    back, ahead = shift(value, axis, 4, 1), shift(value, axis, 4, -1)
    far = [shift(back[:cut], axis, 4, 1), shift(ahead[cut:], axis, 4, -1)]
    return jnp.concatenate([value, back] + far + [ahead], axis=0)


def messages(chunks):
    _, back, far, ahead = chunks
    cut = far.shape[0] // 16 * 8
    return (
        jnp.concatenate([far[:cut], back[cut:]], axis=0),
        jnp.concatenate([ahead[:cut], far[cut:]], axis=0),
    )


def scatter_four(chunks, down, up, axis):
    own, back, _, ahead = chunks
    cut = own.shape[0] // 16 * 8
    first, second = shift(down, axis, 4, -1), shift(up, axis, 4, 1)
    first_more = shift(add_up([back[:cut], first[:cut]]), axis, 4, -1)
    second_more = shift(add_up([ahead[cut:], second[cut:]]), axis, 4, 1)
    upper = add_up([own[:cut], second[:cut], first_more])
    lower = add_up([own[cut:], first[cut:], second_more])
    return jnp.concatenate([upper, lower], axis=0)


def add_up(chunks):
    total = chunks[0].astype(F32)
    for chunk in chunks[1:]:
        total = total + chunk.astype(F32)
    return total.astype(BF16)


def tie(*values):
    return lax.optimization_barrier(values)


def normalize(values):
    center = jnp.mean(values, axis=-1, keepdims=True)
    shifted = values - center
    spread = jnp.mean(shifted * shifted, axis=-1, keepdims=True)
    inverse_scale = lax.rsqrt(spread + EPSILON)
    return (shifted * inverse_scale, inverse_scale)


def depthwise(padded, kernel, length):
    running = jnp.zeros((length, padded.shape[1]), F32)
    for offset in range(kernel.shape[0]):
        running = running + kernel[offset] * padded[offset : offset + length].astype(F32)
    return running


def kernel_terms(grad_mixed, padded, length, taps):
    grad_float = grad_mixed.astype(F32)
    return jnp.stack(
        [
            jnp.sum(grad_float * padded[offset : offset + length].astype(F32), axis=0)
            for offset in range(taps)
        ]
    )


def marked(values, marks):
    row = jnp.pad(marks.astype(values.dtype), (0, values.shape[1] - marks.shape[0]))[None]
    return jnp.concatenate([values, row], axis=0)


def both_cores(own, other):
    return pick(jnp.concatenate([own, other], axis=0), jnp.concatenate([other, own], axis=0))


def from_neighbours(head, tail):
    count = Z * YL
    before = lax.ppermute(tail, CHIPS, [(i, i + 1) for i in range(count - 1)])
    after_ = lax.ppermute(head, CHIPS, [(i + 1, i) for i in range(count - 1)])
    return before, after_


def from_edges(near, far):
    ends = range(Z * YL - 1)
    ahead = [(2 * i + 1, 2 * i + 2) for i in ends] + [(2 * i + 2, 2 * i + 1) for i in ends]
    along = [(2 * i + 1, 2 * i + 3) for i in ends] + [(2 * i + 2, 2 * i) for i in ends]
    return lax.ppermute(near, TM, ahead), lax.ppermute(far, TM, along)


def feature_order(x_first):
    row = jnp.arange(X * Y * Z * CORE * SHARE, dtype=jnp.int32)
    within = row % (CORE * SHARE)
    zs = row // (CORE * SHARE) % Z
    second = row // (CORE * SHARE * Z) % 4
    first = row // (CORE * SHARE * Z * 4) % 4
    xs, ky = ((lax.axis_index(XA) - first) % X, second) if x_first else (second, first)
    ys = (lax.axis_index(YA) - ky) % Y
    device = (((xs * YH + ys // YL) * Z + zs) * YL + ys % YL) * CORE
    return device * SHARE + within


def own_columns(value):
    rows, width = value.shape
    parts = value.reshape(rows, 2, CORE, width // 4)
    low = parts[:, :, 0].reshape(rows, width // 2)
    high = parts[:, :, 1].reshape(rows, width // 2)
    return pick(low, high), pick(high, low)


def gather_weight(column, target, partner, beside):
    rows, width = column.shape[0], column.shape[1] // 2
    slots = target.shape[1]
    known = jnp.concatenate([target, partner], axis=1).astype(BF16)
    known = jnp.pad(known, ((0, 7), (0, width - 2 * slots)))
    lin = gather_ring(column[:, :width], YA, Y)
    gate = gather(jnp.concatenate([column[:, width:], known], axis=0), XA, X)
    gate, beside = tie(gate.reshape(X, rows + 8, width), beside)
    here, there = gate[:, rows, :slots], gate[:, rows, slots : 2 * slots]
    first = lax.axis_index("yh") == 0
    targets = jnp.stack([jnp.where(first, here, there), jnp.where(first, there, here)], axis=1)
    targets = targets.reshape(X * YH, slots).astype(jnp.int32)
    return lin, gate[:, :rows].reshape(X * rows, width), targets, beside


def in_turn(pieces, at):
    count = len(pieces)
    ring = jnp.stack([pieces[(-j) % count] for j in range(2 * count - 1)])
    turned = lax.dynamic_slice_in_dim(ring, (-at) % count, count, axis=0)
    return turned.reshape(count * pieces[0].shape[0], pieces[0].shape[1])


def scatter_middle(lin, gate, part, beside):
    rows, width = lin.shape[0] // Y, lin.shape[1]
    stacked = jnp.concatenate(
        [piece for k in range(Y) for piece in (lin[k * rows : (k + 1) * rows], part)], axis=0
    )
    lin = add_up(ring_chunks(stacked, YA, Y))
    part = lin[rows:].reshape(part.shape[0] // 2, 2 * width)
    gate = scatter(gate, XA, X).astype(BF16)
    pair = jnp.concatenate([lin[:rows], gate], axis=1).reshape(Z, rows // Z, 2 * width)
    full = jnp.concatenate([pair, jnp.broadcast_to(part[None], (Z,) + part.shape)], axis=1)
    return tie(full, beside)


def scatter_last(arrived, pair_rows):
    share, width = pair_rows // 2, arrived.shape[2] // 2
    taps = 2 * (arrived.shape[1] - pair_rows)
    total = jnp.sum(arrived.astype(F32), axis=0)
    low, high, part = total[:share], total[share:pair_rows], total[pair_rows:]
    mine = pick(low, high)
    there = swap(jnp.concatenate([pick(high, low), part], axis=0))
    other = there[:share]
    first, second = pick(mine, other), pick(other, mine)
    weight_grad = jnp.concatenate(
        [first[:, :width], second[:, :width], first[:, width:], second[:, width:]], axis=1
    )
    part, other = part.reshape(taps, width), there[share:].reshape(taps, width)
    part = jnp.concatenate([pick(part, other), pick(other, part)], axis=1)
    parts = [part] + [shift(part, XA, X, k) for k in range(1, X)]
    return weight_grad, in_turn(parts, lax.axis_index(XA))


def back_kernel(pre_lin, pre_gate, lin, gate, order_lin, order_gate, out):
    @pl.when(pl.program_id(0) == 0)
    def _():
        out[...] = jnp.zeros_like(out)

    across = (((1,), (1,)), ((), ()))
    total = out[...]
    for pre, weight, order in ((pre_lin, lin, order_lin), (pre_gate, gate, order_gate)):
        value = lax.dot_general(pre[...], weight[...], across, preferred_element_type=F32)
        feature = lax.broadcasted_iota(jnp.int32, (out.shape[1], order.shape[1]), 0)
        place = jnp.where(feature == order[...], 1.0, 0.0).astype(BF16)
        total = total + lax.dot_general(
            value.astype(BF16), place, across, preferred_element_type=F32
        )
    out[...] = total


def back_product(pre_lin, pre_gate, lin, gate, order_lin, order_gate):
    rows, half = pre_lin.shape
    width, block = lin.shape[0], 384
    whole = pl.BlockSpec((rows, half), lambda i: (0, 0))
    part = pl.BlockSpec((block, half), lambda i: (i, 0))
    order = pl.BlockSpec((1, block), lambda i: (0, i))
    return pl.pallas_call(
        back_kernel,
        grid=(width // block,),
        in_specs=[whole, whole, part, part, order, order],
        out_specs=pl.BlockSpec((rows, width), lambda i: (0, 0)),
        out_shape=jax.ShapeDtypeStruct((rows, width), F32),
        compiler_params=pltpu.CompilerParams(vmem_limit_bytes=32 * 1024 * 1024),
        cost_estimate=pl.CostEstimate(
            flops=4 * rows * width * (half + width), bytes_accessed=8 * rows * width, transcendentals=0
        ),
        name="back_product",
    )(pre_lin, pre_gate, lin, gate, order_lin[None], order_gate[None])


def shards(frames, live_mask, stretch_target, pw_weight, kernel, out_grad):
    groups = X * YH
    own_group = lax.axis_index(DP)
    slot_count = stretch_target.shape[1]
    width = frames.shape[2]
    stretch_len = frames.shape[1] // slot_count
    capacity = out_grad.shape[1] // stretch_len
    per_peer = slot_count // 4
    entries = groups * per_peer
    taps = kernel.shape[0]
    length = slot_count * stretch_len
    rows_here = capacity * stretch_len
    half = width // CORE
    loss_scale = float(groups * Z * YL * CORE * rows_here) ** (-0.5)
    capacity_index = jnp.arange(capacity, dtype=jnp.int32)
    entry_ids = jnp.arange(entries, dtype=jnp.int32)
    slot_index = jnp.arange(slot_count, dtype=jnp.int32)
    earlier = slot_index[:, None] > slot_index[None, :]

    columns, others = own_columns(pw_weight)
    pair = both_cores(columns, swap(others))
    pair, frames, stretch_target = tie(pair, frames, stretch_target)
    partner = lax.ppermute(stretch_target, "yh", [(0, 1), (1, 0)])
    column = gather(pair, ZA, Z)

    window = CORE * length
    outer = 2 * SPAN
    normed, inverse_scale = normalize(frames[0].astype(F32))
    packet = marked(normed.astype(BF16), live_mask[0])
    packet_other = swap(packet)
    rows_win = both_cores(packet[:length], packet_other[:length])
    live_win = both_cores(packet[length, :length], packet_other[length, :length])
    before, behind = from_neighbours(
        marked(rows_win[:outer], live_win[:outer]),
        marked(rows_win[window - outer :], live_win[window - outer :]),
    )
    rows_ext = jnp.concatenate([before[:outer], rows_win, behind[:outer]], axis=0)
    live_ext = jnp.concatenate([before[outer, :outer], live_win, behind[outer, :outer]]).astype(F32)
    live_ext = live_ext[:, None]

    column, rows_ext, kernel, partner = tie(column, rows_ext, kernel, partner)
    lin, gate, all_targets, rows_ext = gather_weight(column, stretch_target, partner, rows_ext)

    feature = jnp.arange(width, dtype=jnp.int32)
    order_lin, order_gate = feature_order(True), feature_order(False)
    to_lin = (feature[:, None] == order_lin[None, :]).astype(BF16)
    to_gate = (feature[:, None] == order_gate[None, :]).astype(BF16)
    normed_lin = jnp.dot(rows_ext, to_lin, preferred_element_type=F32).astype(BF16)
    normed_gate = jnp.dot(rows_ext, to_gate, preferred_element_type=F32).astype(BF16)


    def entries_of(target, group):
        dest = jnp.where(target >= 0, target // capacity, -1)
        away = (target >= 0) & (dest != group)
        alike = (dest[:, None] == dest[None, :]) & away[None, :] & earlier
        rank = jnp.sum(alike.astype(jnp.int32), axis=1)
        return jnp.where(away, dest * per_peer + rank, -1)

    target = stretch_target[0]
    named_slot = target >= 0
    local = named_slot & (target // capacity == own_group)
    selector = (entries_of(target, own_group)[None, :] == entry_ids[:, None]).astype(BF16)
    local_pick = ((target % capacity)[None, :] == capacity_index[:, None]) & local[None, :]
    local_pick = local_pick.astype(BF16)

    group_ids = jnp.arange(groups, dtype=jnp.int32)
    arriving = jax.vmap(entries_of)(all_targets, group_ids)
    wanted = own_group * per_peer + jnp.arange(per_peer, dtype=jnp.int32)
    carried = arriving[:, None, :] == wanted[None, :, None]
    codes_home = (
        jnp.sum(jnp.where(carried, (all_targets % capacity + 1)[:, None, :], 0), axis=2) - 1
    ).reshape(entries)

    def leaving(values):
        pieces = values.reshape(slot_count, stretch_len, width)
        return jnp.einsum("es,sfw->efw", selector, pieces, preferred_element_type=F32).astype(BF16)

    def place_home(values, arrived):
        pieces = values.reshape(slot_count, stretch_len, width)
        placing = (codes_home[None, :] == capacity_index[:, None]).astype(BF16)
        placed = jnp.einsum("ce,efw->cfw", placing, arrived, preferred_element_type=F32)
        placed = placed + jnp.einsum("cs,sfw->cfw", local_pick, pieces, preferred_element_type=F32)
        return placed.astype(BF16).reshape(rows_here, width)

    def returning(values):
        pieces = values.reshape(capacity, stretch_len, width)
        picking = (codes_home[:, None] == capacity_index[None, :]).astype(BF16)
        return jnp.einsum("ec,cfw->efw", picking, pieces, preferred_element_type=F32).astype(BF16)

    def place_back(values, arrived):
        pieces = values.reshape(capacity, stretch_len, width)
        placed = jnp.einsum("es,efw->sfw", selector, arrived, preferred_element_type=F32)
        placed = placed + jnp.einsum("cs,cfw->sfw", local_pick, pieces, preferred_element_type=F32)
        return placed.astype(BF16).reshape(length, width)

    weight_lin, weight_gate = gather_four(lin, XA), gather_four(gate, YA)
    weight_lin, weight_gate, outgoing = tie(weight_lin, weight_gate, returning(out_grad[0]))
    grad_arrived = exchange(outgoing, DP)

    linear = jnp.dot(normed_lin, weight_lin, preferred_element_type=F32)
    gate = jax.nn.sigmoid(jnp.dot(normed_gate, weight_gate, preferred_element_type=F32))
    unit_ext = jnp.where(live_ext > 0, linear * gate, 0.0).astype(BF16)

    core = lax.axis_index(CA)
    taps_own = lax.dynamic_slice_in_dim(kernel, core * half, half, axis=1)
    inner = window + 2 * SPAN
    live_inner = live_ext[SPAN : SPAN + inner]
    live_own = live_ext[outer : outer + window]
    mixed_time = live_inner * depthwise(unit_ext[1:], taps_own, inner)
    grad_arrived, mixed_time = tie(grad_arrived, mixed_time)
    grad_time = place_back(out_grad[0], grad_arrived)
    mine = pick(grad_time[:, :half], grad_time[:, half:])
    others = pick(grad_time[:, half:], grad_time[:, :half])
    grad_win = both_cores(mine, swap(others))
    near, far = from_edges(
        pick(others[:SPAN], others[length - SPAN :]), pick(mine[:SPAN], mine[length - SPAN :])
    )
    grad_ext = jnp.concatenate([pick(near, far), grad_win, pick(far, near)], axis=0).astype(F32)

    mean_own = jnp.mean(mixed_time, axis=-1)
    rest_own = mixed_time - mean_own[:, None]
    square_own = jnp.sum(rest_own * rest_own, axis=-1)
    mean_there, square_there = swap(jnp.stack([mean_own, square_own]))
    apart = 0.5 * (mean_there - mean_own)
    spread = (square_own + square_there) / width + apart * apart
    norm_scale = lax.rsqrt(spread + EPSILON)[:, None]
    norm_time = (rest_own - apart[:, None]) * norm_scale
    sigma = jax.nn.sigmoid(norm_time)
    inner_rows = slice(SPAN, SPAN + window)
    silu = (norm_time * sigma)[inner_rows].astype(BF16)
    silu_low, silu_high = silu[:length], silu[length:]
    silu_there = swap(pick(silu_high, silu_low))
    silu_here = pick(silu_low, silu_high)
    silu_own = jnp.concatenate([pick(silu_here, silu_there), pick(silu_there, silu_here)], axis=1)
    output_time = (frames[0].astype(F32) + silu_own.astype(F32)).astype(BF16)

    grad_norm = grad_ext * sigma * (1.0 + norm_time * (1.0 - sigma))
    sums = jnp.stack([jnp.sum(grad_norm, axis=-1), jnp.sum(grad_norm * norm_time, axis=-1)])
    means = (sums + swap(sums)) / width
    grad_mixed = (
        live_inner * norm_scale * (grad_norm - means[0][:, None] - norm_time * means[1][:, None])
    ).astype(BF16)
    grad_mixed, outgoing = tie(grad_mixed, leaving(output_time))
    mixed_arrived = exchange(outgoing, DP)
    grad_unit = (live_own * depthwise(grad_mixed[1:], taps_own[::-1], window)).astype(BF16)
    terms = kernel_terms(grad_mixed[inner_rows], unit_ext[SPAN + 1 :], window, taps)

    outer_rows = slice(outer, outer + window)
    grad_float = grad_unit.astype(F32)
    gate_own = gate[outer_rows]
    pre_lin = (grad_float * gate_own).astype(BF16)
    pre_gate = (grad_float * linear[outer_rows] * gate_own * (1.0 - gate_own)).astype(BF16)

    pre_lin, pre_gate, terms, mixed_arrived = tie(pre_lin, pre_gate, terms, mixed_arrived)

    def term(left, right):
        value = lax.dot_general(
            left[outer_rows], right, (((0,), (0,)), ((), ())), preferred_element_type=F32
        )
        return (loss_scale * value).astype(BF16)

    term_lin, term_gate = term(normed_lin, pre_lin), term(normed_gate, pre_gate)
    terms = (loss_scale * jnp.pad(terms, ((0, 1), (0, 0)))).astype(BF16)
    rows, quarters = width // X, terms.reshape(X, terms.shape[0] // X, half)
    at = lax.axis_index(XA)

    def with_taps(k):
        part = lax.dynamic_index_in_dim(quarters, (at - k) % X, 0, keepdims=False)
        return jnp.concatenate([term_lin[k * rows : (k + 1) * rows], part], axis=0)

    gate_chunks = [term_gate[k * rows : (k + 1) * rows] for k in range(Y)]
    lin_chunks = [with_taps(k) for k in range(X)]
    gate_down, gate_up, lin_down, lin_up, pre_lin, pre_gate, mixed_arrived = tie(
        *messages(gate_chunks), *messages(lin_chunks), pre_lin, pre_gate, mixed_arrived
    )
    gate_sum = scatter_four(gate_chunks, gate_down, gate_up, YA)
    lin = scatter_four(lin_chunks, lin_down, lin_up, XA)
    partial_grad = back_product(pre_lin, pre_gate, weight_lin, weight_gate, order_lin, order_gate)
    mixed_rows = place_home(output_time, mixed_arrived)
    lin, gate_sum, partial_grad, mixed_rows = tie(lin, gate_sum, partial_grad, mixed_rows)
    full, partial_grad = scatter_middle(lin[:rows], gate_sum, lin[rows:], partial_grad)
    low, high = partial_grad[:length], partial_grad[length:]
    grad_normed = pick(low, high) + swap(pick(high, low).astype(BF16)).astype(F32)
    branch = inverse_scale * (
        grad_normed
        - jnp.mean(grad_normed, axis=-1, keepdims=True)
        - normed * jnp.mean(grad_normed * normed, axis=-1, keepdims=True)
    )
    named_rows = jnp.repeat(named_slot, stretch_len)[:, None]
    frame_grad = jnp.where(named_rows, grad_time.astype(F32) + branch, 0.0).astype(BF16)
    arrived, frame_grad = tie(exchange(full, ZA), frame_grad)
    weight_grad, kernel_grad = scatter_last(arrived, rows // Y // Z)
    kernel_grad = kernel_grad[:taps]
    return (mixed_rows[None], frame_grad[None], weight_grad, kernel_grad)


def solution(mesh):
    fine = Mesh(mesh.devices.reshape(X, YH, Z, YL, CORE), ("x", "yh", "z", "yl", "core"))
    every = DP + TM
    placed = (
        P(DP, TM, None),
        P(DP, TM),
        P(DP, TM),
        P(every, None),
        P(),
        P(DP, TM, None),
    )
    return jax.shard_map(
        shards,
        mesh=fine,
        in_specs=placed,
        out_specs=(P(DP, TM, None), P(DP, TM, None), P(every, None), P()),
        check_vma=False,
    )
```

```python
import jax
import jax.numpy as jnp
from jax import lax
from jax.experimental import pallas as pl
from jax.experimental.pallas import tpu as pltpu
from jax.sharding import Mesh
from jax.sharding import PartitionSpec as P

EPSILON = 1e-05
X, YH, Z, YL, CORE = 4, 2, 8, 2, 2
Y = YH * YL
XA, YA, ZA, CA = "x", ("yh", "yl"), "z", "core"
DP = ("x", "yh")
TM = ("z", "yl", "core")
CHIPS = ("z", "yl")
SHARE = 6
SPAN = 16
F32, BF16 = jnp.float32, jnp.bfloat16


def swap(value):
    return lax.ppermute(value, CA, [(0, 1), (1, 0)])


def pick(low, high):
    return jnp.where(lax.axis_index(CA) == 0, low, high)


def exchange(value, axis):
    return lax.all_to_all(value, axis, split_axis=0, concat_axis=0, tiled=True)


def gather(value, axis, count):
    rows, width = value.shape
    copies = jnp.broadcast_to(value[None], (count, rows, width))
    return exchange(copies, axis).reshape(count * rows, width)


def scatter(value, axis, count):
    rows, width = value.shape
    arrived = exchange(value.reshape(count, rows // count, width), axis)
    return jnp.sum(arrived.astype(F32), axis=0)


def shift(value, axis, count, by):
    return lax.ppermute(value, axis, [(i, (i + by) % count) for i in range(count)])


def gather_ring(value, axis, count):
    return jnp.concatenate([value] + [shift(value, axis, count, k) for k in range(1, count)], axis=0)


def ring_chunks(value, axis, count):
    rows = value.shape[0] // count
    return [value[:rows]] + [
        shift(value[k * rows : (k + 1) * rows], axis, count, -k) for k in range(1, count)
    ]


def gather_four(value, axis):
    cut = value.shape[0] // 16 * 8
    back, ahead = shift(value, axis, 4, 1), shift(value, axis, 4, -1)
    far = [shift(back[:cut], axis, 4, 1), shift(ahead[cut:], axis, 4, -1)]
    return jnp.concatenate([value, back] + far + [ahead], axis=0)


def messages(chunks):
    _, back, far, ahead = chunks
    cut = far.shape[0] // 16 * 8
    return (
        jnp.concatenate([far[:cut], back[cut:]], axis=0),
        jnp.concatenate([ahead[:cut], far[cut:]], axis=0),
    )


def scatter_four(chunks, down, up, axis):
    own, back, _, ahead = chunks
    cut = own.shape[0] // 16 * 8
    first, second = shift(down, axis, 4, -1), shift(up, axis, 4, 1)
    first_more = shift(add_up([back[:cut], first[:cut]]), axis, 4, -1)
    second_more = shift(add_up([ahead[cut:], second[cut:]]), axis, 4, 1)
    upper = add_up([own[:cut], second[:cut], first_more])
    lower = add_up([own[cut:], first[cut:], second_more])
    return jnp.concatenate([upper, lower], axis=0)


def add_up(chunks):
    total = chunks[0].astype(F32)
    for chunk in chunks[1:]:
        total = total + chunk.astype(F32)
    return total.astype(BF16)


def tie(*values):
    return lax.optimization_barrier(values)


def normalize(values):
    center = jnp.mean(values, axis=-1, keepdims=True)
    shifted = values - center
    spread = jnp.mean(shifted * shifted, axis=-1, keepdims=True)
    inverse_scale = lax.rsqrt(spread + EPSILON)
    return (shifted * inverse_scale, inverse_scale)


def depthwise(padded, kernel, length):
    running = jnp.zeros((length, padded.shape[1]), F32)
    for offset in range(kernel.shape[0]):
        running = running + kernel[offset] * padded[offset : offset + length].astype(F32)
    return running


def marked(values, marks):
    row = jnp.pad(marks.astype(values.dtype), (0, values.shape[1] - marks.shape[0]))[None]
    return jnp.concatenate([values, row], axis=0)


def both_cores(own, other):
    return pick(jnp.concatenate([own, other], axis=0), jnp.concatenate([other, own], axis=0))


def from_neighbours(head, tail):
    count = Z * YL
    before = lax.ppermute(tail, CHIPS, [(i, i + 1) for i in range(count - 1)])
    after_ = lax.ppermute(head, CHIPS, [(i + 1, i) for i in range(count - 1)])
    return before, after_


def from_edges(near, far):
    ends = range(Z * YL - 1)
    ahead = [(2 * i + 1, 2 * i + 2) for i in ends] + [(2 * i + 2, 2 * i + 1) for i in ends]
    along = [(2 * i + 1, 2 * i + 3) for i in ends] + [(2 * i + 2, 2 * i) for i in ends]
    return lax.ppermute(near, TM, ahead), lax.ppermute(far, TM, along)


def feature_order(x_first):
    row = jnp.arange(X * Y * Z * CORE * SHARE, dtype=jnp.int32)
    within = row % (CORE * SHARE)
    zs = row // (CORE * SHARE) % Z
    second = row // (CORE * SHARE * Z) % 4
    first = row // (CORE * SHARE * Z * 4) % 4
    xs, ky = ((lax.axis_index(XA) - first) % X, second) if x_first else (second, first)
    ys = (lax.axis_index(YA) - ky) % Y
    device = (((xs * YH + ys // YL) * Z + zs) * YL + ys % YL) * CORE
    return device * SHARE + within


def own_columns(value):
    rows, width = value.shape
    parts = value.reshape(rows, 2, CORE, width // 4)
    low = parts[:, :, 0].reshape(rows, width // 2)
    high = parts[:, :, 1].reshape(rows, width // 2)
    return pick(low, high), pick(high, low)


def gather_weight(column, target, partner, beside):
    rows, width = column.shape[0], column.shape[1] // 2
    slots = target.shape[1]
    known = jnp.concatenate([target, partner], axis=1).astype(BF16)
    known = jnp.pad(known, ((0, 7), (0, width - 2 * slots)))
    lin = gather_ring(column[:, :width], YA, Y)
    gate = gather(jnp.concatenate([column[:, width:], known], axis=0), XA, X)
    gate, beside = tie(gate.reshape(X, rows + 8, width), beside)
    here, there = gate[:, rows, :slots], gate[:, rows, slots : 2 * slots]
    first = lax.axis_index("yh") == 0
    targets = jnp.stack([jnp.where(first, here, there), jnp.where(first, there, here)], axis=1)
    targets = targets.reshape(X * YH, slots).astype(jnp.int32)
    return lin, gate[:, :rows].reshape(X * rows, width), targets, beside


def in_turn(pieces, at):
    count = len(pieces)
    ring = jnp.stack([pieces[(-j) % count] for j in range(2 * count - 1)])
    turned = lax.dynamic_slice_in_dim(ring, (-at) % count, count, axis=0)
    return turned.reshape(count * pieces[0].shape[0], pieces[0].shape[1])


def scatter_middle(lin, gate, part, beside):
    rows, width = lin.shape[0] // Y, lin.shape[1]
    stacked = jnp.concatenate(
        [piece for k in range(Y) for piece in (lin[k * rows : (k + 1) * rows], part)], axis=0
    )
    lin = add_up(ring_chunks(stacked, YA, Y))
    part = lin[rows:].reshape(part.shape[0] // 2, 2 * width)
    gate = scatter(gate, XA, X).astype(BF16)
    pair = jnp.concatenate([lin[:rows], gate], axis=1).reshape(Z, rows // Z, 2 * width)
    full = jnp.concatenate([pair, jnp.broadcast_to(part[None], (Z,) + part.shape)], axis=1)
    return tie(full, beside)


def scatter_last(arrived, pair_rows):
    share, width = pair_rows // 2, arrived.shape[2] // 2
    taps = 2 * (arrived.shape[1] - pair_rows)
    total = jnp.sum(arrived.astype(F32), axis=0)
    low, high, part = total[:share], total[share:pair_rows], total[pair_rows:]
    mine = pick(low, high)
    there = swap(jnp.concatenate([pick(high, low), part], axis=0))
    other = there[:share]
    first, second = pick(mine, other), pick(other, mine)
    weight_grad = jnp.concatenate(
        [first[:, :width], second[:, :width], first[:, width:], second[:, width:]], axis=1
    )
    part, other = part.reshape(taps, width), there[share:].reshape(taps, width)
    part = jnp.concatenate([pick(part, other), pick(other, part)], axis=1)
    parts = [part] + [shift(part, XA, X, k) for k in range(1, X)]
    return weight_grad, in_turn(parts, lax.axis_index(XA))


def back_kernel(pre_lin, pre_gate, lin, gate, order_lin, order_gate, out):
    @pl.when(pl.program_id(0) == 0)
    def _():
        out[...] = jnp.zeros_like(out)

    across = (((1,), (1,)), ((), ()))
    total = out[...]
    for pre, weight, order in ((pre_lin, lin, order_lin), (pre_gate, gate, order_gate)):
        value = lax.dot_general(pre[...], weight[...], across, preferred_element_type=F32)
        feature = lax.broadcasted_iota(jnp.int32, (out.shape[1], order.shape[1]), 0)
        place = jnp.where(feature == order[...], 1.0, 0.0).astype(BF16)
        total = total + lax.dot_general(
            value.astype(BF16), place, across, preferred_element_type=F32
        )
    out[...] = total


def back_product(pre_lin, pre_gate, lin, gate, order_lin, order_gate):
    rows, half = pre_lin.shape
    width, block = lin.shape[0], 384
    whole = pl.BlockSpec((rows, half), lambda i: (0, 0))
    part = pl.BlockSpec((block, half), lambda i: (i, 0))
    order = pl.BlockSpec((1, block), lambda i: (0, i))
    return pl.pallas_call(
        back_kernel,
        grid=(width // block,),
        in_specs=[whole, whole, part, part, order, order],
        out_specs=pl.BlockSpec((rows, width), lambda i: (0, 0)),
        out_shape=jax.ShapeDtypeStruct((rows, width), F32),
        compiler_params=pltpu.CompilerParams(vmem_limit_bytes=32 * 1024 * 1024),
        cost_estimate=pl.CostEstimate(
            flops=4 * rows * width * (half + width), bytes_accessed=8 * rows * width, transcendentals=0
        ),
        name="back_product",
    )(pre_lin, pre_gate, lin, gate, order_lin[None], order_gate[None])


def taps_kernel(grad, unit, live, linear, gate, taps, pre_lin, pre_gate, terms, grad_wide, unit_wide):
    grad_wide[...] = grad[...].astype(F32)
    unit_wide[...] = unit[...].astype(F32)
    count, tile = terms.shape[0] - 1, 64
    sums = [jnp.zeros((8, grad.shape[1]), F32) for _ in range(count)]
    for start in range(0, pre_lin.shape[0], tile):
        total = jnp.zeros((tile, grad.shape[1]), F32)
        for k in range(count):
            total = total + taps[k : k + 1, :] * grad_wide[start + count - k : start + count - k + tile, :]
        total = (live[start : start + tile, :] * total).astype(BF16).astype(F32)
        rows = slice(start + 2 * SPAN, start + 2 * SPAN + tile)
        share = gate[rows, :]
        pre_lin[start : start + tile, :] = (total * share).astype(BF16)
        pre_gate[start : start + tile, :] = (total * linear[rows, :] * share * (1.0 - share)).astype(BF16)
        here = grad_wide[start + SPAN : start + SPAN + tile, :]
        for k in range(count):
            first = start + SPAN + 1 + k
            product = here * unit_wide[first : first + tile, :]
            sums[k] = sums[k] + jnp.sum(product.reshape(tile // 8, 8, grad.shape[1]), axis=0)
    for k in range(count):
        terms[k : k + 1, :] = jnp.sum(sums[k], axis=0, keepdims=True)
    terms[count:, :] = jnp.zeros_like(terms[count:, :])


def taps_back(grad, unit, live, linear, gate, taps):
    width, block = grad.shape[1], 128
    rows = live.shape[0]

    def columns(length):
        return pl.BlockSpec((length, block), lambda i: (0, i))

    padded = taps.shape[0] + 1
    return pl.pallas_call(
        taps_kernel,
        grid=(width // block,),
        in_specs=[
            columns(grad.shape[0]),
            columns(unit.shape[0]),
            pl.BlockSpec((rows, 1), lambda i: (0, 0)),
            columns(unit.shape[0]),
            columns(unit.shape[0]),
            columns(padded),
        ],
        out_specs=[columns(rows), columns(rows), columns(padded)],
        out_shape=[
            jax.ShapeDtypeStruct((rows, width), BF16),
            jax.ShapeDtypeStruct((rows, width), BF16),
            jax.ShapeDtypeStruct((padded, width), F32),
        ],
        scratch_shapes=[
            pltpu.VMEM((grad.shape[0], block), F32),
            pltpu.VMEM((unit.shape[0], block), F32),
        ],
        compiler_params=pltpu.CompilerParams(vmem_limit_bytes=32 * 1024 * 1024),
        cost_estimate=pl.CostEstimate(
            flops=4 * rows * width * taps.shape[0], bytes_accessed=16 * rows * width, transcendentals=0
        ),
        name="taps_back",
    )(grad, unit, live, linear, gate, jnp.pad(taps, ((0, 1), (0, 0))))


def shards(frames, live_mask, stretch_target, pw_weight, kernel, out_grad):
    groups = X * YH
    own_group = lax.axis_index(DP)
    slot_count = stretch_target.shape[1]
    width = frames.shape[2]
    stretch_len = frames.shape[1] // slot_count
    capacity = out_grad.shape[1] // stretch_len
    per_peer = slot_count // 4
    entries = groups * per_peer
    taps = kernel.shape[0]
    length = slot_count * stretch_len
    rows_here = capacity * stretch_len
    half = width // CORE
    loss_scale = float(groups * Z * YL * CORE * rows_here) ** (-0.5)
    capacity_index = jnp.arange(capacity, dtype=jnp.int32)
    entry_ids = jnp.arange(entries, dtype=jnp.int32)
    slot_index = jnp.arange(slot_count, dtype=jnp.int32)
    earlier = slot_index[:, None] > slot_index[None, :]

    columns, others = own_columns(pw_weight)
    pair = both_cores(columns, swap(others))
    pair, frames, stretch_target = tie(pair, frames, stretch_target)
    partner = lax.ppermute(stretch_target, "yh", [(0, 1), (1, 0)])
    column = gather(pair, ZA, Z)

    window = CORE * length
    outer = 2 * SPAN
    normed, inverse_scale = normalize(frames[0].astype(F32))
    packet = marked(normed.astype(BF16), live_mask[0])
    packet_other = swap(packet)
    rows_win = both_cores(packet[:length], packet_other[:length])
    live_win = both_cores(packet[length, :length], packet_other[length, :length])
    before, behind = from_neighbours(
        marked(rows_win[:outer], live_win[:outer]),
        marked(rows_win[window - outer :], live_win[window - outer :]),
    )
    rows_ext = jnp.concatenate([before[:outer], rows_win, behind[:outer]], axis=0)
    live_ext = jnp.concatenate([before[outer, :outer], live_win, behind[outer, :outer]]).astype(F32)
    live_ext = live_ext[:, None]

    column, rows_ext, kernel, partner = tie(column, rows_ext, kernel, partner)
    lin, gate, all_targets, rows_ext = gather_weight(column, stretch_target, partner, rows_ext)

    feature = jnp.arange(width, dtype=jnp.int32)
    order_lin, order_gate = feature_order(True), feature_order(False)
    to_lin = (feature[:, None] == order_lin[None, :]).astype(BF16)
    to_gate = (feature[:, None] == order_gate[None, :]).astype(BF16)
    normed_lin = jnp.dot(rows_ext, to_lin, preferred_element_type=F32).astype(BF16)
    normed_gate = jnp.dot(rows_ext, to_gate, preferred_element_type=F32).astype(BF16)


    def entries_of(target, group):
        dest = jnp.where(target >= 0, target // capacity, -1)
        away = (target >= 0) & (dest != group)
        alike = (dest[:, None] == dest[None, :]) & away[None, :] & earlier
        rank = jnp.sum(alike.astype(jnp.int32), axis=1)
        return jnp.where(away, dest * per_peer + rank, -1)

    target = stretch_target[0]
    named_slot = target >= 0
    local = named_slot & (target // capacity == own_group)
    selector = (entries_of(target, own_group)[None, :] == entry_ids[:, None]).astype(BF16)
    local_pick = ((target % capacity)[None, :] == capacity_index[:, None]) & local[None, :]
    local_pick = local_pick.astype(BF16)

    group_ids = jnp.arange(groups, dtype=jnp.int32)
    arriving = jax.vmap(entries_of)(all_targets, group_ids)
    wanted = own_group * per_peer + jnp.arange(per_peer, dtype=jnp.int32)
    carried = arriving[:, None, :] == wanted[None, :, None]
    codes_home = (
        jnp.sum(jnp.where(carried, (all_targets % capacity + 1)[:, None, :], 0), axis=2) - 1
    ).reshape(entries)

    def leaving(values):
        pieces = values.reshape(slot_count, stretch_len, width)
        return jnp.einsum("es,sfw->efw", selector, pieces, preferred_element_type=F32).astype(BF16)

    def place_home(values, arrived):
        pieces = values.reshape(slot_count, stretch_len, width)
        placing = (codes_home[None, :] == capacity_index[:, None]).astype(BF16)
        placed = jnp.einsum("ce,efw->cfw", placing, arrived, preferred_element_type=F32)
        placed = placed + jnp.einsum("cs,sfw->cfw", local_pick, pieces, preferred_element_type=F32)
        return placed.astype(BF16).reshape(rows_here, width)

    def returning(values):
        pieces = values.reshape(capacity, stretch_len, width)
        picking = (codes_home[:, None] == capacity_index[None, :]).astype(BF16)
        return jnp.einsum("ec,cfw->efw", picking, pieces, preferred_element_type=F32).astype(BF16)

    def place_back(values, arrived):
        pieces = values.reshape(capacity, stretch_len, width)
        placed = jnp.einsum("es,efw->sfw", selector, arrived, preferred_element_type=F32)
        placed = placed + jnp.einsum("cs,cfw->sfw", local_pick, pieces, preferred_element_type=F32)
        return placed.astype(BF16).reshape(length, width)

    weight_lin, weight_gate = gather_four(lin, XA), gather_four(gate, YA)
    weight_lin, weight_gate, outgoing = tie(weight_lin, weight_gate, returning(out_grad[0]))
    grad_arrived = exchange(outgoing, DP)

    linear = jnp.dot(normed_lin, weight_lin, preferred_element_type=F32)
    gate = jax.nn.sigmoid(jnp.dot(normed_gate, weight_gate, preferred_element_type=F32))
    unit_ext = jnp.where(live_ext > 0, linear * gate, 0.0).astype(BF16)

    core = lax.axis_index(CA)
    taps_own = lax.dynamic_slice_in_dim(kernel, core * half, half, axis=1)
    inner = window + 2 * SPAN
    live_inner = live_ext[SPAN : SPAN + inner]
    live_own = live_ext[outer : outer + window]
    mixed_time = live_inner * depthwise(unit_ext[1:], taps_own, inner)
    grad_arrived, mixed_time = tie(grad_arrived, mixed_time)
    grad_time = place_back(out_grad[0], grad_arrived)
    mine = pick(grad_time[:, :half], grad_time[:, half:])
    others = pick(grad_time[:, half:], grad_time[:, :half])
    grad_win = both_cores(mine, swap(others))
    near, far = from_edges(
        pick(others[:SPAN], others[length - SPAN :]), pick(mine[:SPAN], mine[length - SPAN :])
    )
    grad_ext = jnp.concatenate([pick(near, far), grad_win, pick(far, near)], axis=0).astype(F32)

    mean_own = jnp.mean(mixed_time, axis=-1)
    rest_own = mixed_time - mean_own[:, None]
    square_own = jnp.sum(rest_own * rest_own, axis=-1)
    mean_there, square_there = swap(jnp.stack([mean_own, square_own]))
    apart = 0.5 * (mean_there - mean_own)
    spread = (square_own + square_there) / width + apart * apart
    norm_scale = lax.rsqrt(spread + EPSILON)[:, None]
    norm_time = (rest_own - apart[:, None]) * norm_scale
    sigma = jax.nn.sigmoid(norm_time)
    inner_rows = slice(SPAN, SPAN + window)
    silu = (norm_time * sigma)[inner_rows].astype(BF16)
    silu_low, silu_high = silu[:length], silu[length:]
    silu_there = swap(pick(silu_high, silu_low))
    silu_here = pick(silu_low, silu_high)
    silu_own = jnp.concatenate([pick(silu_here, silu_there), pick(silu_there, silu_here)], axis=1)
    output_time = (frames[0].astype(F32) + silu_own.astype(F32)).astype(BF16)

    grad_norm = grad_ext * sigma * (1.0 + norm_time * (1.0 - sigma))
    sums = jnp.stack([jnp.sum(grad_norm, axis=-1), jnp.sum(grad_norm * norm_time, axis=-1)])
    means = (sums + swap(sums)) / width
    grad_mixed = (
        live_inner * norm_scale * (grad_norm - means[0][:, None] - norm_time * means[1][:, None])
    ).astype(BF16)
    grad_mixed, outgoing = tie(grad_mixed, leaving(output_time))
    mixed_arrived = exchange(outgoing, DP)
    pre_lin, pre_gate, terms = taps_back(grad_mixed, unit_ext, live_own, linear, gate, taps_own)

    outer_rows = slice(outer, outer + window)
    pre_lin, pre_gate, terms, mixed_arrived = tie(pre_lin, pre_gate, terms, mixed_arrived)

    def term(left, right):
        value = lax.dot_general(
            left[outer_rows], right, (((0,), (0,)), ((), ())), preferred_element_type=F32
        )
        return (loss_scale * value).astype(BF16)

    term_lin, term_gate = term(normed_lin, pre_lin), term(normed_gate, pre_gate)
    terms = (loss_scale * terms).astype(BF16)
    rows, quarters = width // X, terms.reshape(X, terms.shape[0] // X, half)
    at = lax.axis_index(XA)

    def with_taps(k):
        part = lax.dynamic_index_in_dim(quarters, (at - k) % X, 0, keepdims=False)
        return jnp.concatenate([term_lin[k * rows : (k + 1) * rows], part], axis=0)

    gate_chunks = [term_gate[k * rows : (k + 1) * rows] for k in range(Y)]
    lin_chunks = [with_taps(k) for k in range(X)]
    gate_down, gate_up, lin_down, lin_up, pre_lin, pre_gate, mixed_arrived = tie(
        *messages(gate_chunks), *messages(lin_chunks), pre_lin, pre_gate, mixed_arrived
    )
    gate_sum = scatter_four(gate_chunks, gate_down, gate_up, YA)
    lin = scatter_four(lin_chunks, lin_down, lin_up, XA)
    partial_grad = back_product(pre_lin, pre_gate, weight_lin, weight_gate, order_lin, order_gate)
    mixed_rows = place_home(output_time, mixed_arrived)
    lin, gate_sum, partial_grad, mixed_rows = tie(lin, gate_sum, partial_grad, mixed_rows)
    full, partial_grad = scatter_middle(lin[:rows], gate_sum, lin[rows:], partial_grad)
    low, high = partial_grad[:length], partial_grad[length:]
    grad_normed = pick(low, high) + swap(pick(high, low).astype(BF16)).astype(F32)
    branch = inverse_scale * (
        grad_normed
        - jnp.mean(grad_normed, axis=-1, keepdims=True)
        - normed * jnp.mean(grad_normed * normed, axis=-1, keepdims=True)
    )
    named_rows = jnp.repeat(named_slot, stretch_len)[:, None]
    frame_grad = jnp.where(named_rows, grad_time.astype(F32) + branch, 0.0).astype(BF16)
    arrived, frame_grad = tie(exchange(full, ZA), frame_grad)
    weight_grad, kernel_grad = scatter_last(arrived, rows // Y // Z)
    kernel_grad = kernel_grad[:taps]
    return (mixed_rows[None], frame_grad[None], weight_grad, kernel_grad)


def solution(mesh):
    fine = Mesh(mesh.devices.reshape(X, YH, Z, YL, CORE), ("x", "yh", "z", "yl", "core"))
    every = DP + TM
    placed = (
        P(DP, TM, None),
        P(DP, TM),
        P(DP, TM),
        P(every, None),
        P(),
        P(DP, TM, None),
    )
    return jax.shard_map(
        shards,
        mesh=fine,
        in_specs=placed,
        out_specs=(P(DP, TM, None), P(DP, TM, None), P(every, None), P()),
        check_vma=False,
    )
```

```python
import jax
import jax.numpy as jnp
from jax import lax
from jax.experimental import pallas as pl
from jax.experimental.pallas import tpu as pltpu
from jax.sharding import Mesh
from jax.sharding import PartitionSpec as P

EPSILON = 1e-05
X, YH, Z, YL, CORE = 4, 2, 8, 2, 2
Y = YH * YL
XA, YA, ZA, CA = "x", ("yh", "yl"), "z", "core"
DP = ("x", "yh")
TM = ("z", "yl", "core")
CHIPS = ("z", "yl")
SHARE = 6
SPAN = 16
F32, BF16 = jnp.float32, jnp.bfloat16


def swap(value):
    return lax.ppermute(value, CA, [(0, 1), (1, 0)])


def pick(low, high):
    return jnp.where(lax.axis_index(CA) == 0, low, high)


def exchange(value, axis):
    return lax.all_to_all(value, axis, split_axis=0, concat_axis=0, tiled=True)


def gather(value, axis, count):
    rows, width = value.shape
    copies = jnp.broadcast_to(value[None], (count, rows, width))
    return exchange(copies, axis).reshape(count * rows, width)


def scatter(value, axis, count):
    rows, width = value.shape
    arrived = exchange(value.reshape(count, rows // count, width), axis)
    return jnp.sum(arrived.astype(F32), axis=0)


def shift(value, axis, count, by):
    return lax.ppermute(value, axis, [(i, (i + by) % count) for i in range(count)])


def gather_ring(value, axis, count):
    return jnp.concatenate([value] + [shift(value, axis, count, k) for k in range(1, count)], axis=0)


def ring_chunks(value, axis, count):
    rows = value.shape[0] // count
    return [value[:rows]] + [
        shift(value[k * rows : (k + 1) * rows], axis, count, -k) for k in range(1, count)
    ]


def gather_four(value, axis):
    cut = value.shape[0] // 16 * 8
    back, ahead = shift(value, axis, 4, 1), shift(value, axis, 4, -1)
    far = [shift(back[:cut], axis, 4, 1), shift(ahead[cut:], axis, 4, -1)]
    return jnp.concatenate([value, back] + far + [ahead], axis=0)


def messages(chunks):
    _, back, far, ahead = chunks
    cut = far.shape[0] // 16 * 8
    return (
        jnp.concatenate([far[:cut], back[cut:]], axis=0),
        jnp.concatenate([ahead[:cut], far[cut:]], axis=0),
    )


def scatter_four(chunks, down, up, axis):
    own, back, _, ahead = chunks
    cut = own.shape[0] // 16 * 8
    first, second = shift(down, axis, 4, -1), shift(up, axis, 4, 1)
    first_more = shift(add_up([back[:cut], first[:cut]]), axis, 4, -1)
    second_more = shift(add_up([ahead[cut:], second[cut:]]), axis, 4, 1)
    upper = add_up([own[:cut], second[:cut], first_more])
    lower = add_up([own[cut:], first[cut:], second_more])
    return jnp.concatenate([upper, lower], axis=0)


def add_up(chunks):
    total = chunks[0].astype(F32)
    for chunk in chunks[1:]:
        total = total + chunk.astype(F32)
    return total.astype(BF16)


def tie(*values):
    return lax.optimization_barrier(values)


def normalize(values):
    center = jnp.mean(values, axis=-1, keepdims=True)
    shifted = values - center
    spread = jnp.mean(shifted * shifted, axis=-1, keepdims=True)
    inverse_scale = lax.rsqrt(spread + EPSILON)
    return (shifted * inverse_scale, inverse_scale)


def depthwise(padded, kernel, length):
    running = jnp.zeros((length, padded.shape[1]), F32)
    for offset in range(kernel.shape[0]):
        running = running + kernel[offset] * padded[offset : offset + length].astype(F32)
    return running


def marked(values, marks):
    row = jnp.pad(marks.astype(values.dtype), (0, values.shape[1] - marks.shape[0]))[None]
    return jnp.concatenate([values, row], axis=0)


def both_cores(own, other):
    return pick(jnp.concatenate([own, other], axis=0), jnp.concatenate([other, own], axis=0))


def from_neighbours(head, tail):
    count = Z * YL
    before = lax.ppermute(tail, CHIPS, [(i, i + 1) for i in range(count - 1)])
    after_ = lax.ppermute(head, CHIPS, [(i + 1, i) for i in range(count - 1)])
    return before, after_


def from_edges(near, far):
    ends = range(Z * YL - 1)
    ahead = [(2 * i + 1, 2 * i + 2) for i in ends] + [(2 * i + 2, 2 * i + 1) for i in ends]
    along = [(2 * i + 1, 2 * i + 3) for i in ends] + [(2 * i + 2, 2 * i) for i in ends]
    return lax.ppermute(near, TM, ahead), lax.ppermute(far, TM, along)


def feature_order(x_first):
    row = jnp.arange(X * Y * Z * CORE * SHARE, dtype=jnp.int32)
    within = row % (CORE * SHARE)
    zs = row // (CORE * SHARE) % Z
    second = row // (CORE * SHARE * Z) % 4
    first = row // (CORE * SHARE * Z * 4) % 4
    xs, ky = ((lax.axis_index(XA) - first) % X, second) if x_first else (second, first)
    ys = (lax.axis_index(YA) - ky) % Y
    device = (((xs * YH + ys // YL) * Z + zs) * YL + ys % YL) * CORE
    return device * SHARE + within


def own_columns(value):
    rows, width = value.shape
    parts = value.reshape(rows, 2, CORE, width // 4)
    low = parts[:, :, 0].reshape(rows, width // 2)
    high = parts[:, :, 1].reshape(rows, width // 2)
    return pick(low, high), pick(high, low)


def gather_weight(column, target, partner, beside):
    rows, width = column.shape[0], column.shape[1] // 2
    slots = target.shape[1]
    known = jnp.concatenate([target, partner], axis=1).astype(BF16)
    known = jnp.pad(known, ((0, 7), (0, width - 2 * slots)))
    lin = gather_ring(column[:, :width], YA, Y)
    gate = gather(jnp.concatenate([column[:, width:], known], axis=0), XA, X)
    gate, beside = tie(gate.reshape(X, rows + 8, width), beside)
    here, there = gate[:, rows, :slots], gate[:, rows, slots : 2 * slots]
    first = lax.axis_index("yh") == 0
    targets = jnp.stack([jnp.where(first, here, there), jnp.where(first, there, here)], axis=1)
    targets = targets.reshape(X * YH, slots).astype(jnp.int32)
    return lin, gate[:, :rows].reshape(X * rows, width), targets, beside


def in_turn(pieces, at):
    count = len(pieces)
    ring = jnp.stack([pieces[(-j) % count] for j in range(2 * count - 1)])
    turned = lax.dynamic_slice_in_dim(ring, (-at) % count, count, axis=0)
    return turned.reshape(count * pieces[0].shape[0], pieces[0].shape[1])


def scatter_middle(lin, gate, part, beside):
    rows, width = lin.shape[0] // Y, lin.shape[1]
    stacked = jnp.concatenate(
        [piece for k in range(Y) for piece in (lin[k * rows : (k + 1) * rows], part)], axis=0
    )
    lin = add_up(ring_chunks(stacked, YA, Y))
    part = lin[rows:].reshape(part.shape[0] // 2, 2 * width)
    gate = scatter(gate, XA, X).astype(BF16)
    pair = jnp.concatenate([lin[:rows], gate], axis=1).reshape(Z, rows // Z, 2 * width)
    full = jnp.concatenate([pair, jnp.broadcast_to(part[None], (Z,) + part.shape)], axis=1)
    return tie(full, beside)


def scatter_last(arrived, pair_rows):
    share, width = pair_rows // 2, arrived.shape[2] // 2
    taps = 2 * (arrived.shape[1] - pair_rows)
    total = jnp.sum(arrived.astype(F32), axis=0)
    low, high, part = total[:share], total[share:pair_rows], total[pair_rows:]
    mine = pick(low, high)
    there = swap(jnp.concatenate([pick(high, low), part], axis=0))
    other = there[:share]
    first, second = pick(mine, other), pick(other, mine)
    weight_grad = jnp.concatenate(
        [first[:, :width], second[:, :width], first[:, width:], second[:, width:]], axis=1
    )
    part, other = part.reshape(taps, width), there[share:].reshape(taps, width)
    part = jnp.concatenate([pick(part, other), pick(other, part)], axis=1)
    parts = [part] + [shift(part, XA, X, k) for k in range(1, X)]
    return weight_grad, in_turn(parts, lax.axis_index(XA))


def back_kernel(pre_lin, pre_gate, lin, gate, order_lin, order_gate, out):
    @pl.when(pl.program_id(0) == 0)
    def _():
        out[...] = jnp.zeros_like(out)

    across = (((1,), (1,)), ((), ()))
    total = out[...]
    for pre, weight, order in ((pre_lin, lin, order_lin), (pre_gate, gate, order_gate)):
        value = lax.dot_general(pre[...], weight[...], across, preferred_element_type=F32)
        feature = lax.broadcasted_iota(jnp.int32, (out.shape[1], order.shape[1]), 0)
        place = jnp.where(feature == order[...], 1.0, 0.0).astype(BF16)
        total = total + lax.dot_general(
            value.astype(BF16), place, across, preferred_element_type=F32
        )
    out[...] = total


def back_product(pre_lin, pre_gate, lin, gate, order_lin, order_gate):
    rows, half = pre_lin.shape
    width, block = lin.shape[0], 384
    whole = pl.BlockSpec((rows, half), lambda i: (0, 0))
    part = pl.BlockSpec((block, half), lambda i: (i, 0))
    order = pl.BlockSpec((1, block), lambda i: (0, i))
    return pl.pallas_call(
        back_kernel,
        grid=(width // block,),
        in_specs=[whole, whole, part, part, order, order],
        out_specs=pl.BlockSpec((rows, width), lambda i: (0, 0)),
        out_shape=jax.ShapeDtypeStruct((rows, width), F32),
        compiler_params=pltpu.CompilerParams(vmem_limit_bytes=32 * 1024 * 1024),
        cost_estimate=pl.CostEstimate(
            flops=4 * rows * width * (half + width), bytes_accessed=8 * rows * width, transcendentals=0
        ),
        name="back_product",
    )(pre_lin, pre_gate, lin, gate, order_lin[None], order_gate[None])


def taps_kernel(grad, unit, live, linear, gate, taps, pre_lin, pre_gate, terms, grad_wide, unit_wide):
    grad_wide[...] = grad[...].astype(F32)
    unit_wide[...] = unit[...].astype(F32)
    count, tile = terms.shape[0] - 1, 64
    sums = [jnp.zeros((8, grad.shape[1]), F32) for _ in range(count)]
    for start in range(0, pre_lin.shape[0], tile):
        total = jnp.zeros((tile, grad.shape[1]), F32)
        for k in range(count):
            total = total + taps[k : k + 1, :] * grad_wide[start + count - k : start + count - k + tile, :]
        total = (live[start : start + tile, :] * total).astype(BF16).astype(F32)
        rows = slice(start + 2 * SPAN, start + 2 * SPAN + tile)
        share = gate[rows, :]
        pre_lin[start : start + tile, :] = (total * share).astype(BF16)
        pre_gate[start : start + tile, :] = (total * linear[rows, :] * share * (1.0 - share)).astype(BF16)
        here = grad_wide[start + SPAN : start + SPAN + tile, :]
        for k in range(count):
            first = start + SPAN + 1 + k
            product = here * unit_wide[first : first + tile, :]
            sums[k] = sums[k] + jnp.sum(product.reshape(tile // 8, 8, grad.shape[1]), axis=0)
    for k in range(count):
        terms[k : k + 1, :] = jnp.sum(sums[k], axis=0, keepdims=True)
    terms[count:, :] = jnp.zeros_like(terms[count:, :])


def taps_back(grad, unit, live, linear, gate, taps):
    width, block = grad.shape[1], 128
    rows = live.shape[0]

    def columns(length):
        return pl.BlockSpec((length, block), lambda i: (0, i))

    padded = taps.shape[0] + 1
    return pl.pallas_call(
        taps_kernel,
        grid=(width // block,),
        in_specs=[
            columns(grad.shape[0]),
            columns(unit.shape[0]),
            pl.BlockSpec((rows, 1), lambda i: (0, 0)),
            columns(unit.shape[0]),
            columns(unit.shape[0]),
            columns(padded),
        ],
        out_specs=[columns(rows), columns(rows), columns(padded)],
        out_shape=[
            jax.ShapeDtypeStruct((rows, width), BF16),
            jax.ShapeDtypeStruct((rows, width), BF16),
            jax.ShapeDtypeStruct((padded, width), F32),
        ],
        scratch_shapes=[
            pltpu.VMEM((grad.shape[0], block), F32),
            pltpu.VMEM((unit.shape[0], block), F32),
        ],
        compiler_params=pltpu.CompilerParams(vmem_limit_bytes=32 * 1024 * 1024),
        cost_estimate=pl.CostEstimate(
            flops=4 * rows * width * taps.shape[0], bytes_accessed=16 * rows * width, transcendentals=0
        ),
        name="taps_back",
    )(grad, unit, live, linear, gate, jnp.pad(taps, ((0, 1), (0, 0))))


def shards(frames, live_mask, stretch_target, pw_weight, kernel, out_grad):
    groups = X * YH
    own_group = lax.axis_index(DP)
    slot_count = stretch_target.shape[1]
    width = frames.shape[2]
    stretch_len = frames.shape[1] // slot_count
    capacity = out_grad.shape[1] // stretch_len
    per_peer = slot_count // 4
    entries = groups * per_peer
    taps = kernel.shape[0]
    length = slot_count * stretch_len
    rows_here = capacity * stretch_len
    half = width // CORE
    loss_scale = float(groups * Z * YL * CORE * rows_here) ** (-0.5)
    capacity_index = jnp.arange(capacity, dtype=jnp.int32)
    entry_ids = jnp.arange(entries, dtype=jnp.int32)
    slot_index = jnp.arange(slot_count, dtype=jnp.int32)
    earlier = slot_index[:, None] > slot_index[None, :]

    columns, others = own_columns(pw_weight)
    pair = both_cores(columns, swap(others))
    pair, frames, stretch_target = tie(pair, frames, stretch_target)
    partner = lax.ppermute(stretch_target, "yh", [(0, 1), (1, 0)])
    column = gather(pair, ZA, Z)

    window = CORE * length
    outer = 2 * SPAN
    normed, inverse_scale = normalize(frames[0].astype(F32))
    packet = marked(normed.astype(BF16), live_mask[0])
    packet_other = swap(packet)
    rows_win = both_cores(packet[:length], packet_other[:length])
    live_win = both_cores(packet[length, :length], packet_other[length, :length])
    before, behind = from_neighbours(
        marked(rows_win[:outer], live_win[:outer]),
        marked(rows_win[window - outer :], live_win[window - outer :]),
    )
    rows_ext = jnp.concatenate([before[:outer], rows_win, behind[:outer]], axis=0)
    live_ext = jnp.concatenate([before[outer, :outer], live_win, behind[outer, :outer]]).astype(F32)
    live_ext = live_ext[:, None]

    column, rows_ext, kernel, partner = tie(column, rows_ext, kernel, partner)
    lin, gate, all_targets, rows_ext = gather_weight(column, stretch_target, partner, rows_ext)

    feature = jnp.arange(width, dtype=jnp.int32)
    order_lin, order_gate = feature_order(True), feature_order(False)
    to_lin = (feature[:, None] == order_lin[None, :]).astype(BF16)
    to_gate = (feature[:, None] == order_gate[None, :]).astype(BF16)
    normed_lin = jnp.dot(rows_ext, to_lin, preferred_element_type=F32).astype(BF16)
    normed_gate = jnp.dot(rows_ext, to_gate, preferred_element_type=F32).astype(BF16)


    def entries_of(target, group):
        dest = jnp.where(target >= 0, target // capacity, -1)
        away = (target >= 0) & (dest != group)
        alike = (dest[:, None] == dest[None, :]) & away[None, :] & earlier
        rank = jnp.sum(alike.astype(jnp.int32), axis=1)
        return jnp.where(away, dest * per_peer + rank, -1)

    target = stretch_target[0]
    named_slot = target >= 0
    local = named_slot & (target // capacity == own_group)
    selector = (entries_of(target, own_group)[None, :] == entry_ids[:, None]).astype(BF16)
    local_pick = ((target % capacity)[None, :] == capacity_index[:, None]) & local[None, :]
    local_pick = local_pick.astype(BF16)

    group_ids = jnp.arange(groups, dtype=jnp.int32)
    arriving = jax.vmap(entries_of)(all_targets, group_ids)
    wanted = own_group * per_peer + jnp.arange(per_peer, dtype=jnp.int32)
    carried = arriving[:, None, :] == wanted[None, :, None]
    codes_home = (
        jnp.sum(jnp.where(carried, (all_targets % capacity + 1)[:, None, :], 0), axis=2) - 1
    ).reshape(entries)

    def leaving(values):
        pieces = values.reshape(slot_count, stretch_len, width)
        return jnp.einsum("es,sfw->efw", selector, pieces, preferred_element_type=F32).astype(BF16)

    def place_home(values, arrived):
        pieces = values.reshape(slot_count, stretch_len, width)
        placing = (codes_home[None, :] == capacity_index[:, None]).astype(BF16)
        placed = jnp.einsum("ce,efw->cfw", placing, arrived, preferred_element_type=F32)
        placed = placed + jnp.einsum("cs,sfw->cfw", local_pick, pieces, preferred_element_type=F32)
        return placed.astype(BF16).reshape(rows_here, width)

    def returning(values):
        pieces = values.reshape(capacity, stretch_len, width)
        picking = (codes_home[:, None] == capacity_index[None, :]).astype(BF16)
        return jnp.einsum("ec,cfw->efw", picking, pieces, preferred_element_type=F32).astype(BF16)

    def place_back(values, arrived):
        pieces = values.reshape(capacity, stretch_len, width)
        placed = jnp.einsum("es,efw->sfw", selector, arrived, preferred_element_type=F32)
        placed = placed + jnp.einsum("cs,cfw->sfw", local_pick, pieces, preferred_element_type=F32)
        return placed.astype(BF16).reshape(length, width)

    weight_lin, weight_gate = gather_four(lin, XA), gather_four(gate, YA)
    weight_lin, weight_gate, outgoing = tie(weight_lin, weight_gate, returning(out_grad[0]))
    grad_arrived = exchange(outgoing, DP)

    linear = jnp.dot(normed_lin, weight_lin, preferred_element_type=F32)
    gate = jax.nn.sigmoid(jnp.dot(normed_gate, weight_gate, preferred_element_type=F32))
    unit_ext = jnp.where(live_ext > 0, linear * gate, 0.0).astype(BF16)

    core = lax.axis_index(CA)
    taps_own = lax.dynamic_slice_in_dim(kernel, core * half, half, axis=1)
    inner = window + 2 * SPAN
    live_inner = live_ext[SPAN : SPAN + inner]
    live_own = live_ext[outer : outer + window]
    mixed_time = live_inner * depthwise(unit_ext[1:], taps_own, inner)
    grad_arrived, mixed_time = tie(grad_arrived, mixed_time)
    grad_time = place_back(out_grad[0], grad_arrived)
    mine = pick(grad_time[:, :half], grad_time[:, half:])
    others = pick(grad_time[:, half:], grad_time[:, :half])
    grad_win = both_cores(mine, swap(others))
    near, far = from_edges(
        pick(others[:SPAN], others[length - SPAN :]), pick(mine[:SPAN], mine[length - SPAN :])
    )
    grad_ext = jnp.concatenate([pick(near, far), grad_win, pick(far, near)], axis=0).astype(F32)

    mean_own = jnp.mean(mixed_time, axis=-1)
    rest_own = mixed_time - mean_own[:, None]
    square_own = jnp.sum(rest_own * rest_own, axis=-1)
    mean_there, square_there = swap(jnp.stack([mean_own, square_own]))
    apart = 0.5 * (mean_there - mean_own)
    spread = (square_own + square_there) / width + apart * apart
    norm_scale = lax.rsqrt(spread + EPSILON)[:, None]
    norm_time = (rest_own - apart[:, None]) * norm_scale
    sigma = jax.nn.sigmoid(norm_time)
    inner_rows = slice(SPAN, SPAN + window)
    silu = (norm_time * sigma)[inner_rows].astype(BF16)
    silu_low, silu_high = silu[:length], silu[length:]
    silu_there = swap(pick(silu_high, silu_low))
    silu_here = pick(silu_low, silu_high)
    silu_own = jnp.concatenate([pick(silu_here, silu_there), pick(silu_there, silu_here)], axis=1)
    output_time = (frames[0].astype(F32) + silu_own.astype(F32)).astype(BF16)

    grad_ext, outgoing = tie(grad_ext, leaving(output_time))
    mixed_arrived = exchange(outgoing, DP)
    grad_norm = grad_ext * sigma * (1.0 + norm_time * (1.0 - sigma))
    sums = jnp.stack([jnp.sum(grad_norm, axis=-1), jnp.sum(grad_norm * norm_time, axis=-1)])
    means = (sums + swap(sums)) / width
    grad_mixed = (
        live_inner * norm_scale * (grad_norm - means[0][:, None] - norm_time * means[1][:, None])
    ).astype(BF16)
    pre_lin, pre_gate, terms = taps_back(grad_mixed, unit_ext, live_own, linear, gate, taps_own)

    outer_rows = slice(outer, outer + window)
    def term(left, right):
        value = lax.dot_general(
            left[outer_rows], right, (((0,), (0,)), ((), ())), preferred_element_type=F32
        )
        return (loss_scale * value).astype(BF16)

    term_lin, term_gate = term(normed_lin, pre_lin), term(normed_gate, pre_gate)
    terms = (loss_scale * terms).astype(BF16)
    rows, quarters = width // X, terms.reshape(X, terms.shape[0] // X, half)
    at = lax.axis_index(XA)

    def with_taps(k):
        part = lax.dynamic_index_in_dim(quarters, (at - k) % X, 0, keepdims=False)
        return jnp.concatenate([term_lin[k * rows : (k + 1) * rows], part], axis=0)

    gate_chunks = [term_gate[k * rows : (k + 1) * rows] for k in range(Y)]
    lin_chunks = [with_taps(k) for k in range(X)]
    gate_down, gate_up, lin_down, lin_up, pre_lin, pre_gate, mixed_arrived = tie(
        *messages(gate_chunks), *messages(lin_chunks), pre_lin, pre_gate, mixed_arrived
    )
    gate_sum = scatter_four(gate_chunks, gate_down, gate_up, YA)
    lin = scatter_four(lin_chunks, lin_down, lin_up, XA)
    partial_grad = back_product(pre_lin, pre_gate, weight_lin, weight_gate, order_lin, order_gate)
    partial_grad, mixed_arrived = tie(partial_grad, mixed_arrived)
    mixed_rows = place_home(output_time, mixed_arrived)
    lin, gate_sum, partial_grad, mixed_rows = tie(lin, gate_sum, partial_grad, mixed_rows)
    full, partial_grad = scatter_middle(lin[:rows], gate_sum, lin[rows:], partial_grad)
    low, high = partial_grad[:length], partial_grad[length:]
    grad_normed = pick(low, high) + swap(pick(high, low).astype(BF16)).astype(F32)
    branch = inverse_scale * (
        grad_normed
        - jnp.mean(grad_normed, axis=-1, keepdims=True)
        - normed * jnp.mean(grad_normed * normed, axis=-1, keepdims=True)
    )
    named_rows = jnp.repeat(named_slot, stretch_len)[:, None]
    frame_grad = jnp.where(named_rows, grad_time.astype(F32) + branch, 0.0).astype(BF16)
    arrived, frame_grad = tie(exchange(full, ZA), frame_grad)
    weight_grad, kernel_grad = scatter_last(arrived, rows // Y // Z)
    kernel_grad = kernel_grad[:taps]
    return (mixed_rows[None], frame_grad[None], weight_grad, kernel_grad)


def solution(mesh):
    fine = Mesh(mesh.devices.reshape(X, YH, Z, YL, CORE), ("x", "yh", "z", "yl", "core"))
    every = DP + TM
    placed = (
        P(DP, TM, None),
        P(DP, TM),
        P(DP, TM),
        P(every, None),
        P(),
        P(DP, TM, None),
    )
    return jax.shard_map(
        shards,
        mesh=fine,
        in_specs=placed,
        out_specs=(P(DP, TM, None), P(DP, TM, None), P(every, None), P()),
        check_vma=False,
    )
```

```python
import jax
import jax.numpy as jnp
from jax import lax
from jax.experimental import pallas as pl
from jax.experimental.pallas import tpu as pltpu
from jax.sharding import Mesh
from jax.sharding import PartitionSpec as P

EPSILON = 1e-05
X, YH, Z, YL, CORE = 4, 2, 8, 2, 2
Y = YH * YL
XA, YA, ZA, CA = "x", ("yh", "yl"), "z", "core"
DP = ("x", "yh")
TM = ("z", "yl", "core")
CHIPS = ("z", "yl")
SHARE = 6
SPAN = 16
F32, BF16 = jnp.float32, jnp.bfloat16


def swap(value):
    return lax.ppermute(value, CA, [(0, 1), (1, 0)])


def pick(low, high):
    return jnp.where(lax.axis_index(CA) == 0, low, high)


def exchange(value, axis):
    return lax.all_to_all(value, axis, split_axis=0, concat_axis=0, tiled=True)


def gather(value, axis, count):
    rows, width = value.shape
    copies = jnp.broadcast_to(value[None], (count, rows, width))
    return exchange(copies, axis).reshape(count * rows, width)


def scatter(value, axis, count):
    rows, width = value.shape
    arrived = exchange(value.reshape(count, rows // count, width), axis)
    return jnp.sum(arrived.astype(F32), axis=0)


def shift(value, axis, count, by):
    return lax.ppermute(value, axis, [(i, (i + by) % count) for i in range(count)])


def gather_ring(value, axis, count):
    return jnp.concatenate([value] + [shift(value, axis, count, k) for k in range(1, count)], axis=0)


def ring_chunks(value, axis, count):
    rows = value.shape[0] // count
    return [value[:rows]] + [
        shift(value[k * rows : (k + 1) * rows], axis, count, -k) for k in range(1, count)
    ]


def gather_four(value, axis):
    cut = value.shape[0] // 16 * 8
    back, ahead = shift(value, axis, 4, 1), shift(value, axis, 4, -1)
    far = [shift(back[:cut], axis, 4, 1), shift(ahead[cut:], axis, 4, -1)]
    return jnp.concatenate([value, back] + far + [ahead], axis=0)


def messages(chunks):
    _, back, far, ahead = chunks
    cut = far.shape[0] // 16 * 8
    return (
        jnp.concatenate([far[:cut], back[cut:]], axis=0),
        jnp.concatenate([ahead[:cut], far[cut:]], axis=0),
    )


def scatter_four(chunks, down, up, axis):
    own, back, _, ahead = chunks
    cut = own.shape[0] // 16 * 8
    first, second = shift(down, axis, 4, -1), shift(up, axis, 4, 1)
    first_more = shift(add_up([back[:cut], first[:cut]]), axis, 4, -1)
    second_more = shift(add_up([ahead[cut:], second[cut:]]), axis, 4, 1)
    upper = add_up([own[:cut], second[:cut], first_more])
    lower = add_up([own[cut:], first[cut:], second_more])
    return jnp.concatenate([upper, lower], axis=0)


def add_up(chunks):
    total = chunks[0].astype(F32)
    for chunk in chunks[1:]:
        total = total + chunk.astype(F32)
    return total.astype(BF16)


def tie(*values):
    return lax.optimization_barrier(values)


def normalize(values):
    center = jnp.mean(values, axis=-1, keepdims=True)
    shifted = values - center
    spread = jnp.mean(shifted * shifted, axis=-1, keepdims=True)
    inverse_scale = lax.rsqrt(spread + EPSILON)
    return (shifted * inverse_scale, inverse_scale)


def depthwise(padded, kernel, length):
    running = jnp.zeros((length, padded.shape[1]), F32)
    for offset in range(kernel.shape[0]):
        running = running + kernel[offset] * padded[offset : offset + length].astype(F32)
    return running


def marked(values, marks):
    row = jnp.pad(marks.astype(values.dtype), (0, values.shape[1] - marks.shape[0]))[None]
    return jnp.concatenate([values, row], axis=0)


def both_cores(own, other):
    return pick(jnp.concatenate([own, other], axis=0), jnp.concatenate([other, own], axis=0))


def from_neighbours(head, tail):
    count = Z * YL
    before = lax.ppermute(tail, CHIPS, [(i, i + 1) for i in range(count - 1)])
    after_ = lax.ppermute(head, CHIPS, [(i + 1, i) for i in range(count - 1)])
    return before, after_


def from_edges(near, far):
    ends = range(Z * YL - 1)
    ahead = [(2 * i + 1, 2 * i + 2) for i in ends] + [(2 * i + 2, 2 * i + 1) for i in ends]
    along = [(2 * i + 1, 2 * i + 3) for i in ends] + [(2 * i + 2, 2 * i) for i in ends]
    return lax.ppermute(near, TM, ahead), lax.ppermute(far, TM, along)


def feature_order(x_first):
    row = jnp.arange(X * Y * Z * CORE * SHARE, dtype=jnp.int32)
    within = row % (CORE * SHARE)
    zs = row // (CORE * SHARE) % Z
    second = row // (CORE * SHARE * Z) % 4
    first = row // (CORE * SHARE * Z * 4) % 4
    xs, ky = ((lax.axis_index(XA) - first) % X, second) if x_first else (second, first)
    ys = (lax.axis_index(YA) - ky) % Y
    device = (((xs * YH + ys // YL) * Z + zs) * YL + ys % YL) * CORE
    return device * SHARE + within


def own_columns(value):
    rows, width = value.shape
    parts = value.reshape(rows, 2, CORE, width // 4)
    low = parts[:, :, 0].reshape(rows, width // 2)
    high = parts[:, :, 1].reshape(rows, width // 2)
    return pick(low, high), pick(high, low)


def gather_weight(column, target, partner, beside):
    rows, width = column.shape[0], column.shape[1] // 2
    slots = target.shape[1]
    known = jnp.concatenate([target, partner], axis=1).astype(BF16)
    known = jnp.pad(known, ((0, 7), (0, width - 2 * slots)))
    lin = gather_ring(column[:, :width], YA, Y)
    gate = gather(jnp.concatenate([column[:, width:], known], axis=0), XA, X)
    gate, beside = tie(gate.reshape(X, rows + 8, width), beside)
    here, there = gate[:, rows, :slots], gate[:, rows, slots : 2 * slots]
    first = lax.axis_index("yh") == 0
    targets = jnp.stack([jnp.where(first, here, there), jnp.where(first, there, here)], axis=1)
    targets = targets.reshape(X * YH, slots).astype(jnp.int32)
    return lin, gate[:, :rows].reshape(X * rows, width), targets, beside


def in_turn(pieces, at):
    count = len(pieces)
    ring = jnp.stack([pieces[(-j) % count] for j in range(2 * count - 1)])
    turned = lax.dynamic_slice_in_dim(ring, (-at) % count, count, axis=0)
    return turned.reshape(count * pieces[0].shape[0], pieces[0].shape[1])


def scatter_middle(lin, gate, part, beside):
    rows, width = lin.shape[0] // Y, lin.shape[1]
    stacked = jnp.concatenate(
        [piece for k in range(Y) for piece in (lin[k * rows : (k + 1) * rows], part)], axis=0
    )
    lin = add_up(ring_chunks(stacked, YA, Y))
    part = lin[rows:].reshape(part.shape[0] // 2, 2 * width)
    gate = scatter(gate, XA, X).astype(BF16)
    pair = jnp.concatenate([lin[:rows], gate], axis=1).reshape(Z, rows // Z, 2 * width)
    full = jnp.concatenate([pair, jnp.broadcast_to(part[None], (Z,) + part.shape)], axis=1)
    return tie(full, beside)


def scatter_last(arrived, pair_rows):
    share, width = pair_rows // 2, arrived.shape[2] // 2
    taps = 2 * (arrived.shape[1] - pair_rows)
    total = jnp.sum(arrived.astype(F32), axis=0)
    low, high, part = total[:share], total[share:pair_rows], total[pair_rows:]
    mine = pick(low, high)
    there = swap(jnp.concatenate([pick(high, low), part], axis=0))
    other = there[:share]
    first, second = pick(mine, other), pick(other, mine)
    weight_grad = jnp.concatenate(
        [first[:, :width], second[:, :width], first[:, width:], second[:, width:]], axis=1
    )
    part, other = part.reshape(taps, width), there[share:].reshape(taps, width)
    part = jnp.concatenate([pick(part, other), pick(other, part)], axis=1)
    parts = [part] + [shift(part, XA, X, k) for k in range(1, X)]
    return weight_grad, in_turn(parts, lax.axis_index(XA))


def back_kernel(pre_lin, pre_gate, lin, gate, order_lin, order_gate, out):
    @pl.when(pl.program_id(0) == 0)
    def _():
        out[...] = jnp.zeros_like(out)

    across = (((1,), (1,)), ((), ()))
    total = out[...]
    for pre, weight, order in ((pre_lin, lin, order_lin), (pre_gate, gate, order_gate)):
        value = lax.dot_general(pre[...], weight[...], across, preferred_element_type=F32)
        feature = lax.broadcasted_iota(jnp.int32, (out.shape[1], order.shape[1]), 0)
        place = jnp.where(feature == order[...], 1.0, 0.0).astype(BF16)
        total = total + lax.dot_general(
            value.astype(BF16), place, across, preferred_element_type=F32
        )
    out[...] = total


def back_product(pre_lin, pre_gate, lin, gate, order_lin, order_gate):
    rows, half = pre_lin.shape
    width, block = lin.shape[0], 384
    whole = pl.BlockSpec((rows, half), lambda i: (0, 0))
    part = pl.BlockSpec((block, half), lambda i: (i, 0))
    order = pl.BlockSpec((1, block), lambda i: (0, i))
    return pl.pallas_call(
        back_kernel,
        grid=(width // block,),
        in_specs=[whole, whole, part, part, order, order],
        out_specs=pl.BlockSpec((rows, width), lambda i: (0, 0)),
        out_shape=jax.ShapeDtypeStruct((rows, width), F32),
        compiler_params=pltpu.CompilerParams(vmem_limit_bytes=32 * 1024 * 1024),
        cost_estimate=pl.CostEstimate(
            flops=4 * rows * width * (half + width), bytes_accessed=8 * rows * width, transcendentals=0
        ),
        name="back_product",
    )(pre_lin, pre_gate, lin, gate, order_lin[None], order_gate[None])


def taps_kernel(grad, unit, live, linear, gate, taps, pre_lin, pre_gate, terms, grad_wide, unit_wide):
    grad_wide[...] = grad[...].astype(F32)
    unit_wide[...] = unit[...].astype(F32)
    count, tile = terms.shape[0] - 1, 64
    sums = [jnp.zeros((8, grad.shape[1]), F32) for _ in range(count)]
    for start in range(0, pre_lin.shape[0], tile):
        total = jnp.zeros((tile, grad.shape[1]), F32)
        for k in range(count):
            total = total + taps[k : k + 1, :] * grad_wide[start + count - k : start + count - k + tile, :]
        total = (live[start : start + tile, :] * total).astype(BF16).astype(F32)
        rows = slice(start + 2 * SPAN, start + 2 * SPAN + tile)
        share = gate[rows, :]
        pre_lin[start : start + tile, :] = (total * share).astype(BF16)
        pre_gate[start : start + tile, :] = (total * linear[rows, :] * share * (1.0 - share)).astype(BF16)
        here = grad_wide[start + SPAN : start + SPAN + tile, :]
        for k in range(count):
            first = start + SPAN + 1 + k
            product = here * unit_wide[first : first + tile, :]
            sums[k] = sums[k] + jnp.sum(product.reshape(tile // 8, 8, grad.shape[1]), axis=0)
    for k in range(count):
        terms[k : k + 1, :] = jnp.sum(sums[k], axis=0, keepdims=True)
    terms[count:, :] = jnp.zeros_like(terms[count:, :])


def taps_back(grad, unit, live, linear, gate, taps):
    width, block = grad.shape[1], 128
    rows = live.shape[0]

    def columns(length):
        return pl.BlockSpec((length, block), lambda i: (0, i))

    padded = taps.shape[0] + 1
    return pl.pallas_call(
        taps_kernel,
        grid=(width // block,),
        in_specs=[
            columns(grad.shape[0]),
            columns(unit.shape[0]),
            pl.BlockSpec((rows, 1), lambda i: (0, 0)),
            columns(unit.shape[0]),
            columns(unit.shape[0]),
            columns(padded),
        ],
        out_specs=[columns(rows), columns(rows), columns(padded)],
        out_shape=[
            jax.ShapeDtypeStruct((rows, width), BF16),
            jax.ShapeDtypeStruct((rows, width), BF16),
            jax.ShapeDtypeStruct((padded, width), F32),
        ],
        scratch_shapes=[
            pltpu.VMEM((grad.shape[0], block), F32),
            pltpu.VMEM((unit.shape[0], block), F32),
        ],
        compiler_params=pltpu.CompilerParams(vmem_limit_bytes=32 * 1024 * 1024),
        cost_estimate=pl.CostEstimate(
            flops=4 * rows * width * taps.shape[0], bytes_accessed=16 * rows * width, transcendentals=0
        ),
        name="taps_back",
    )(grad, unit, live, linear, gate, jnp.pad(taps, ((0, 1), (0, 0))))


def shards(frames, live_mask, stretch_target, pw_weight, kernel, out_grad):
    groups = X * YH
    own_group = lax.axis_index(DP)
    slot_count = stretch_target.shape[1]
    width = frames.shape[2]
    stretch_len = frames.shape[1] // slot_count
    capacity = out_grad.shape[1] // stretch_len
    per_peer = slot_count // 4
    entries = groups * per_peer
    taps = kernel.shape[0]
    length = slot_count * stretch_len
    rows_here = capacity * stretch_len
    half = width // CORE
    loss_scale = float(groups * Z * YL * CORE * rows_here) ** (-0.5)
    capacity_index = jnp.arange(capacity, dtype=jnp.int32)
    entry_ids = jnp.arange(entries, dtype=jnp.int32)
    slot_index = jnp.arange(slot_count, dtype=jnp.int32)
    earlier = slot_index[:, None] > slot_index[None, :]

    columns, others = own_columns(pw_weight)
    pair = both_cores(columns, swap(others))
    pair, frames, stretch_target = tie(pair, frames, stretch_target)
    partner = lax.ppermute(stretch_target, "yh", [(0, 1), (1, 0)])
    column = gather(pair, ZA, Z)

    window = CORE * length
    outer = 2 * SPAN
    normed, inverse_scale = normalize(frames[0].astype(F32))
    packet = marked(normed.astype(BF16), live_mask[0])
    packet_other = swap(packet)
    rows_win = both_cores(packet[:length], packet_other[:length])
    live_win = both_cores(packet[length, :length], packet_other[length, :length])
    before, behind = from_neighbours(
        marked(rows_win[:outer], live_win[:outer]),
        marked(rows_win[window - outer :], live_win[window - outer :]),
    )
    rows_ext = jnp.concatenate([before[:outer], rows_win, behind[:outer]], axis=0)
    live_ext = jnp.concatenate([before[outer, :outer], live_win, behind[outer, :outer]]).astype(F32)
    live_ext = live_ext[:, None]

    column, rows_ext, kernel, partner = tie(column, rows_ext, kernel, partner)
    lin, gate, all_targets, rows_ext = gather_weight(column, stretch_target, partner, rows_ext)

    feature = jnp.arange(width, dtype=jnp.int32)
    order_lin, order_gate = feature_order(True), feature_order(False)
    to_lin = (feature[:, None] == order_lin[None, :]).astype(BF16)
    to_gate = (feature[:, None] == order_gate[None, :]).astype(BF16)
    normed_lin = jnp.dot(rows_ext, to_lin, preferred_element_type=F32).astype(BF16)
    normed_gate = jnp.dot(rows_ext, to_gate, preferred_element_type=F32).astype(BF16)


    def entries_of(target, group):
        dest = jnp.where(target >= 0, target // capacity, -1)
        away = (target >= 0) & (dest != group)
        alike = (dest[:, None] == dest[None, :]) & away[None, :] & earlier
        rank = jnp.sum(alike.astype(jnp.int32), axis=1)
        return jnp.where(away, dest * per_peer + rank, -1)

    target = stretch_target[0]
    named_slot = target >= 0
    local = named_slot & (target // capacity == own_group)
    selector = (entries_of(target, own_group)[None, :] == entry_ids[:, None]).astype(BF16)
    local_pick = ((target % capacity)[None, :] == capacity_index[:, None]) & local[None, :]
    local_pick = local_pick.astype(BF16)

    group_ids = jnp.arange(groups, dtype=jnp.int32)
    arriving = jax.vmap(entries_of)(all_targets, group_ids)
    wanted = own_group * per_peer + jnp.arange(per_peer, dtype=jnp.int32)
    carried = arriving[:, None, :] == wanted[None, :, None]
    codes_home = (
        jnp.sum(jnp.where(carried, (all_targets % capacity + 1)[:, None, :], 0), axis=2) - 1
    ).reshape(entries)

    def leaving(values):
        pieces = values.reshape(slot_count, stretch_len, width)
        return jnp.einsum("es,sfw->efw", selector, pieces, preferred_element_type=F32).astype(BF16)

    def place_home(values, arrived):
        pieces = values.reshape(slot_count, stretch_len, width)
        placing = (codes_home[None, :] == capacity_index[:, None]).astype(BF16)
        placed = jnp.einsum("ce,efw->cfw", placing, arrived, preferred_element_type=F32)
        placed = placed + jnp.einsum("cs,sfw->cfw", local_pick, pieces, preferred_element_type=F32)
        return placed.astype(BF16).reshape(rows_here, width)

    def returning(values):
        pieces = values.reshape(capacity, stretch_len, width)
        picking = (codes_home[:, None] == capacity_index[None, :]).astype(BF16)
        return jnp.einsum("ec,cfw->efw", picking, pieces, preferred_element_type=F32).astype(BF16)

    def place_back(values, arrived):
        pieces = values.reshape(capacity, stretch_len, width)
        placed = jnp.einsum("es,efw->sfw", selector, arrived, preferred_element_type=F32)
        placed = placed + jnp.einsum("cs,cfw->sfw", local_pick, pieces, preferred_element_type=F32)
        return placed.astype(BF16).reshape(length, width)

    weight_lin, weight_gate = gather_four(lin, XA), gather_four(gate, YA)
    weight_lin, weight_gate, outgoing = tie(weight_lin, weight_gate, returning(out_grad[0]))
    grad_arrived = exchange(outgoing, DP)

    linear = jnp.dot(normed_lin, weight_lin, preferred_element_type=F32)
    gate = jax.nn.sigmoid(jnp.dot(normed_gate, weight_gate, preferred_element_type=F32))
    unit_ext = jnp.where(live_ext > 0, linear * gate, 0.0).astype(BF16)

    core = lax.axis_index(CA)
    taps_own = lax.dynamic_slice_in_dim(kernel, core * half, half, axis=1)
    inner = window + 2 * SPAN
    live_inner = live_ext[SPAN : SPAN + inner]
    live_own = live_ext[outer : outer + window]
    mixed_time = live_inner * depthwise(unit_ext[1:], taps_own, inner)
    grad_arrived, mixed_time = tie(grad_arrived, mixed_time)
    grad_time = place_back(out_grad[0], grad_arrived)
    mine = pick(grad_time[:, :half], grad_time[:, half:])
    others = pick(grad_time[:, half:], grad_time[:, :half])
    grad_win = both_cores(mine, swap(others))
    near, far = from_edges(
        pick(others[:SPAN], others[length - SPAN :]), pick(mine[:SPAN], mine[length - SPAN :])
    )
    grad_ext = jnp.concatenate([pick(near, far), grad_win, pick(far, near)], axis=0).astype(F32)

    mean_own = jnp.mean(mixed_time, axis=-1)
    rest_own = mixed_time - mean_own[:, None]
    square_own = jnp.sum(rest_own * rest_own, axis=-1)
    mean_there, square_there = swap(jnp.stack([mean_own, square_own]))
    apart = 0.5 * (mean_there - mean_own)
    spread = (square_own + square_there) / width + apart * apart
    norm_scale = lax.rsqrt(spread + EPSILON)[:, None]
    norm_time = (rest_own - apart[:, None]) * norm_scale
    sigma = jax.nn.sigmoid(norm_time)
    inner_rows = slice(SPAN, SPAN + window)
    silu = (norm_time * sigma)[inner_rows].astype(BF16)
    silu_low, silu_high = silu[:length], silu[length:]
    silu_there = swap(pick(silu_high, silu_low))
    silu_here = pick(silu_low, silu_high)
    silu_own = jnp.concatenate([pick(silu_here, silu_there), pick(silu_there, silu_here)], axis=1)
    output_time = (frames[0].astype(F32) + silu_own.astype(F32)).astype(BF16)

    grad_norm = grad_ext * sigma * (1.0 + norm_time * (1.0 - sigma))
    sums = jnp.stack([jnp.sum(grad_norm, axis=-1), jnp.sum(grad_norm * norm_time, axis=-1)])
    means = (sums + swap(sums)) / width
    grad_mixed = (
        live_inner * norm_scale * (grad_norm - means[0][:, None] - norm_time * means[1][:, None])
    ).astype(BF16)
    grad_mixed, outgoing = tie(grad_mixed, leaving(output_time))
    mixed_arrived = exchange(outgoing, DP)
    pre_lin, pre_gate, terms = taps_back(grad_mixed, unit_ext, live_own, linear, gate, taps_own)

    outer_rows = slice(outer, outer + window)
    def term(left, right):
        value = lax.dot_general(
            left[outer_rows], right, (((0,), (0,)), ((), ())), preferred_element_type=F32
        )
        return (loss_scale * value).astype(BF16)

    term_lin = term(normed_lin, pre_lin)
    term_lin, pre_gate, terms, mixed_arrived = tie(term_lin, pre_gate, terms, mixed_arrived)
    term_gate = term(normed_gate, pre_gate)
    terms = (loss_scale * terms).astype(BF16)
    rows, quarters = width // X, terms.reshape(X, terms.shape[0] // X, half)
    at = lax.axis_index(XA)

    def with_taps(k):
        part = lax.dynamic_index_in_dim(quarters, (at - k) % X, 0, keepdims=False)
        return jnp.concatenate([term_lin[k * rows : (k + 1) * rows], part], axis=0)

    gate_chunks = [term_gate[k * rows : (k + 1) * rows] for k in range(Y)]
    lin_chunks = [with_taps(k) for k in range(X)]
    gate_down, gate_up, lin_down, lin_up, pre_lin, pre_gate, mixed_arrived = tie(
        *messages(gate_chunks), *messages(lin_chunks), pre_lin, pre_gate, mixed_arrived
    )
    gate_sum = scatter_four(gate_chunks, gate_down, gate_up, YA)
    lin = scatter_four(lin_chunks, lin_down, lin_up, XA)
    partial_grad = back_product(pre_lin, pre_gate, weight_lin, weight_gate, order_lin, order_gate)
    mixed_rows = place_home(output_time, mixed_arrived)
    lin, gate_sum, partial_grad, mixed_rows = tie(lin, gate_sum, partial_grad, mixed_rows)
    full, partial_grad = scatter_middle(lin[:rows], gate_sum, lin[rows:], partial_grad)
    low, high = partial_grad[:length], partial_grad[length:]
    grad_normed = pick(low, high) + swap(pick(high, low).astype(BF16)).astype(F32)
    branch = inverse_scale * (
        grad_normed
        - jnp.mean(grad_normed, axis=-1, keepdims=True)
        - normed * jnp.mean(grad_normed * normed, axis=-1, keepdims=True)
    )
    named_rows = jnp.repeat(named_slot, stretch_len)[:, None]
    frame_grad = jnp.where(named_rows, grad_time.astype(F32) + branch, 0.0).astype(BF16)
    arrived, frame_grad = tie(exchange(full, ZA), frame_grad)
    weight_grad, kernel_grad = scatter_last(arrived, rows // Y // Z)
    kernel_grad = kernel_grad[:taps]
    return (mixed_rows[None], frame_grad[None], weight_grad, kernel_grad)


def solution(mesh):
    fine = Mesh(mesh.devices.reshape(X, YH, Z, YL, CORE), ("x", "yh", "z", "yl", "core"))
    every = DP + TM
    placed = (
        P(DP, TM, None),
        P(DP, TM),
        P(DP, TM),
        P(every, None),
        P(),
        P(DP, TM, None),
    )
    return jax.shard_map(
        shards,
        mesh=fine,
        in_specs=placed,
        out_specs=(P(DP, TM, None), P(DP, TM, None), P(every, None), P()),
        check_vma=False,
    )
```
